512 devices in a mesh: query: 8 (over y_lo, core), index: 64 (over x, z, y_hi).
Axes of the slice: x: 4, y: 8 (y_hi: 2, y_lo: 4; y = y_hi * 4 + y_lo), z: 8, core: 2. Of those that a mesh axis runs over, the one named last changes fastest.
Arguments:
- queries: bfloat16 [512, 768], P('query'), may hold values from -30 to 30
- passages: bfloat16 [262144, 768], P(('query', 'index')), may hold values from -30 to 30
- positive: int32 [512], replicated, may hold values from 0 to 262143
Outputs:
- loss: float32 [], replicated
- query_grad: bfloat16 [512, 768], P('query')
- passage_grad: bfloat16 [262144, 768], P(('query', 'index'))
The draws below stay inside these ranges and needn't reach their ends.
All inputs are finite; a program needn't handle non-finite values.
Results may differ from the reference program's by a relative error of at most 0.009.
Values may be sent and summed in bfloat16 or wider, within the bound.
No kernel may reach another device: no remote copies, remote signals or barrier semaphores. Data moves between devices by JAX's collectives and lax.ppermute only.
A program may use at most 64 MiB of HBM per device.

```python
import math
import jax
import jax.numpy as jnp
from jax import lax

D = 768
PD = 512
NQ = 512
NP = 262144
N_QUERY = 8
N_INDEX = 64


def shared_parts(key):
    anchor_key = jax.random.fold_in(key, 101)
    sign_key = jax.random.fold_in(key, 103)
    magnitude = jax.random.uniform(anchor_key, (4, D), jnp.float32, 2.0, 2.99)
    signs = jnp.where(jax.random.normal(sign_key, (4, D), jnp.float32) >= 0.0, 1.0, -1.0)
    anchors = magnitude * signs
    power = jnp.mean(anchors * anchors, axis=1)
    target = jnp.array([120.0, 160.0, 200.0, 240.0], jnp.float32)
    strength = jnp.sqrt(target / (math.sqrt(D) * power))
    return (anchors, strength, target)


def scaled_rows(key, count):
    first, second = jax.random.split(key)
    values = jnp.clip(jax.random.normal(first, (count, D), jnp.float32), -5.0, 5.0)
    spread = jnp.exp(jax.random.uniform(second, (count, 1), jnp.float32, jnp.log(0.3), jnp.log(3.0)))
    return values * spread


def draw_queries(key, part):
    anchors, strength, target = shared_parts(key)
    key = jax.random.fold_in(key, 1)
    first = jax.random.fold_in(key, 0)
    values = scaled_rows(first, NQ)
    rows = jnp.arange(4, dtype=jnp.int32) * (NQ // 4)
    values = values.at[rows].set(strength[:, None] * anchors)
    return values.astype(jnp.bfloat16)


def draw_passages(key, part):
    anchors, strength, target = shared_parts(key)
    key = jax.random.fold_in(key, 2)
    first = jax.random.fold_in(key, 0)
    values = scaled_rows(first, NP)
    rows = jnp.arange(4, dtype=jnp.int32) * (NP // 4)
    gap = 2.0 / target
    pairs = anchors.reshape(4, D // 2, 2)
    turned = jnp.stack([pairs[:, :, 1], -pairs[:, :, 0]], axis=2).reshape(4, D)
    twin = anchors * (1.0 - gap[:, None]) + 0.5 * turned
    values = values.at[rows].set(strength[:, None] * anchors).at[rows + 1].set(strength[:, None] * twin)
    return values.astype(jnp.bfloat16)


def place_ends(values, stream_key, least, high):
    spot = [jax.random.randint(jax.random.fold_in(stream_key, axis), (), 0, length) for axis, length in enumerate(values.shape)]
    main_axis = values.shape.index(max(values.shape))
    next_to = spot[:main_axis] + [(spot[main_axis] + 1) % values.shape[main_axis]] + spot[main_axis + 1:]
    return values.at[tuple(spot)].set(least).at[tuple(next_to)].set(high)


def setup_inputs(seed: int = 0) -> dict:
    key_list = jax.random.split(jax.random.key(seed), 4)
    return {
        "queries": draw_queries(jax.random.fold_in(key_list[3], 71), 0),
        "passages": draw_passages(jax.random.fold_in(key_list[3], 71), 0),
        "positive": place_ends(jax.random.randint(key_list[2], (NQ,), 0, NP), jax.random.fold_in(key_list[2], 1), 0, NP - 1).astype(jnp.int32),
    }


def reference(queries, passages, positive):
    scale = 1.0 / math.sqrt(D)
    rows_blk = PD * N_QUERY
    blocks = passages.reshape(N_INDEX, rows_blk, D)
    offsets = jnp.arange(N_INDEX, dtype=jnp.int32) * rows_blk

    def scores_of(block, offset):
        scores = jnp.dot(queries, block.T, preferred_element_type=jnp.float32) * scale
        hit = positive[:, None] == (offset + jnp.arange(rows_blk, dtype=jnp.int32))[None, :]
        return (scores, hit)

    def forward(carry, inputs):
        high, total, picked = carry
        block, offset = inputs
        scores, hit = scores_of(block, offset)
        top = jnp.maximum(high, lax.optimization_barrier(jnp.max(scores, axis=1)))
        total = total * jnp.exp(high - top) + lax.optimization_barrier(jnp.sum(jnp.exp(scores - top[:, None]), axis=1))
        picked = picked + lax.optimization_barrier(jnp.sum(jnp.where(hit, scores, jnp.zeros_like(scores)), axis=1))
        return ((top, total, picked), None)
    init = (jnp.full((NQ,), -1e+30, jnp.float32), jnp.zeros((NQ,), jnp.float32), jnp.zeros((NQ,), jnp.float32))
    (high, total, picked), _ = lax.scan(forward, init, (blocks, offsets))
    lse = high + jnp.log(total)
    loss = jnp.mean(lse - picked)

    def backward(carry, inputs):
        block, offset = inputs
        scores, hit = scores_of(block, offset)
        weights = ((jnp.exp(scores - lse[:, None]) - hit.astype(jnp.float32)) / NQ).astype(jnp.bfloat16)
        carry = carry + jnp.dot(weights, block, preferred_element_type=jnp.float32)
        grad_block = (jnp.dot(weights.T, queries, preferred_element_type=jnp.float32) * scale).astype(jnp.bfloat16)
        return (carry, grad_block)
    query_acc, grad_blocks = lax.scan(backward, jnp.zeros((NQ, D), jnp.float32), (blocks, offsets))
    query_grad = (query_acc * scale).astype(jnp.bfloat16)
    passage_grad = grad_blocks.reshape(NP, D)
    return (loss, query_grad, passage_grad)
```

```python
import math

import jax
import jax.numpy as jnp
import numpy as np
from jax import lax
from jax.sharding import Mesh
from jax.sharding import PartitionSpec as P

QUERY = ("yl", "core")
INDEX = ("x", "z", "yh")
ALL = QUERY + INDEX
NEAR = ("yl", "core", "yh")
PLANE = ("x", "z")
LOW = -1e30
PAD = 128


def share(value, axes):
    count = math.prod(lax.axis_size(a) for a in axes)
    sent = jnp.broadcast_to(value[None], (count,) + value.shape)
    return lax.all_to_all(sent, axes, 0, 0, tiled=True)


def merge(stats):
    top, total, picked = stats[:, 0], stats[:, 1], stats[:, 2]
    high = jnp.max(top, axis=0)
    total = jnp.sum(total * jnp.exp(top - high[None]), axis=0)
    return jnp.stack([high, total, jnp.sum(picked, axis=0)])


def split3(value):
    a = lax.reduce_precision(value, 8, 7)
    b = lax.reduce_precision(value - a, 8, 7)
    c = lax.reduce_precision(value - a - b, 8, 7)
    return jnp.stack([a, b, c], axis=1)


def on_device(queries, passages, positive):
    group, width = queries.shape
    scale = 1.0 / math.sqrt(width)
    total_q = positive.shape[0]
    shard = passages.shape[0]
    devices = math.prod(lax.axis_size(a) for a in ALL)
    bf16, f32 = jnp.bfloat16, jnp.float32
    me = lax.axis_index(ALL)
    core = lax.axis_index("core")
    columns = me * shard + jnp.arange(shard, dtype=jnp.int32)

    mine = share(queries, ("yl",)).reshape(-1, width)
    every = lax.all_gather(mine, "core", axis=0, tiled=True)
    n_yl = lax.axis_size("yl")
    target = positive.reshape(n_yl, 2, group).transpose(1, 0, 2).reshape(total_q)

    scores = jnp.einsum("rd,pd->rp", every, passages, preferred_element_type=f32) * scale
    hit = target[:, None] == columns[None, :]
    others = jnp.where(hit, LOW, scores)
    top = jnp.max(others, axis=1)
    terms = jnp.exp(others - top[:, None])
    stats = jnp.stack([top, jnp.sum(terms, axis=1), jnp.sum(jnp.where(hit, scores, 0.0), axis=1)])

    pulled = jnp.dot(terms.astype(bf16), passages, preferred_element_type=f32)
    chosen = jnp.dot(hit.astype(bf16), passages, preferred_element_type=f32).astype(bf16)
    marks = jnp.pad(split3(top).astype(bf16), ((0, 0), (0, PAD - 3)))

    even = core == 0
    away = jnp.where(even, chosen, pulled.astype(bf16))
    away = jnp.concatenate([away, marks], axis=1)
    came = lax.ppermute(away, "core", [(0, 1), (1, 0)])
    top2 = jnp.sum(came[:, width : width + 3].astype(f32), axis=1)
    both = jnp.maximum(top, top2)
    joined = (
        pulled * jnp.exp(top - both)[:, None]
        + came[:, :width].astype(f32) * jnp.exp(top2 - both)[:, None]
    ).astype(bf16)
    rows = jnp.where(even, joined, chosen + came[:, :width])
    marks2 = jnp.pad(split3(both).astype(bf16), ((0, 0), (0, PAD - 3)))
    rows = jnp.concatenate([rows, marks2], axis=1)
    rows = rows.reshape(2, n_yl, group, width + PAD).transpose(1, 0, 2, 3).reshape(total_q, -1)
    got = lax.all_to_all(rows, ALL, 0, 0, tiled=True)

    stats = merge(share(stats, NEAR))
    stats = merge(share(stats, PLANE))
    top, total, picked = stats[0], stats[1], stats[2]
    high = jnp.maximum(top, picked)
    rest = total * jnp.exp(top - high)
    full = rest + jnp.exp(picked - high)
    lse = high + jnp.log(full)
    loss = jnp.mean(lse - picked)

    weights = ((jnp.exp(scores - lse[:, None]) - hit.astype(f32)) / total_q).astype(bf16)
    passage_term = jnp.einsum("rp,rd->pd", weights, every, preferred_element_type=f32)
    passage_grad = (passage_term * scale).astype(bf16)

    index_size = devices // (n_yl * 2)
    own = (core * n_yl + lax.axis_index("yl")) * group + lax.axis_index(INDEX)
    pick = lambda v: lax.dynamic_index_in_dim(v, own, 0, keepdims=False)
    got = got.reshape(n_yl, 2, index_size, width + PAD)
    terms_in = got[:, 0].reshape(-1, width + PAD)
    from_top = jnp.sum(terms_in[:, width : width + 3].astype(f32), axis=1)
    factor = jnp.exp(from_top - pick(high)) / pick(full)
    pull = jnp.sum(terms_in[:, :width].astype(f32) * factor[:, None], axis=0)
    row = jnp.sum(got[:, 1, :, :width].astype(f32), axis=(0, 1))
    grad = (pull - (pick(rest) / pick(full)) * row) * (scale / total_q)
    query_grad = share(grad.astype(bf16)[None], INDEX).reshape(group, width)
    return (loss, query_grad, passage_grad)


def build(mesh):
    return jax.shard_map(
        on_device,
        mesh=mesh,
        in_specs=(P(QUERY, None), P(ALL, None), P()),
        out_specs=(P(), P(QUERY, None), P(ALL, None)),
        check_vma=False,
    )


def solution(mesh):
    devices = np.asarray(mesh.devices).reshape(4, 2, 4, 8, 2)
    return build(Mesh(devices, ("yl", "core", "x", "z", "yh")))
```

```python
import math

import jax
import jax.numpy as jnp
import numpy as np
from jax import lax
from jax.sharding import Mesh
from jax.sharding import PartitionSpec as P

QUERY = ("yl", "core")
INDEX = ("x", "z", "yh")
ALL = QUERY + INDEX
NEAR = ("yl", "core", "yh")
PLANE = ("x", "z")
RING = ("yl", "yh")
LOW = -1e30
PAD = 128


def share(value, axes):
    count = math.prod(lax.axis_size(a) for a in axes)
    sent = jnp.broadcast_to(value[None], (count,) + value.shape)
    return lax.all_to_all(sent, axes, 0, 0, tiled=True)


def merge(stats):
    top, total, picked = stats[:, 0], stats[:, 1], stats[:, 2]
    high = jnp.max(top, axis=0)
    total = jnp.sum(total * jnp.exp(top - high[None]), axis=0)
    return jnp.stack([high, total, jnp.sum(picked, axis=0)])


def split3(value):
    a = lax.reduce_precision(value, 8, 7)
    b = lax.reduce_precision(value - a, 8, 7)
    c = lax.reduce_precision(value - a - b, 8, 7)
    return jnp.stack([a, b, c], axis=1)


def on_device(queries, passages, positive):
    group, width = queries.shape
    scale = 1.0 / math.sqrt(width)
    total_q = positive.shape[0]
    half = total_q // 2
    shard = passages.shape[0]
    bf16, f32 = jnp.bfloat16, jnp.float32
    core = lax.axis_index("core")
    n_yl = lax.axis_size("yl")
    columns = lax.axis_index(ALL) * shard + jnp.arange(shard, dtype=jnp.int32)

    def swap(value):
        return lax.ppermute(value, "core", [(0, 1), (1, 0)])

    def ordered(value):
        return jnp.where(core == 0, value, value[..., ::-1, :])

    mine = share(queries, ("yl",)).reshape(half, width)
    theirs = swap(mine)
    target = positive.reshape(n_yl, 2, group).transpose(1, 0, 2).reshape(2, half)
    target = ordered(target)

    def local(block, aim):
        scores = jnp.einsum("rd,pd->rp", block, passages, preferred_element_type=f32) * scale
        hit = aim[:, None] == columns[None, :]
        others = jnp.where(hit, LOW, scores)
        top = jnp.max(others, axis=1)
        terms = jnp.exp(others - top[:, None])
        stats = jnp.stack([top, jnp.sum(terms, axis=1), jnp.sum(jnp.where(hit, scores, 0.0), axis=1)])
        pulled = jnp.dot(terms.astype(bf16), passages, preferred_element_type=f32)
        chosen = jnp.dot(hit.astype(bf16), passages, preferred_element_type=f32).astype(bf16)
        return scores, hit, top, stats, pulled, chosen

    def packed(top, pulled, chosen):
        marks = jnp.pad(split3(top).astype(bf16), ((0, 0), (0, PAD - 3)))
        return jnp.concatenate([pulled.astype(bf16), chosen, marks], axis=1)

    def unpacked(rows):
        top = jnp.sum(rows[..., 2 * width : 2 * width + 3].astype(f32), axis=-1)
        return top, rows[..., :width].astype(f32), rows[..., width : 2 * width]

    scores2, hit2, top2, stats2, pulled2, chosen2 = local(theirs, target[1])
    came = swap(packed(top2, pulled2, chosen2))
    scores1, hit1, top1, stats1, pulled1, chosen1 = local(mine, target[0])
    top2, pulled2, chosen2 = unpacked(came)
    top = jnp.maximum(top1, top2)
    pulled = pulled1 * jnp.exp(top1 - top)[:, None] + pulled2 * jnp.exp(top2 - top)[:, None]
    rows = packed(top, pulled, chosen1 + chosen2)

    stats = ordered(jnp.stack([stats1, stats2], axis=1)).reshape(3, total_q)
    rows, stats = lax.optimization_barrier((rows, stats))
    got = lax.all_to_all(rows, RING, 0, 0, tiled=True)
    stats = merge(share(stats, NEAR))
    got = got.reshape(n_yl * lax.axis_size("yh"), -1, 2 * width + PAD)
    tops, pulls, picks = unpacked(got)
    top = jnp.max(tops, axis=0)
    pulled = jnp.sum(pulls * jnp.exp(tops - top[None])[:, :, None], axis=0)
    rows = packed(top, pulled, jnp.sum(picks.astype(f32), axis=0).astype(bf16))

    rows, stats = lax.optimization_barrier((rows, stats))
    got = lax.all_to_all(rows, PLANE, 0, 0, tiled=True)
    stats = merge(share(stats, PLANE))
    top, total, picked = stats[0], stats[1], stats[2]
    high = jnp.maximum(top, picked)
    rest = total * jnp.exp(top - high)
    full = rest + jnp.exp(picked - high)
    lse = high + jnp.log(full)
    loss = jnp.mean(lse - picked)

    own = (core * n_yl + lax.axis_index("yl")) * group + lax.axis_index(("yh", "x", "z"))
    here = lax.dynamic_slice_in_dim(jnp.stack([high, rest, full]), own, 1, axis=1)
    tops, pulls, picks = unpacked(got)
    factor = jnp.exp(tops - here[0]) / here[2]
    pull = jnp.sum(pulls * factor[:, None], axis=0)
    row = jnp.sum(picks.astype(f32), axis=0)
    grad = (pull - (here[1] / here[2]) * row) * (scale / total_q)
    query_grad = share(grad.astype(bf16)[None], ("yh", "x", "z")).reshape(group, width)

    level = ordered(lse.reshape(2, half))

    def weights(scores, hit, lse):
        return ((jnp.exp(scores - lse[:, None]) - hit.astype(f32)) / total_q).astype(bf16)

    passage_term = jnp.einsum(
        "rp,rd->pd", weights(scores1, hit1, level[0]), mine, preferred_element_type=f32
    ) + jnp.einsum(
        "rp,rd->pd", weights(scores2, hit2, level[1]), theirs, preferred_element_type=f32
    )
    passage_grad = (passage_term * scale).astype(bf16)
    return (loss, query_grad, passage_grad)


def build(mesh):
    return jax.shard_map(
        on_device,
        mesh=mesh,
        in_specs=(P(QUERY, None), P(ALL, None), P()),
        out_specs=(P(), P(QUERY, None), P(ALL, None)),
        check_vma=False,
    )


def solution(mesh):
    devices = np.asarray(mesh.devices).reshape(4, 2, 4, 8, 2)
    return build(Mesh(devices, ("yl", "core", "x", "z", "yh")))
```

```python
import math

import jax
import jax.numpy as jnp
import numpy as np
from jax import lax
from jax.sharding import Mesh
from jax.sharding import PartitionSpec as P

QUERY = ("yl", "core")
INDEX = ("x", "z", "yh")
ALL = QUERY + INDEX
PLANE = ("x", "z")
RING = ("yl", "yh")
SPREAD = ("yh", "x", "z")
LOW = -1e30
SLOTS = 5
F32 = jnp.float32
BF16 = jnp.bfloat16


def size(axes):
    return math.prod(lax.axis_size(a) for a in axes)


def share(value, axes):
    sent = jnp.broadcast_to(value[None], (size(axes),) + value.shape)
    return lax.all_to_all(sent, axes, 0, 0, tiled=True)


def coded(value, width):
    a = lax.reduce_precision(value, 8, 7)
    b = lax.reduce_precision(value - a, 8, 7)
    c = lax.reduce_precision(value - a - b, 8, 7)
    terms = jnp.concatenate([a, b, c], axis=-1).astype(BF16)
    fill = -terms.shape[-1] % width
    return jnp.pad(terms, [(0, 0)] * (terms.ndim - 1) + [(0, fill)])


def decoded(terms, count):
    terms = terms[..., : 3 * count].astype(F32)
    return terms[..., :count] + terms[..., count : 2 * count] + terms[..., 2 * count :]


def log_sum(values, axis=0):
    high = jnp.max(values, axis=axis, keepdims=True)
    total = jnp.sum(jnp.exp(values - high), axis=axis)
    return jnp.squeeze(high, axis) + jnp.log(total)


def parted_sum(values):
    coarse = jnp.round(values / 16.0) * 16.0
    middle = jnp.round((values - coarse) * 64.0) / 64.0
    return jnp.stack([jnp.sum(coarse), jnp.sum(middle), jnp.sum(values - coarse - middle)])


def on_device(queries, passages, positive):
    group, width = queries.shape
    scale = 1.0 / math.sqrt(width)
    total_q = positive.shape[0]
    half = total_q // 2
    shard = passages.shape[0]
    n_index = size(INDEX)
    n_ring = size(RING)
    n_plane = size(PLANE)
    block = half // n_ring
    core = lax.axis_index("core")
    n_yl, n_yh = lax.axis_size("yl"), lax.axis_size("yh")
    columns = lax.axis_index(ALL) * shard + jnp.arange(shard, dtype=jnp.int32)

    def swap(value):
        return lax.ppermute(value, "core", [(0, 1), (1, 0)])

    def ordered(value):
        return jnp.where(core == 0, value, value[::-1])

    aims = positive.reshape(n_yl, 2, group).transpose(1, 0, 2).reshape(2, n_ring, block)
    aims = ordered(aims)
    owner = aims // shard
    chip = (owner // n_index) // 2 * n_index + owner % n_index
    same = chip[..., :, None] == chip[..., None, :]
    before = jnp.arange(block)[:, None] > jnp.arange(block)[None, :]
    rank = jnp.sum((same & before).astype(jnp.int32), axis=-1)
    rounds = jnp.max(rank) // SLOTS
    slots = jnp.arange(SLOTS, dtype=jnp.int32)
    this_chip = lax.axis_index("yl") * n_index + lax.axis_index(INDEX)
    place = lax.axis_index(RING)
    my_chip = lax.dynamic_index_in_dim(chip[0], place, 0, keepdims=False)
    my_rank = lax.dynamic_index_in_dim(rank[0], place, 0, keepdims=False)
    peer = jnp.arange(n_ring, dtype=jnp.int32)
    peer_chip = (peer // n_yh) * n_index + lax.axis_index(PLANE) * n_yh + peer % n_yh

    def slot_rows(turn):
        fits = (chip == this_chip)[..., None] & (rank[..., None] == turn * SLOTS + slots)
        wanted = jnp.max(jnp.where(fits, aims[..., None], -1), axis=2)
        match = (wanted.reshape(-1)[:, None] == columns[None, :]).astype(BF16)
        rows = jnp.dot(match, passages, preferred_element_type=F32).astype(BF16)
        return rows.reshape(2, n_ring * SLOTS, width)

    def placed_rows(turn, rows):
        fits = (my_chip[:, None] == peer_chip[None, :])[..., None]
        fits = fits & (my_rank[:, None, None] == turn * SLOTS + slots)
        fits = fits.astype(BF16).reshape(block, n_ring * SLOTS)
        rows = rows.reshape(n_ring * SLOTS, width)
        return jnp.dot(fits, rows, preferred_element_type=F32)

    def later_turn(turn, held):
        rows = slot_rows(turn)
        rows = (rows[0] + swap(rows[1])).reshape(n_ring, SLOTS, width)
        return held + placed_rows(turn, lax.all_to_all(rows, RING, 0, 0, tiled=True))

    picks = slot_rows(0)
    mine = share(queries, ("yl",)).reshape(half, width)
    came = swap(jnp.concatenate([mine, picks[1]], axis=0))
    theirs = came[:half]
    picks = (picks[0] + came[half:]).reshape(n_ring, SLOTS, width)

    def scored(rows, aim):
        scores = jnp.einsum("rd,pd->rp", rows, passages, preferred_element_type=F32) * scale
        hit = aim[:, None] == columns[None, :]
        others = jnp.where(hit, LOW, scores)
        top = jnp.max(others, axis=1)
        terms = jnp.exp(others - top[:, None])
        total = jnp.sum(terms, axis=1)
        picked = jnp.sum(jnp.where(hit, scores, 0.0), axis=1)
        only = jnp.max(jnp.where(hit, scores, LOW), axis=1)
        high = jnp.maximum(top, only)
        level = high + jnp.log(total * jnp.exp(top - high) + jnp.exp(only - high))
        pulled = jnp.dot(terms.astype(BF16), passages, preferred_element_type=F32)
        return scores, hit, top, total, picked, level, pulled

    scores2, hit2, top2, total2, picked2, level2, pulled2 = scored(theirs, aims[1].reshape(half))
    scores1, hit1, top1, total1, picked1, level1, pulled1 = scored(mine, aims[0].reshape(half))
    chosen_sum = parted_sum(picked1) + parted_sum(picked2)
    notes = jnp.concatenate([top2, total2, picked2, level2, level1, chosen_sum])
    count = notes.shape[0]
    notes = coded(notes, width).reshape(-1, width)
    came = swap(jnp.concatenate([pulled2.astype(BF16), notes], axis=0))
    notes = decoded(came[half:].reshape(-1), count)
    top2, total2, picked2, other1, other2 = notes[:-3].reshape(5, half)
    top = jnp.maximum(top1, top2)
    keep1, keep2 = jnp.exp(top1 - top), jnp.exp(top2 - top)
    pulled = pulled1 * keep1[:, None] + came[:half].astype(F32) * keep2[:, None]
    total = total1 * keep1 + total2 * keep2
    marks = jnp.stack([top, total, picked1 + picked2])
    level = log_sum(jnp.stack([jnp.stack([level1, level2]), jnp.stack([other1, other2])]))
    level = ordered(level).reshape(total_q)
    chosen_sum = chosen_sum + notes[-3:]

    def tagged(marks, blocks):
        marks = marks.reshape(3, blocks, -1).transpose(1, 0, 2).reshape(blocks, -1)
        return jnp.concatenate([marks, jnp.broadcast_to(chosen_sum, (blocks, 3))], axis=1)

    marks = coded(tagged(marks, n_ring), width).reshape(n_ring, -1, width)
    levels = coded(level, width).reshape(1, -1, width)
    levels = jnp.broadcast_to(levels, (n_ring,) + levels.shape[1:])
    rows = jnp.concatenate(
        [pulled.astype(BF16).reshape(n_ring, block, width), picks, marks, levels], axis=1
    )
    got = lax.all_to_all(rows, RING, 0, 0, tiled=True)
    tail = block + SLOTS
    notes_rows = marks.shape[1]
    marks = decoded(got[:, tail : tail + notes_rows].reshape(n_ring, -1), 3 * block + 3)
    chosen_sum = jnp.sum(marks[:, -3:], axis=0)
    tops, totals, pickeds = (marks[:, i * block : (i + 1) * block] for i in range(3))
    top = jnp.max(tops, axis=0)
    keep = jnp.exp(tops - top[None])
    pulled = jnp.sum(got[:, :block].astype(F32) * keep[:, :, None], axis=0)
    marks = jnp.stack([top, jnp.sum(totals * keep, axis=0), jnp.sum(pickeds, axis=0)])
    level = log_sum(decoded(got[:, tail + notes_rows :].reshape(n_ring, -1), total_q))
    chosen = placed_rows(0, got[:, block:tail])
    chosen = lax.fori_loop(1, rounds + 1, later_turn, chosen)

    marks = coded(tagged(marks, n_plane), 128)
    levels = coded(level, 128)
    span = levels.shape[0]
    levels = jnp.broadcast_to(levels[None], (n_plane, span))
    rows = jnp.concatenate([pulled.astype(BF16), chosen.astype(BF16), levels, marks], axis=1)
    got = lax.all_to_all(rows, PLANE, 0, 0, tiled=True)
    marks = decoded(got[:, 2 * width + span :], 6)
    tops, totals = marks[:, 0], marks[:, 1]
    picked, chosen_sum = jnp.sum(marks[:, 2]), jnp.sum(marks[:, 3:], axis=0)
    lse = log_sum(decoded(got[:, 2 * width : 2 * width + span], total_q))
    loss = jnp.sum(parted_sum(lse) - chosen_sum) / total_q

    high = jnp.maximum(jnp.max(tops), picked)
    keep = jnp.exp(tops - high)
    rest = jnp.sum(totals * keep)
    full = rest + jnp.exp(picked - high)
    pull = jnp.sum(got[:, :width].astype(F32) * (keep / full)[:, None], axis=0)
    row = jnp.sum(got[:, width : 2 * width].astype(F32), axis=0)
    grad = (pull - (rest / full) * row) * (scale / total_q)
    query_grad = share(grad.astype(BF16)[None], SPREAD).reshape(group, width)

    level = ordered(lse.reshape(2, half))

    def weights(scores, hit, lse):
        return ((jnp.exp(scores - lse[:, None]) - hit.astype(F32)) / total_q).astype(BF16)

    passage_term = jnp.einsum(
        "rp,rd->pd", weights(scores1, hit1, level[0]), mine, preferred_element_type=F32
    ) + jnp.einsum(
        "rp,rd->pd", weights(scores2, hit2, level[1]), theirs, preferred_element_type=F32
    )
    passage_grad = (passage_term * scale).astype(BF16)
    return (loss, query_grad, passage_grad)


def build(mesh):
    return jax.shard_map(
        on_device,
        mesh=mesh,
        in_specs=(P(QUERY, None), P(ALL, None), P()),
        out_specs=(P(), P(QUERY, None), P(ALL, None)),
        check_vma=False,
    )


def solution(mesh):
    devices = np.asarray(mesh.devices).reshape(4, 2, 4, 8, 2)
    return build(Mesh(devices, ("yl", "core", "x", "z", "yh")))
```

```python
import math

import jax
import jax.numpy as jnp
import numpy as np
from jax import lax
from jax.experimental import pallas as pl
from jax.experimental.pallas import tpu as pltpu
from jax.sharding import Mesh
from jax.sharding import PartitionSpec as P

QUERY = ("yl", "core")
INDEX = ("x", "z", "yh")
ALL = QUERY + INDEX
PLANE = ("x", "z")
RING = ("yl", "yh")
SPREAD = ("yh", "x", "z")
LOW = -1e30
SLOTS = 5
LANES = 128
F32 = jnp.float32
BF16 = jnp.bfloat16


def size(axes):
    return math.prod(lax.axis_size(a) for a in axes)


def index(axes):
    place = 0
    for a in axes:
        place = place * lax.axis_size(a) + lax.axis_index(a)
    return place


def call(body, outs, ins, flops, scratch=()):
    moved = sum(math.prod(o.shape) * o.dtype.itemsize for o in list(outs) + list(ins))
    return pl.pallas_call(
        body,
        out_shape=tuple(outs),
        scratch_shapes=list(scratch),
        cost_estimate=pl.CostEstimate(flops=flops, bytes_accessed=moved, transcendentals=0),
        compiler_params=pltpu.CompilerParams(vmem_limit_bytes=40 << 20),
    )(*ins)


def shaped(shape, dtype):
    return jax.ShapeDtypeStruct(shape, dtype)


def iota(shape, dim):
    return lax.broadcasted_iota(jnp.int32, shape, dim)


def split3(value):
    a = value.astype(BF16).astype(F32)
    b = (value - a).astype(BF16).astype(F32)
    c = (value - a - b).astype(BF16).astype(F32)
    return a, b, c


def parted_sum(values):
    coarse = jnp.round(values * (1 / 16)) * 16.0
    middle = jnp.round((values - coarse) * 64.0) * (1 / 64)
    parts = (coarse, middle, values - coarse - middle)
    return [jnp.sum(p, axis=(0, 1), keepdims=True) for p in parts]


def sums_out(sums, lane, first):
    spread = jnp.zeros(lane.shape, F32)
    for i in range(3):
        spread = jnp.where((lane - first) % 3 == i, sums[i], spread)
    a, b, c = split3(spread)
    terms = jnp.where(lane < first + 3, a, jnp.where(lane < first + 6, b, c))
    return jnp.where((lane >= first) & (lane < first + 9), terms, 0.0)


def sums_in(terms, lane, first):
    inside = (lane >= first) & (lane < first + 9)
    return [
        jnp.sum(jnp.where(inside & ((lane - first) % 3 == i), terms, 0.0), axis=(0, 1), keepdims=True)
        for i in range(3)
    ]


def notes_out(level, rest, sums):
    total_q = level.shape[1]
    value = jnp.concatenate([level, rest], axis=1)
    width = value.shape[1]
    lane = iota((1, width), 1)
    a, b, c = split3(value)
    c = jnp.where(lane < total_q, c, sums_out(sums, lane, total_q))
    sub = iota((8, width), 0)
    return jnp.where(sub == 5, a, jnp.where(sub == 6, b, jnp.where(sub == 7, c, 0.0)))


def notes_in(tile, total_q):
    a, b, c = tile[5:6], tile[6:7], tile[7:8]
    lane = iota(a.shape, 1)
    value = a + b + jnp.where(lane < total_q, c, 0.0)
    return value[:, :total_q], value[:, total_q:], c


def log_sum(values):
    high = jnp.max(values, axis=0, keepdims=True)
    return high + jnp.log(jnp.sum(jnp.exp(values - high), axis=0, keepdims=True))


def columns_of(rows):
    fill = jnp.zeros((LANES - rows.shape[0], rows.shape[1]), F32)
    return jnp.concatenate([rows, fill], axis=0).T


def first_kernel(every, passages, aims, wanted, sent, scores, terms, notes, slots):
    shard, width = passages.shape
    half = scores.shape[2]
    core = lax.axis_index("core")
    base = index(ALL) * shard
    down = base + iota((shard, 1), 0)
    scale = 1.0 / math.sqrt(width)
    found = []
    for side in (1, 0):
        block = every[:, lax.rem(core + side, 2)].reshape(half, width)
        score = scale * lax.dot_general(
            passages[...], block, (((1,), (1,)), ((), ())), preferred_element_type=F32
        )
        scores[side] = score
        hit = aims[:, side * half : (side + 1) * half] == down
        others = jnp.where(hit, LOW, score)
        only = jnp.max(jnp.where(hit, score, LOW), axis=0, keepdims=True)
        picked = jnp.where(only > LOW, only, 0.0)
        top = jnp.max(others, axis=0, keepdims=True)
        term = jnp.exp(others - top)
        total = jnp.sum(term, axis=0, keepdims=True)
        high = jnp.maximum(top, only)
        level = high + jnp.log(total * jnp.exp(top - high) + jnp.exp(only - high))
        share = jnp.exp(top - level)
        term = (term * share).astype(BF16)
        if side:
            pulled = lax.dot_general(
                term, passages[...], (((0,), (0,)), ((), ())), preferred_element_type=F32
            )
            sent[:half] = pulled.astype(BF16)
        else:
            terms[...] = term
        found.append((level, total * share, parted_sum(picked)))
    (level2, rest2, sum2), (level1, rest1, sum1) = found
    sums = [a + b for a, b in zip(sum1, sum2)]
    swapped = core == 1
    level = jnp.concatenate(
        [jnp.where(swapped, level2, level1), jnp.where(swapped, level1, level2)], axis=1
    )
    match = (wanted[...] == base + iota((1, shard), 1)).astype(BF16)
    rows = jnp.dot(match, passages[...], preferred_element_type=F32)
    count = rows.shape[0] // 2
    slots[...] = rows[:count].astype(BF16)
    tail = rows[count:]
    tail = jnp.concatenate([tail[:8] + notes_out(level, rest2, sums), tail[8:]], axis=0)
    sent[half:] = tail.astype(BF16)
    notes[...] = notes_out_plain(level, rest1, sums)


def notes_out_plain(level, rest, sums):
    value = jnp.concatenate([level, rest], axis=1)
    lane = iota((1, value.shape[1]), 1)
    row = jnp.where(lane == 0, sums[0], jnp.where(lane == 1, sums[1], jnp.where(lane == 2, sums[2], 0.0)))
    sub = iota((8, value.shape[1]), 0)
    return jnp.where(sub == 0, value, jnp.where(sub == 1, row, 0.0))


def chip_kernel(came, pulled, notes, slots, sent):
    half, width = pulled.shape
    total_q = 2 * half
    blocks = sent.shape[0]
    rows = half // blocks
    core = lax.axis_index("core")
    other = came[half:].astype(F32)
    level2, rest2, last = notes_in(other[:8], total_q)
    sums2 = sums_in(last, iota(last.shape, 1), total_q)
    level1, rest1 = notes[0:1, :total_q], notes[0:1, total_q:]
    sums = [notes[1:2, i : i + 1] + sums2[i] for i in range(3)]
    level = log_sum(jnp.concatenate([level1, level2], axis=0))
    swapped = core == 1

    def kept(value):
        return jnp.where(swapped, value[:, half:], value[:, :half])

    keep1 = jnp.exp(kept(level1) - kept(level))
    keep2 = jnp.exp(kept(level2) - kept(level))
    tile = notes_out(level, rest1 * keep1 + rest2 * keep2, sums)
    keeps = columns_of(jnp.concatenate([keep1, keep2], axis=0))
    both = pulled[...] * keeps[:, 0:1] + came[:half].astype(F32) * keeps[:, 1:2]
    mine = slots[...].astype(F32)
    clean = jnp.where(iota((8, width), 0) < 5, other[:8], 0.0)
    other = jnp.concatenate([clean, other[8:]], axis=0) + mine
    for b in range(blocks):
        block = jnp.concatenate(
            [both[b * rows : (b + 1) * rows], other[b * 8 : (b + 1) * 8] + tile], axis=0
        )
        sent[b] = block.astype(BF16)


def ring_kernel(got, fits, extra, sent, turned):
    peers, height, width = got.shape
    rows = height - 8
    planes = sent.shape[0]
    half = rows * peers
    total_q = 2 * half
    core = lax.axis_index("core")
    parts = [got[s].astype(F32) for s in range(peers)]
    read = [notes_in(p[rows:], total_q) for p in parts]
    levels = jnp.concatenate([r[0] for r in read], axis=0)
    rests = jnp.concatenate([r[1] for r in read], axis=0)
    last = jnp.concatenate([r[2] for r in read], axis=0)
    sums = sums_in(last, iota(last.shape, 1), total_q)
    level = log_sum(levels)
    keep = jnp.exp(levels - level)
    swapped = core == 1
    keep = jnp.where(swapped, keep[:, half:], keep[:, :half])
    own = jnp.where(swapped, level[:, half:], level[:, :half])
    rest = jnp.sum(rests * keep, axis=0, keepdims=True)
    turned[...] = columns_of(jnp.concatenate([keep, rest, own], axis=0))
    cols = turned[pl.ds(pl.multiple_of(index(RING) * rows, 8), rows), :]
    pulled = parts[0][:rows] * cols[:, 0:1]
    for s in range(1, peers):
        pulled = pulled + parts[s][:rows] * cols[:, s : s + 1]
    whole = jnp.concatenate(parts, axis=0).astype(BF16)
    chosen = jnp.dot(fits[...], whole, preferred_element_type=F32) + extra[...]
    lane = iota((rows, LANES), 1)
    beside = sums_out(sums, lane, 16)
    for i, term in enumerate(split3(cols[:, peers + 1 : peers + 2]) + split3(cols[:, peers : peers + 1])):
        beside = jnp.where(lane == i, term, beside)
    chunks = total_q // LANES
    sub = iota((16, LANES), 0)
    wide = jnp.zeros((16, LANES), F32)
    for t, term in enumerate(split3(level)):
        for j in range(chunks):
            wide = jnp.where(sub == t * chunks + j, term[:, j * LANES : (j + 1) * LANES], wide)
    across = width // LANES
    for d in range(planes):
        r, c = d // across, d % across
        if r * 8 < rows:
            here, span = slice(r * 8, r * 8 + 8), slice(c * LANES, (c + 1) * LANES)
            tile = [pulled[here, span], chosen[here, span], beside[here]]
        else:
            tile = [jnp.zeros((16, LANES), F32), beside[:8]]
        sent[d] = jnp.concatenate(tile + [wide], axis=0).astype(BF16)


def make_plane_kernel(total_q, scale):
    chunks = total_q // LANES

    def plane_kernel(got, sent, level, loss):
        peers = got.shape[0]
        lane = iota((8, LANES), 1)
        tops, rests, wides = [], [], []
        chosen = jnp.zeros((8, LANES), F32)
        beside = jnp.zeros((8, LANES), F32)
        for s in range(peers):
            part = got[s].astype(F32)
            note = part[16:24]
            tops.append(jnp.sum(jnp.where(lane < 3, note, 0.0), axis=1, keepdims=True))
            rests.append(
                jnp.sum(jnp.where((lane >= 3) & (lane < 6), note, 0.0), axis=1, keepdims=True)
            )
            wide = part[24:]
            wides.append(wide[:chunks] + wide[chunks : 2 * chunks] + wide[2 * chunks : 3 * chunks])
            chosen = chosen + part[8:16]
            beside = beside + note
        high, top = wides[0], tops[0]
        for s in range(1, peers):
            high, top = jnp.maximum(high, wides[s]), jnp.maximum(top, tops[s])
        total = jnp.zeros((chunks, LANES), F32)
        full = jnp.zeros((8, 1), F32)
        rest = jnp.zeros((8, 1), F32)
        pulled = jnp.zeros((8, LANES), F32)
        for s in range(peers):
            total = total + jnp.exp(wides[s] - high)
            keep = jnp.exp(tops[s] - top)
            full = full + keep
            rest = rest + keep * rests[s]
            pulled = pulled + keep * got[s].astype(F32)[:8]
        lse = high + jnp.log(total)
        tile = ((pulled - rest * chosen) / full * (scale / total_q)).astype(BF16)
        for d in range(sent.shape[0]):
            sent[d] = tile
        level[...] = lse
        picked = sums_in(beside[0:1], lane[0:1], 16)
        terms = [a - b for a, b in zip(parted_sum(lse), picked)]
        loss[...] = (terms[0] + terms[1] + terms[2]) * (1.0 / total_q)

    return plane_kernel


def passage_kernel(scores, level, every, aims, out):
    shard, width = out.shape
    half = scores.shape[2]
    total_q = 2 * half
    core = lax.axis_index("core")
    down = index(ALL) * shard + iota((shard, 1), 0)
    scale = 1.0 / math.sqrt(width)
    total = None
    for side in range(2):
        which = lax.rem(core + side, 2)
        chunks = half // LANES
        lse = jnp.concatenate(
            [level[pl.ds(which * chunks + j, 1), :] for j in range(chunks)], axis=1
        )
        hit = aims[:, side * half : (side + 1) * half] == down
        weight = (jnp.exp(scores[side] - lse) - hit.astype(F32)) * (1.0 / total_q)
        block = every[:, which].reshape(half, width)
        term = jnp.dot(weight.astype(BF16), block, preferred_element_type=F32)
        total = term if total is None else total + term
    out[...] = (total * scale).astype(BF16)


def on_device(queries, passages, positive):
    group, width = queries.shape
    scale = 1.0 / math.sqrt(width)
    total_q = positive.shape[0]
    half = total_q // 2
    shard = passages.shape[0]
    n_index = size(INDEX)
    n_ring = size(RING)
    n_plane = size(PLANE)
    block = half // n_ring
    core = lax.axis_index("core")
    n_yl, n_yh = lax.axis_size("yl"), lax.axis_size("yh")
    columns = lax.axis_index(ALL) * shard + jnp.arange(shard, dtype=jnp.int32)

    def swap(value):
        return lax.ppermute(value, "core", [(0, 1), (1, 0)])

    aims = positive.reshape(n_yl, 2, group).transpose(1, 0, 2).reshape(2, n_ring, block)
    aims = jnp.where(core == 0, aims, aims[::-1])
    owner = aims // shard
    chip = (owner // n_index) // 2 * n_index + owner % n_index
    same = chip[..., :, None] == chip[..., None, :]
    before = jnp.arange(block)[:, None] > jnp.arange(block)[None, :]
    rank = jnp.sum((same & before).astype(jnp.int32), axis=-1)
    rounds = jnp.max(rank) // SLOTS
    slots = jnp.arange(SLOTS, dtype=jnp.int32)
    this_chip = lax.axis_index("yl") * n_index + lax.axis_index(INDEX)
    place = lax.axis_index(RING)
    my_chip = lax.dynamic_index_in_dim(chip[0], place, 0, keepdims=False)
    my_rank = lax.dynamic_index_in_dim(rank[0], place, 0, keepdims=False)
    peer = jnp.arange(n_ring, dtype=jnp.int32)
    peer_chip = (peer // n_yh) * n_index + lax.axis_index(PLANE) * n_yh + peer % n_yh

    def slot_aims(turn):
        fits = (chip == this_chip)[..., None] & (rank[..., None] == turn * SLOTS + slots)
        return jnp.max(jnp.where(fits, aims[..., None], -1), axis=2)

    def slot_fits(turn):
        fits = (my_chip[:, None] == peer_chip[None, :])[..., None]
        return (fits & (my_rank[:, None, None] == turn * SLOTS + slots)).astype(BF16)

    def later_turn(turn, held):
        match = (slot_aims(turn).reshape(-1)[:, None] == columns[None, :]).astype(BF16)
        rows = jnp.dot(match, passages, preferred_element_type=F32).astype(BF16)
        rows = rows.reshape(2, n_ring, SLOTS, width)
        rows = lax.all_to_all(rows[0] + swap(rows[1]), RING, 0, 0, tiled=True)
        fits = slot_fits(turn).reshape(block, n_ring * SLOTS)
        return held + jnp.dot(fits, rows.reshape(-1, width), preferred_element_type=F32)

    extra = lax.fori_loop(1, rounds + 1, later_turn, jnp.zeros((block, width), F32))
    wanted = jnp.pad(slot_aims(0), ((0, 0), (0, 0), (0, 8 - SLOTS)), constant_values=-1)
    wanted = wanted.reshape(-1, 1)
    fits = jnp.pad(slot_fits(0), ((0, 0), (0, 0), (block, 8 - SLOTS))).reshape(block, -1)
    aims = aims.reshape(1, total_q)

    every = lax.all_gather(queries, QUERY, axis=0, tiled=True).reshape(n_yl, 2, group, width)
    product = 2 * total_q * shard * width
    sent, scores, terms, notes, own_slots = call(
        first_kernel,
        [
            shaped((half + 8 * n_ring, width), BF16),
            shaped((2, shard, half), F32),
            shaped((shard, half), BF16),
            shaped((8, width), F32),
            shaped((8 * n_ring, width), BF16),
        ],
        [every, passages, aims, wanted],
        2 * product,
    )
    came = swap(sent)
    pulled = lax.dot_general(terms, passages, (((0,), (0,)), ((), ())), preferred_element_type=F32)
    (sent,) = call(
        chip_kernel,
        [shaped((n_ring, block + 8, width), BF16)],
        [came, pulled, notes, own_slots],
        half * width * 8,
    )
    got = lax.all_to_all(sent, RING, 0, 0, tiled=True)
    (sent,) = call(
        ring_kernel,
        [shaped((n_plane, 40, LANES), BF16)],
        [got, fits, extra],
        half * width * 8,
        [pltpu.VMEM((half, LANES), F32)],
    )
    got = lax.all_to_all(sent, PLANE, 0, 0, tiled=True)
    spread = n_plane * n_yh
    sent, level, loss = call(
        make_plane_kernel(total_q, scale),
        [
            shaped((spread, 8, LANES), BF16),
            shaped((total_q // LANES, LANES), F32),
            shaped((1, 1), F32),
        ],
        [got],
        half * width * 8,
    )
    tiles = lax.all_to_all(sent, SPREAD, 0, 0, tiled=True)
    (passage_grad,) = call(
        passage_kernel,
        [shaped((shard, width), BF16)],
        [scores, level, every, aims],
        product,
    )
    down, across = block // 8, width // LANES
    tiles = tiles.reshape(n_yh, n_plane, 8, LANES)[:, : down * across]
    tiles = tiles.reshape(n_yh, down, across, 8, LANES).transpose(0, 1, 3, 2, 4)
    return (loss[0, 0], tiles.reshape(group, width), passage_grad)


def build(mesh):
    return jax.shard_map(
        on_device,
        mesh=mesh,
        in_specs=(P(QUERY, None), P(ALL, None), P()),
        out_specs=(P(), P(QUERY, None), P(ALL, None)),
        check_vma=False,
    )


def solution(mesh):
    devices = np.asarray(mesh.devices).reshape(4, 2, 4, 8, 2)
    return build(Mesh(devices, ("yl", "core", "x", "z", "yh")))
```

```python
import math

import jax
import jax.numpy as jnp
import numpy as np
from jax import lax
from jax.experimental import pallas as pl
from jax.experimental.pallas import tpu as pltpu
from jax.sharding import Mesh
from jax.sharding import PartitionSpec as P

QUERY = ("yl", "core")
INDEX = ("x", "z", "yh")
ALL = QUERY + INDEX
PLANE = ("x", "z")
RING = ("yl", "yh")
SPREAD = ("yh", "x", "z")
LOW = -1e30
SLOTS = 5
LANES = 128
F32 = jnp.float32
BF16 = jnp.bfloat16


def size(axes):
    return math.prod(lax.axis_size(a) for a in axes)


def index(axes):
    place = 0
    for a in axes:
        place = place * lax.axis_size(a) + lax.axis_index(a)
    return place


def call(body, outs, ins, flops, scratch=()):
    moved = sum(math.prod(o.shape) * o.dtype.itemsize for o in list(outs) + list(ins))
    return pl.pallas_call(
        body,
        out_shape=tuple(outs),
        scratch_shapes=list(scratch),
        cost_estimate=pl.CostEstimate(flops=flops, bytes_accessed=moved, transcendentals=0),
        compiler_params=pltpu.CompilerParams(vmem_limit_bytes=40 << 20),
    )(*ins)


def shaped(shape, dtype):
    return jax.ShapeDtypeStruct(shape, dtype)


def iota(shape, dim):
    return lax.broadcasted_iota(jnp.int32, shape, dim)


def split3(value):
    a = value.astype(BF16).astype(F32)
    b = (value - a).astype(BF16).astype(F32)
    c = (value - a - b).astype(BF16).astype(F32)
    return a, b, c


def parted_sum(values):
    coarse = jnp.round(values * (1 / 16)) * 16.0
    middle = jnp.round((values - coarse) * 64.0) * (1 / 64)
    parts = (coarse, middle, values - coarse - middle)
    return [jnp.sum(p, axis=(0, 1), keepdims=True) for p in parts]


def sums_out(sums, lane, first):
    spread = jnp.zeros(lane.shape, F32)
    for i in range(3):
        spread = jnp.where((lane - first) % 3 == i, sums[i], spread)
    a, b, c = split3(spread)
    terms = jnp.where(lane < first + 3, a, jnp.where(lane < first + 6, b, c))
    return jnp.where((lane >= first) & (lane < first + 9), terms, 0.0)


def sums_in(terms, lane, first):
    inside = (lane >= first) & (lane < first + 9)
    return [
        jnp.sum(jnp.where(inside & ((lane - first) % 3 == i), terms, 0.0), axis=(0, 1), keepdims=True)
        for i in range(3)
    ]


def notes_out(level, rest, sums):
    total_q = level.shape[1]
    value = jnp.concatenate([level, rest], axis=1)
    width = value.shape[1]
    lane = iota((1, width), 1)
    a, b, c = split3(value)
    c = jnp.where(lane < total_q, c, sums_out(sums, lane, total_q))
    sub = iota((8, width), 0)
    return jnp.where(sub == 5, a, jnp.where(sub == 6, b, jnp.where(sub == 7, c, 0.0)))


def notes_in(tile, total_q):
    a, b, c = tile[5:6], tile[6:7], tile[7:8]
    lane = iota(a.shape, 1)
    value = a + b + jnp.where(lane < total_q, c, 0.0)
    return value[:, :total_q], value[:, total_q:], c


def log_sum(values):
    high = jnp.max(values, axis=0, keepdims=True)
    return high + jnp.log(jnp.sum(jnp.exp(values - high), axis=0, keepdims=True))


def columns_of(rows):
    fill = jnp.zeros((LANES - rows.shape[0], rows.shape[1]), F32)
    return jnp.concatenate([rows, fill], axis=0).T


def own_first(positive, group, swapped):
    count = positive.shape[1] // (2 * group)
    even = [positive[:, 2 * i * group : (2 * i + 1) * group] for i in range(count)]
    odd = [positive[:, (2 * i + 1) * group : (2 * i + 2) * group] for i in range(count)]
    even, odd = jnp.concatenate(even, axis=1), jnp.concatenate(odd, axis=1)
    return jnp.concatenate(
        [jnp.where(swapped, odd, even), jnp.where(swapped, even, odd)], axis=1
    )


def chip_of(owner, n_index):
    return lax.div(lax.div(owner, n_index), 2) * n_index + lax.rem(owner, n_index)


def slot_plan(aims, block, shard):
    total_q = aims.shape[1]
    half = total_q // 2
    n_index = size(INDEX)
    n_yh = lax.axis_size("yh")
    owner = lax.div(aims, shard)
    chip = chip_of(owner, n_index)
    query = iota((1, total_q), 1)
    part = lax.div(query, block)
    key = (part * (size(ALL) // 2) + chip).astype(F32)
    down = columns_of(key)[:, 0:1]
    earlier = (down == key) & (iota((total_q, 1), 0) < query)
    rank = jnp.sum(earlier.astype(F32), axis=0, keepdims=True)
    rounds = lax.div(jnp.max(rank, axis=1, keepdims=True).astype(jnp.int32), SLOTS) + 1
    rank = rank.astype(jnp.int32)
    fits = rank < SLOTS
    slot = jnp.where((chip == index(("yl",) + INDEX)) & fits, part * 8 + rank, -1)
    count = total_q // block * 8
    match = slot == iota((count, 1), 0)
    found = jnp.sum(jnp.where(match, (aims + 1).astype(F32), 0.0), axis=1, keepdims=True)
    along = lax.rem(chip, n_index)
    peer = lax.div(chip, n_index) * n_yh + lax.rem(along, n_yh)
    near = (lax.div(along, n_yh) == index(PLANE)) & fits
    code = jnp.where(near, peer * (block + 8) + block + rank, -1)[:, :half]
    return found.astype(jnp.int32) - 1, code.astype(F32), rounds


def first_kernel(every, passages, positive, sent, terms, notes, slots, rounds):
    shard, width = passages.shape
    half = terms.shape[1]
    core = lax.axis_index("core")
    base = index(ALL) * shard
    down = base + iota((shard, 1), 0)
    scale = 1.0 / math.sqrt(width)
    aims = own_first(positive[...], every.shape[2], core == 1)
    wanted, code, rounds[...] = slot_plan(aims, half // size(RING), shard)
    found = []
    for side in (1, 0):
        block = every[:, lax.rem(core + side, 2)].reshape(half, width)
        score = scale * lax.dot_general(
            passages[...], block, (((1,), (1,)), ((), ())), preferred_element_type=F32
        )
        hit = aims[:, side * half : (side + 1) * half] == down
        others = jnp.where(hit, LOW, score)
        only = jnp.max(jnp.where(hit, score, LOW), axis=0, keepdims=True)
        picked = jnp.where(only > LOW, only, 0.0)
        top = jnp.max(others, axis=0, keepdims=True)
        term = jnp.exp(others - top)
        total = jnp.sum(term, axis=0, keepdims=True)
        high = jnp.maximum(top, only)
        level = high + jnp.log(total * jnp.exp(top - high) + jnp.exp(only - high))
        share = jnp.exp(top - level)
        term = (term * share).astype(BF16)
        if side:
            pulled = lax.dot_general(
                term, passages[...], (((0,), (0,)), ((), ())), preferred_element_type=F32
            )
            sent[:half] = pulled.astype(BF16)
        else:
            terms[...] = term
        found.append((level, total * share, parted_sum(picked)))
    (level2, rest2, sum2), (level1, rest1, sum1) = found
    sums = [a + b for a, b in zip(sum1, sum2)]
    swapped = core == 1
    level = jnp.concatenate(
        [jnp.where(swapped, level2, level1), jnp.where(swapped, level1, level2)], axis=1
    )
    match = (wanted == base + iota((1, shard), 1)).astype(BF16)
    rows = jnp.dot(match, passages[...], preferred_element_type=F32)
    count = rows.shape[0] // 2
    slots[...] = rows[:count].astype(BF16)
    tail = rows[count:]
    tail = jnp.concatenate([tail[:8] + notes_out(level, rest2, sums), tail[8:]], axis=0)
    sent[half:] = tail.astype(BF16)
    notes[...] = notes_out_plain(level, rest1, sums, code)


def notes_out_plain(level, rest, sums, code):
    value = jnp.concatenate([level, rest], axis=1)
    code = jnp.concatenate([code, jnp.zeros(level.shape, F32)], axis=1)
    lane = iota((1, value.shape[1]), 1)
    row = jnp.where(lane == 0, sums[0], jnp.where(lane == 1, sums[1], jnp.where(lane == 2, sums[2], 0.0)))
    sub = iota((8, value.shape[1]), 0)
    return jnp.where(sub == 0, value, jnp.where(sub == 1, row, jnp.where(sub == 2, code, 0.0)))


def own_kernel(terms, passages, pulled):
    pulled[...] = lax.dot_general(
        terms[...], passages[...], (((0,), (0,)), ((), ())), preferred_element_type=F32
    )


def chip_kernel(came, pulled, notes, slots, sent):
    half, width = pulled.shape
    total_q = 2 * half
    blocks = sent.shape[0]
    rows = half // blocks
    core = lax.axis_index("core")
    other = came[half:].astype(F32)
    level2, rest2, last = notes_in(other[:8], total_q)
    sums2 = sums_in(last, iota(last.shape, 1), total_q)
    level1, rest1 = notes[0:1, :total_q], notes[0:1, total_q:]
    sums = [notes[1:2, i : i + 1] + sums2[i] for i in range(3)]
    level = log_sum(jnp.concatenate([level1, level2], axis=0))
    swapped = core == 1

    def kept(value):
        return jnp.where(swapped, value[:, half:], value[:, :half])

    keep1 = jnp.exp(kept(level1) - kept(level))
    keep2 = jnp.exp(kept(level2) - kept(level))
    tile = notes_out(level, rest1 * keep1 + rest2 * keep2, sums)
    keeps = columns_of(jnp.concatenate([keep1, keep2], axis=0))
    both = pulled[...] * keeps[:, 0:1] + came[:half].astype(F32) * keeps[:, 1:2]
    mine = slots[...].astype(F32)
    clean = jnp.where(iota((8, width), 0) < 5, other[:8], 0.0)
    other = jnp.concatenate([clean, other[8:]], axis=0) + mine
    for b in range(blocks):
        block = jnp.concatenate(
            [both[b * rows : (b + 1) * rows], other[b * 8 : (b + 1) * 8] + tile], axis=0
        )
        sent[b] = block.astype(BF16)


def ring_kernel(got, notes, extra, sent, turned):
    peers, height, width = got.shape
    rows = height - 8
    planes = sent.shape[0]
    half = rows * peers
    total_q = 2 * half
    core = lax.axis_index("core")
    parts = [got[s].astype(F32) for s in range(peers)]
    read = [notes_in(p[rows:], total_q) for p in parts]
    levels = jnp.concatenate([r[0] for r in read], axis=0)
    rests = jnp.concatenate([r[1] for r in read], axis=0)
    last = jnp.concatenate([r[2] for r in read], axis=0)
    sums = sums_in(last, iota(last.shape, 1), total_q)
    level = log_sum(levels)
    keep = jnp.exp(levels - level)
    swapped = core == 1
    keep = jnp.where(swapped, keep[:, half:], keep[:, :half])
    own = jnp.where(swapped, level[:, half:], level[:, :half])
    rest = jnp.sum(rests * keep, axis=0, keepdims=True)
    turned[...] = columns_of(jnp.concatenate([keep, rest, own, notes[2:3, :half]], axis=0))
    cols = turned[pl.ds(pl.multiple_of(index(RING) * rows, 8), rows), :]
    pulled = parts[0][:rows] * cols[:, 0:1]
    for s in range(1, peers):
        pulled = pulled + parts[s][:rows] * cols[:, s : s + 1]
    whole = jnp.concatenate(parts, axis=0).astype(BF16)
    code = cols[:, peers + 2 : peers + 3].astype(jnp.int32)
    fits = (code == iota((rows, peers * height), 1)).astype(BF16)
    chosen = jnp.dot(fits, whole, preferred_element_type=F32) + extra[...]
    lane = iota((rows, LANES), 1)
    beside = sums_out(sums, lane, 16)
    for i, term in enumerate(split3(cols[:, peers + 1 : peers + 2]) + split3(cols[:, peers : peers + 1])):
        beside = jnp.where(lane == i, term, beside)
    chunks = total_q // LANES
    sub = iota((16, LANES), 0)
    wide = jnp.zeros((16, LANES), F32)
    for t, term in enumerate(split3(level)):
        for j in range(chunks):
            wide = jnp.where(sub == t * chunks + j, term[:, j * LANES : (j + 1) * LANES], wide)
    across = width // LANES
    for d in range(planes):
        r, c = d // across, d % across
        if r * 8 < rows:
            here, span = slice(r * 8, r * 8 + 8), slice(c * LANES, (c + 1) * LANES)
            tile = [pulled[here, span], chosen[here, span], beside[here]]
        else:
            tile = [jnp.zeros((16, LANES), F32), beside[:8]]
        sent[d] = jnp.concatenate(tile + [wide], axis=0).astype(BF16)


def make_plane_kernel(total_q, scale):
    chunks = total_q // LANES

    def plane_kernel(got, sent, level, loss):
        peers = got.shape[0]
        lane = iota((8, LANES), 1)
        tops, rests, wides = [], [], []
        chosen = jnp.zeros((8, LANES), F32)
        beside = jnp.zeros((8, LANES), F32)
        for s in range(peers):
            part = got[s].astype(F32)
            note = part[16:24]
            tops.append(jnp.sum(jnp.where(lane < 3, note, 0.0), axis=1, keepdims=True))
            rests.append(
                jnp.sum(jnp.where((lane >= 3) & (lane < 6), note, 0.0), axis=1, keepdims=True)
            )
            wide = part[24:]
            wides.append(wide[:chunks] + wide[chunks : 2 * chunks] + wide[2 * chunks : 3 * chunks])
            chosen = chosen + part[8:16]
            beside = beside + note
        high, top = wides[0], tops[0]
        for s in range(1, peers):
            high, top = jnp.maximum(high, wides[s]), jnp.maximum(top, tops[s])
        total = jnp.zeros((chunks, LANES), F32)
        full = jnp.zeros((8, 1), F32)
        rest = jnp.zeros((8, 1), F32)
        pulled = jnp.zeros((8, LANES), F32)
        for s in range(peers):
            total = total + jnp.exp(wides[s] - high)
            keep = jnp.exp(tops[s] - top)
            full = full + keep
            rest = rest + keep * rests[s]
            pulled = pulled + keep * got[s].astype(F32)[:8]
        lse = high + jnp.log(total)
        tile = ((pulled - rest * chosen) / full * (scale / total_q)).astype(BF16)
        for d in range(sent.shape[0]):
            sent[d] = tile
        level[...] = lse
        picked = sums_in(beside[0:1], lane[0:1], 16)
        terms = [a - b for a, b in zip(parted_sum(lse), picked)]
        loss[...] = (terms[0] + terms[1] + terms[2]) * (1.0 / total_q)

    return plane_kernel


def passage_kernel(passages, level, every, positive, out):
    shard, width = out.shape
    group = every.shape[2]
    half = every.shape[0] * group
    total_q = 2 * half
    core = lax.axis_index("core")
    down = index(ALL) * shard + iota((shard, 1), 0)
    scale = 1.0 / math.sqrt(width)
    aims = own_first(positive[...], group, core == 1)
    total = None
    for side in range(2):
        which = lax.rem(core + side, 2)
        block = every[:, which].reshape(half, width)
        score = scale * lax.dot_general(
            passages[...], block, (((1,), (1,)), ((), ())), preferred_element_type=F32
        )
        chunks = half // LANES
        lse = jnp.concatenate(
            [level[pl.ds(which * chunks + j, 1), :] for j in range(chunks)], axis=1
        )
        hit = aims[:, side * half : (side + 1) * half] == down
        weight = (jnp.exp(score - lse) - hit.astype(F32)) * (1.0 / total_q)
        term = jnp.dot(weight.astype(BF16), block, preferred_element_type=F32)
        total = term if total is None else total + term
    out[...] = (total * scale).astype(BF16)


def make_assembly(down, across):
    def assembly(tiles, out):
        per = tiles.shape[0] // (out.shape[0] // (8 * down))
        for y in range(out.shape[0] // (8 * down)):
            for r in range(0, down, 2):
                for c in range(across):
                    pair = [tiles[y * per + (r + i) * across + c].astype(F32) for i in range(2)]
                    row = (y * down + r) * 8
                    out[row : row + 16, c * LANES : (c + 1) * LANES] = jnp.concatenate(
                        pair, axis=0
                    ).astype(BF16)

    return assembly


def on_device(queries, passages, positive):
    group, width = queries.shape
    scale = 1.0 / math.sqrt(width)
    total_q = positive.shape[0]
    half = total_q // 2
    shard = passages.shape[0]
    n_index = size(INDEX)
    n_ring = size(RING)
    n_plane = size(PLANE)
    block = half // n_ring
    core = lax.axis_index("core")
    n_yl, n_yh = lax.axis_size("yl"), lax.axis_size("yh")
    columns = lax.axis_index(ALL) * shard + jnp.arange(shard, dtype=jnp.int32)

    def swap(value):
        return lax.ppermute(value, "core", [(0, 1), (1, 0)])

    every = lax.all_gather(queries, QUERY, axis=0, tiled=True).reshape(n_yl, 2, group, width)
    row = positive.reshape(1, total_q)
    product = 2 * total_q * shard * width
    sent, terms, notes, own_slots, rounds = call(
        first_kernel,
        [
            shaped((half + 8 * n_ring, width), BF16),
            shaped((shard, half), BF16),
            shaped((8, width), F32),
            shaped((8 * n_ring, width), BF16),
            shaped((1, 1), jnp.int32),
        ],
        [every, passages, row],
        2 * product,
    )
    came = swap(sent)
    (pulled,) = call(own_kernel, [shaped((half, width), F32)], [terms, passages], product // 2)
    (sent,) = call(
        chip_kernel,
        [shaped((n_ring, block + 8, width), BF16)],
        [came, pulled, notes, own_slots],
        half * width * 8,
    )

    def later_turn(turn, held):
        late, turn = lax.optimization_barrier((positive, turn))
        aims = late.reshape(n_yl, 2, group).transpose(1, 0, 2).reshape(2, n_ring, block)
        aims = jnp.where(core == 0, aims, aims[::-1])
        chip = chip_of(aims // shard, n_index)
        same = chip[..., :, None] == chip[..., None, :]
        before = jnp.arange(block)[:, None] > jnp.arange(block)[None, :]
        rank = jnp.sum((same & before).astype(jnp.int32), axis=-1)
        slots = turn * SLOTS + jnp.arange(SLOTS, dtype=jnp.int32)
        fits = (chip == index(("yl",) + INDEX))[..., None] & (rank[..., None] == slots)
        wanted = jnp.max(jnp.where(fits, aims[..., None], -1), axis=2)
        columns = lax.axis_index(ALL) * shard + jnp.arange(shard, dtype=jnp.int32)
        match = (wanted.reshape(-1)[:, None] == columns[None, :]).astype(BF16)
        rows = jnp.dot(match, passages, preferred_element_type=F32).astype(BF16)
        rows = rows.reshape(2, n_ring, SLOTS, width)
        rows = lax.all_to_all(rows[0] + swap(rows[1]), RING, 0, 0, tiled=True)
        place = lax.axis_index(RING)
        my_chip = lax.dynamic_index_in_dim(chip[0], place, 0, keepdims=False)
        my_rank = lax.dynamic_index_in_dim(rank[0], place, 0, keepdims=False)
        peer = jnp.arange(n_ring, dtype=jnp.int32)
        peer_chip = (peer // n_yh) * n_index + lax.axis_index(PLANE) * n_yh + peer % n_yh
        fits = (my_chip[:, None] == peer_chip[None, :])[..., None]
        fits = (fits & (my_rank[:, None, None] == slots)).astype(BF16)
        fits = fits.reshape(block, n_ring * SLOTS)
        return held + jnp.dot(fits, rows.reshape(-1, width), preferred_element_type=F32)

    extra = lax.fori_loop(1, rounds[0, 0], later_turn, jnp.zeros((block, width), F32))
    got = lax.all_to_all(sent, RING, 0, 0, tiled=True)
    (sent,) = call(
        ring_kernel,
        [shaped((n_plane, 40, LANES), BF16)],
        [got, notes, extra],
        half * width * 8,
        [pltpu.VMEM((half, LANES), F32)],
    )
    got = lax.all_to_all(sent, PLANE, 0, 0, tiled=True)
    spread = n_plane * n_yh
    sent, level, loss = call(
        make_plane_kernel(total_q, scale),
        [
            shaped((spread, 8, LANES), BF16),
            shaped((total_q // LANES, LANES), F32),
            shaped((1, 1), F32),
        ],
        [got],
        half * width * 8,
    )
    tiles = lax.all_to_all(sent, SPREAD, 0, 0, tiled=True)
    (passage_grad,) = call(
        passage_kernel,
        [shaped((shard, width), BF16)],
        [passages, level, every, row],
        2 * product,
    )
    (query_grad,) = call(
        make_assembly(block // 8, width // LANES),
        [shaped((group, width), BF16)],
        [tiles],
        group * width,
    )
    return (loss[0, 0], query_grad, passage_grad)


def build(mesh):
    return jax.shard_map(
        on_device,
        mesh=mesh,
        in_specs=(P(QUERY, None), P(ALL, None), P()),
        out_specs=(P(), P(QUERY, None), P(ALL, None)),
        check_vma=False,
    )


def solution(mesh):
    devices = np.asarray(mesh.devices).reshape(4, 2, 4, 8, 2)
    return build(Mesh(devices, ("yl", "core", "x", "z", "yh")))
```

```python
import math

import jax
import jax.numpy as jnp
import numpy as np
from jax import lax
from jax.experimental import pallas as pl
from jax.experimental.pallas import tpu as pltpu
from jax.sharding import Mesh
from jax.sharding import PartitionSpec as P

QUERY = ("yl", "core")
INDEX = ("x", "z", "yh")
ALL = QUERY + INDEX
PLANE = ("x", "z")
RING = ("yl", "yh")
SPREAD = ("yh", "x", "z")
LOW = -1e30
SLOTS = 5
LANES = 128
F32 = jnp.float32
BF16 = jnp.bfloat16


def size(axes):
    return math.prod(lax.axis_size(a) for a in axes)


def index(axes):
    place = 0
    for a in axes:
        place = place * lax.axis_size(a) + lax.axis_index(a)
    return place


def call(body, outs, ins, flops, scratch=()):
    moved = sum(math.prod(o.shape) * o.dtype.itemsize for o in list(outs) + list(ins))
    return pl.pallas_call(
        body,
        out_shape=tuple(outs),
        scratch_shapes=list(scratch),
        cost_estimate=pl.CostEstimate(flops=flops, bytes_accessed=moved, transcendentals=0),
        compiler_params=pltpu.CompilerParams(vmem_limit_bytes=40 << 20),
    )(*ins)


def shaped(shape, dtype):
    return jax.ShapeDtypeStruct(shape, dtype)


def iota(shape, dim):
    return lax.broadcasted_iota(jnp.int32, shape, dim)


def split3(value):
    a = value.astype(BF16).astype(F32)
    b = (value - a).astype(BF16).astype(F32)
    c = (value - a - b).astype(BF16).astype(F32)
    return a, b, c


def parted_sum(values):
    coarse = jnp.round(values * (1 / 16)) * 16.0
    middle = jnp.round((values - coarse) * 64.0) * (1 / 64)
    parts = (coarse, middle, values - coarse - middle)
    return [jnp.sum(p, axis=(0, 1), keepdims=True) for p in parts]


def sums_out(sums, lane, first):
    spread = jnp.zeros(lane.shape, F32)
    for i in range(3):
        spread = jnp.where((lane - first) % 3 == i, sums[i], spread)
    a, b, c = split3(spread)
    terms = jnp.where(lane < first + 3, a, jnp.where(lane < first + 6, b, c))
    return jnp.where((lane >= first) & (lane < first + 9), terms, 0.0)


def sums_in(terms, lane, first):
    inside = (lane >= first) & (lane < first + 9)
    return [
        jnp.sum(jnp.where(inside & ((lane - first) % 3 == i), terms, 0.0), axis=(0, 1), keepdims=True)
        for i in range(3)
    ]


def notes_out(level, rest, sums, width):
    count = 2 * level.shape[1]
    value = jnp.concatenate([level, rest, jnp.zeros((1, width - count), F32)], axis=1)
    lane = iota((1, width), 1)
    a, b, c = split3(value)
    c = jnp.where(lane < count, c, sums_out(sums, lane, count))
    sub = iota((8, width), 0)
    return jnp.where(sub == 5, a, jnp.where(sub == 6, b, jnp.where(sub == 7, c, 0.0)))


def notes_in(tile, half):
    a, b, c = tile[5:6], tile[6:7], tile[7:8]
    value = a + b + c
    return value[:, :half], value[:, half : 2 * half], c


def log_sum(values):
    high = jnp.max(values, axis=0, keepdims=True)
    return high + jnp.log(jnp.sum(jnp.exp(values - high), axis=0, keepdims=True))


def columns_of(rows):
    fill = jnp.zeros((LANES - rows.shape[0], rows.shape[1]), F32)
    return jnp.concatenate([rows, fill], axis=0).T


def own_first(positive, group, swapped):
    count = positive.shape[1] // (2 * group)
    even = [positive[:, 2 * i * group : (2 * i + 1) * group] for i in range(count)]
    odd = [positive[:, (2 * i + 1) * group : (2 * i + 2) * group] for i in range(count)]
    even, odd = jnp.concatenate(even, axis=1), jnp.concatenate(odd, axis=1)
    return jnp.concatenate(
        [jnp.where(swapped, odd, even), jnp.where(swapped, even, odd)], axis=1
    )


def chip_of(owner, n_index):
    return lax.div(lax.div(owner, n_index), 2) * n_index + lax.rem(owner, n_index)


def slot_plan(aims, block, shard):
    total_q = aims.shape[1]
    half = total_q // 2
    n_index = size(INDEX)
    n_yh = lax.axis_size("yh")
    owner = lax.div(aims, shard)
    chip = chip_of(owner, n_index)
    query = iota((1, total_q), 1)
    part = lax.div(query, block)
    key = (part * (size(ALL) // 2) + chip).astype(F32)
    down = columns_of(key)[:, 0:1]
    earlier = (down == key) & (iota((total_q, 1), 0) < query)
    rank = jnp.sum(earlier.astype(F32), axis=0, keepdims=True)
    rounds = lax.div(jnp.max(rank, axis=1, keepdims=True).astype(jnp.int32), SLOTS) + 1
    rank = rank.astype(jnp.int32)
    fits = rank < SLOTS
    slot = jnp.where((chip == index(("yl",) + INDEX)) & fits, part * 8 + rank, -1)
    count = half // block * 8
    match = slot[:, :half] == iota((count, 1), 0)
    found = jnp.sum(jnp.where(match, (aims[:, :half] + 1).astype(F32), 0.0), axis=1, keepdims=True)
    along = lax.rem(chip, n_index)
    peer = lax.div(chip, n_index) * n_yh + lax.rem(along, n_yh)
    near = (lax.div(along, n_yh) == index(PLANE)) & fits
    code = jnp.where(near, peer * (block + 8) + block + rank, -1)[:, :half]
    return found.astype(jnp.int32) - 1, code.astype(F32), rounds


def copies_kernel(value, out):
    for i in range(out.shape[0]):
        out[i] = value[...]


def first_kernel(queries, passages, partner, positive, sent, notes, rounds):
    shard, width = passages.shape
    group = queries.shape[1]
    half = queries.shape[0] * group
    blocks = sent.shape[0]
    rows = half // blocks
    core = lax.axis_index("core")
    scale = 1.0 / math.sqrt(width)
    bases = [
        (index(("yl",)) * 2 + c) * (size(INDEX) * shard) + index(INDEX) * shard
        for c in (core, 1 - core)
    ]
    tables = [passages, partner]
    aims = own_first(positive[...], group, core == 1)
    wanted, code, rounds[...] = slot_plan(aims, rows, shard)
    notes[...] = jnp.broadcast_to(code, notes.shape)
    block = queries[...].reshape(half, width)
    others, top, only = [], None, None
    for base, table in zip(bases, tables):
        score = scale * lax.dot_general(
            table[...], block, (((1,), (1,)), ((), ())), preferred_element_type=F32
        )
        hit = aims[:, :half] == base + iota((shard, 1), 0)
        others.append(jnp.where(hit, LOW, score))
        high = jnp.max(others[-1], axis=0, keepdims=True)
        one = jnp.max(jnp.where(hit, score, LOW), axis=0, keepdims=True)
        top = high if top is None else jnp.maximum(top, high)
        only = one if only is None else jnp.maximum(only, one)
    picked = jnp.where(only > LOW, only, 0.0)
    terms = [jnp.exp(o - top) for o in others]
    total = sum(jnp.sum(t, axis=0, keepdims=True) for t in terms)
    high = jnp.maximum(top, only)
    level = high + jnp.log(total * jnp.exp(top - high) + jnp.exp(only - high))
    share = jnp.exp(top - level)
    pulled, slots = 0.0, 0.0
    for base, table, term in zip(bases, tables, terms):
        pulled = pulled + lax.dot_general(
            (term * share).astype(BF16),
            table[...],
            (((0,), (0,)), ((), ())),
            preferred_element_type=F32,
        )
        match = (wanted == base + iota((1, shard), 1)).astype(BF16)
        slots = slots + jnp.dot(match, table[...], preferred_element_type=F32)
    tile = notes_out(level, total * share, parted_sum(picked), width)
    for b in range(blocks):
        piece = [pulled[b * rows : (b + 1) * rows], slots[b * 8 : (b + 1) * 8] + tile]
        sent[b] = jnp.concatenate(piece, axis=0).astype(BF16)


def ring_kernel(got, notes, extra, sent, turned):
    peers, height, width = got.shape
    rows = height - 8
    planes = sent.shape[0]
    half = rows * peers
    parts = [got[s].astype(F32) for s in range(peers)]
    read = [notes_in(p[rows:], half) for p in parts]
    levels = jnp.concatenate([r[0] for r in read], axis=0)
    rests = jnp.concatenate([r[1] for r in read], axis=0)
    last = jnp.concatenate([r[2] for r in read], axis=0)
    sums = sums_in(last, iota(last.shape, 1), 2 * half)
    level = log_sum(levels)
    keep = jnp.exp(levels - level)
    rest = jnp.sum(rests * keep, axis=0, keepdims=True)
    turned[...] = columns_of(jnp.concatenate([keep, rest, level, notes[0:1]], axis=0))
    cols = turned[pl.ds(pl.multiple_of(index(RING) * rows, 8), rows), :]
    pulled = parts[0][:rows] * cols[:, 0:1]
    for s in range(1, peers):
        pulled = pulled + parts[s][:rows] * cols[:, s : s + 1]
    whole = jnp.concatenate(parts, axis=0).astype(BF16)
    code = cols[:, peers + 2 : peers + 3].astype(jnp.int32)
    fits = (code == iota((rows, peers * height), 1)).astype(BF16)
    chosen = jnp.dot(fits, whole, preferred_element_type=F32) + extra[...]
    lane = iota((rows, LANES), 1)
    beside = sums_out(sums, lane, 16)
    for i, term in enumerate(split3(cols[:, peers + 1 : peers + 2]) + split3(cols[:, peers : peers + 1])):
        beside = jnp.where(lane == i, term, beside)
    chunks = half // LANES
    sub = iota((8, LANES), 0)
    wide = jnp.zeros((8, LANES), F32)
    for t, term in enumerate(split3(level)):
        for j in range(chunks):
            wide = jnp.where(sub == t * chunks + j, term[:, j * LANES : (j + 1) * LANES], wide)
    across = width // LANES
    for d in range(planes):
        r, c = d // across, d % across
        if r * 8 < rows:
            here, span = slice(r * 8, r * 8 + 8), slice(c * LANES, (c + 1) * LANES)
            tile = [pulled[here, span], chosen[here, span], beside[here]]
        else:
            tile = [jnp.zeros((16, LANES), F32), beside[:8]]
        sent[d] = jnp.concatenate(tile + [wide], axis=0).astype(BF16)


def make_plane_kernel(total_q, scale):
    chunks = total_q // 2 // LANES

    def plane_kernel(got, sent, level):
        peers = got.shape[0]
        lane = iota((8, LANES), 1)
        tops, rests, wides = [], [], []
        chosen = jnp.zeros((8, LANES), F32)
        beside = jnp.zeros((8, LANES), F32)
        for s in range(peers):
            part = got[s].astype(F32)
            note = part[16:24]
            tops.append(jnp.sum(jnp.where(lane < 3, note, 0.0), axis=1, keepdims=True))
            rests.append(
                jnp.sum(jnp.where((lane >= 3) & (lane < 6), note, 0.0), axis=1, keepdims=True)
            )
            wide = part[24:]
            wides.append(wide[:chunks] + wide[chunks : 2 * chunks] + wide[2 * chunks : 3 * chunks])
            chosen = chosen + part[8:16]
            beside = beside + note
        high, top = wides[0], tops[0]
        for s in range(1, peers):
            high, top = jnp.maximum(high, wides[s]), jnp.maximum(top, tops[s])
        total = jnp.zeros((chunks, LANES), F32)
        full = jnp.zeros((8, 1), F32)
        rest = jnp.zeros((8, 1), F32)
        pulled = jnp.zeros((8, LANES), F32)
        for s in range(peers):
            total = total + jnp.exp(wides[s] - high)
            keep = jnp.exp(tops[s] - top)
            full = full + keep
            rest = rest + keep * rests[s]
            pulled = pulled + keep * got[s].astype(F32)[:8]
        lse = high + jnp.log(total)
        tile = ((pulled - rest * chosen) / full * (scale / total_q)).astype(BF16)
        for d in range(sent.shape[0]):
            sent[d] = tile
        picked = sums_in(beside[0:1], lane[0:1], 16)
        terms = [a - b for a, b in zip(parted_sum(lse), picked)]
        for i in range(3):
            level[chunks + i : chunks + i + 1, :] = jnp.broadcast_to(terms[i], (1, LANES))
        level[:chunks, :] = lse

    return plane_kernel


def passage_kernel(passages, level, level2, queries, queries2, positive, out, loss):
    shard, width = out.shape
    group = queries.shape[1]
    half = queries.shape[0] * group
    total_q = 2 * half
    chunks = half // LANES
    core = lax.axis_index("core")
    down = index(ALL) * shard + iota((shard, 1), 0)
    scale = 1.0 / math.sqrt(width)
    aims = own_first(positive[...], group, core == 1)
    total = None
    for side, (block, logs) in enumerate([(queries, level), (queries2, level2)]):
        block = block[...].reshape(half, width)
        score = scale * lax.dot_general(
            passages[...], block, (((1,), (1,)), ((), ())), preferred_element_type=F32
        )
        lse = jnp.concatenate([logs[j : j + 1, :] for j in range(chunks)], axis=1)
        hit = aims[:, side * half : (side + 1) * half] == down
        weight = (jnp.exp(score - lse) - hit.astype(F32)) * (1.0 / total_q)
        term = jnp.dot(weight.astype(BF16), block, preferred_element_type=F32)
        total = term if total is None else total + term
    out[...] = (total * scale).astype(BF16)
    parts = level[chunks : chunks + 3, 0:1] + level2[chunks : chunks + 3, 0:1]
    loss[...] = (parts[0:1] + parts[1:2] + parts[2:3]) * (1.0 / total_q)


def make_assembly(down, across):
    def assembly(tiles, out):
        per = tiles.shape[0] // (out.shape[0] // (8 * down))
        for y in range(out.shape[0] // (8 * down)):
            for r in range(0, down, 2):
                for c in range(across):
                    pair = [tiles[y * per + (r + i) * across + c].astype(F32) for i in range(2)]
                    row = (y * down + r) * 8
                    out[row : row + 16, c * LANES : (c + 1) * LANES] = jnp.concatenate(
                        pair, axis=0
                    ).astype(BF16)

    return assembly


def on_device(queries, passages, positive):
    group, width = queries.shape
    scale = 1.0 / math.sqrt(width)
    total_q = positive.shape[0]
    half = total_q // 2
    shard = passages.shape[0]
    n_index = size(INDEX)
    n_ring = size(RING)
    n_plane = size(PLANE)
    block = half // n_ring
    core = lax.axis_index("core")
    n_yl, n_yh = lax.axis_size("yl"), lax.axis_size("yh")
    columns = lax.axis_index(ALL) * shard + jnp.arange(shard, dtype=jnp.int32)

    def swap(value):
        return lax.ppermute(value, "core", [(0, 1), (1, 0)])

    row = positive.reshape(1, total_q)
    product = total_q * shard * width
    (copies,) = call(copies_kernel, [shaped((n_yl, group, width), BF16)], [queries], group * width)
    mine = lax.all_to_all(copies, "yl", 0, 0, tiled=True)
    partner = swap(passages)
    sent, notes, rounds = call(
        first_kernel,
        [
            shaped((n_ring, block + 8, width), BF16),
            shaped((8, half), F32),
            shaped((1, 1), jnp.int32),
        ],
        [mine, passages, partner, row],
        4 * product,
    )

    def later_turn(turn, held):
        late, turn = lax.optimization_barrier((positive, turn))
        aims = late.reshape(n_yl, 2, group).transpose(1, 0, 2).reshape(2, n_ring, block)
        aims = jnp.where(core == 0, aims, aims[::-1])
        chip = chip_of(aims // shard, n_index)
        same = chip[..., :, None] == chip[..., None, :]
        before = jnp.arange(block)[:, None] > jnp.arange(block)[None, :]
        rank = jnp.sum((same & before).astype(jnp.int32), axis=-1)
        slots = turn * SLOTS + jnp.arange(SLOTS, dtype=jnp.int32)
        fits = (chip[0] == index(("yl",) + INDEX))[..., None] & (rank[0][..., None] == slots)
        wanted = jnp.max(jnp.where(fits, aims[0][..., None], -1), axis=1).reshape(-1, 1)
        rows = 0.0
        for side, table in ((core, passages), (1 - core, partner)):
            owner = (lax.axis_index("yl") * 2 + side) * n_index + lax.axis_index(INDEX)
            match = (wanted == owner * shard + jnp.arange(shard, dtype=jnp.int32)).astype(BF16)
            rows = rows + jnp.dot(match, table, preferred_element_type=F32)
        rows = rows.astype(BF16).reshape(n_ring, SLOTS, width)
        rows = lax.all_to_all(rows, RING, 0, 0, tiled=True)
        place = lax.axis_index(RING)
        my_chip = lax.dynamic_index_in_dim(chip[0], place, 0, keepdims=False)
        my_rank = lax.dynamic_index_in_dim(rank[0], place, 0, keepdims=False)
        peer = jnp.arange(n_ring, dtype=jnp.int32)
        peer_chip = (peer // n_yh) * n_index + lax.axis_index(PLANE) * n_yh + peer % n_yh
        fits = (my_chip[:, None] == peer_chip[None, :])[..., None]
        fits = (fits & (my_rank[:, None, None] == slots)).astype(BF16)
        fits = fits.reshape(block, n_ring * SLOTS)
        return held + jnp.dot(fits, rows.reshape(-1, width), preferred_element_type=F32)

    extra = lax.fori_loop(1, rounds[0, 0], later_turn, jnp.zeros((block, width), F32))
    got = lax.all_to_all(sent, RING, 0, 0, tiled=True)
    theirs = swap(mine)
    (sent,) = call(
        ring_kernel,
        [shaped((n_plane, 32, LANES), BF16)],
        [got, notes, extra],
        half * width * 8,
        [pltpu.VMEM((half, LANES), F32)],
    )
    got = lax.all_to_all(sent, PLANE, 0, 0, tiled=True)
    spread = n_plane * n_yh
    sent, level = call(
        make_plane_kernel(total_q, scale),
        [shaped((spread, 8, LANES), BF16), shaped((8, LANES), F32)],
        [got],
        half * width * 8,
    )
    tiles = lax.all_to_all(sent, SPREAD, 0, 0, tiled=True)
    passage_grad, loss = call(
        passage_kernel,
        [shaped((shard, width), BF16), shaped((1, 1), F32)],
        [passages, level, swap(level), mine, theirs, row],
        4 * product,
    )
    (query_grad,) = call(
        make_assembly(block // 8, width // LANES),
        [shaped((group, width), BF16)],
        [tiles],
        group * width,
    )
    return (loss[0, 0], query_grad, passage_grad)


def build(mesh):
    return jax.shard_map(
        on_device,
        mesh=mesh,
        in_specs=(P(QUERY, None), P(ALL, None), P()),
        out_specs=(P(), P(QUERY, None), P(ALL, None)),
        check_vma=False,
    )


def solution(mesh):
    devices = np.asarray(mesh.devices).reshape(4, 2, 4, 8, 2)
    return build(Mesh(devices, ("yl", "core", "x", "z", "yh")))
```

```python
import math

import jax
import jax.numpy as jnp
import numpy as np
from jax import lax
from jax.experimental import pallas as pl
from jax.experimental.pallas import tpu as pltpu
from jax.sharding import Mesh
from jax.sharding import PartitionSpec as P

QUERY = ("yl", "core")
INDEX = ("x", "z", "yh")
ALL = QUERY + INDEX
LINE = ("x",)
REST = ("yl", "z", "yh")
LOW = -1e30
TAIL = 16
SLOTS = TAIL - 3
LANES = 128
F32 = jnp.float32
BF16 = jnp.bfloat16


def size(axes):
    return math.prod(lax.axis_size(a) for a in axes)


def index(axes):
    place = 0
    for a in axes:
        place = place * lax.axis_size(a) + lax.axis_index(a)
    return place


def call(body, outs, ins, flops, scratch=(), **specs):
    moved = sum(math.prod(o.shape) * o.dtype.itemsize for o in list(outs) + list(ins))
    return pl.pallas_call(
        body,
        out_shape=tuple(outs),
        scratch_shapes=list(scratch),
        **specs,
        cost_estimate=pl.CostEstimate(flops=flops, bytes_accessed=moved, transcendentals=0),
        compiler_params=pltpu.CompilerParams(vmem_limit_bytes=40 << 20),
    )(*ins)


def shaped(shape, dtype):
    return jax.ShapeDtypeStruct(shape, dtype)


def iota(shape, dim):
    return lax.broadcasted_iota(jnp.int32, shape, dim)


def split3(value):
    a = value.astype(BF16).astype(F32)
    b = (value - a).astype(BF16).astype(F32)
    c = (value - a - b).astype(BF16).astype(F32)
    return a, b, c


def parted_sum(values):
    coarse = jnp.round(values * (1 / 16)) * 16.0
    middle = jnp.round((values - coarse) * 64.0) * (1 / 64)
    parts = (coarse, middle, values - coarse - middle)
    return [jnp.sum(p, axis=(0, 1), keepdims=True) for p in parts]


def sums_out(sums, lane, first):
    spread = jnp.zeros(lane.shape, F32)
    for i in range(3):
        spread = jnp.where((lane - first) % 3 == i, sums[i], spread)
    a, b, c = split3(spread)
    terms = jnp.where(lane < first + 3, a, jnp.where(lane < first + 6, b, c))
    return jnp.where((lane >= first) & (lane < first + 9), terms, 0.0)


def sums_in(terms, lane, first):
    inside = (lane >= first) & (lane < first + 9)
    return [
        jnp.sum(jnp.where(inside & ((lane - first) % 3 == i), terms, 0.0), axis=(0, 1), keepdims=True)
        for i in range(3)
    ]


def notes_out(level, rest, sums, width):
    count = 2 * level.shape[1]
    value = jnp.concatenate([level, rest, jnp.zeros((1, width - count), F32)], axis=1)
    lane = iota((1, width), 1)
    a, b, c = split3(value)
    c = jnp.where(lane < count, c, sums_out(sums, lane, count))
    sub = iota((TAIL, width), 0) - SLOTS
    return jnp.where(sub == 0, a, jnp.where(sub == 1, b, jnp.where(sub == 2, c, 0.0)))


def notes_in(tail, half):
    a, b, c = (tail[SLOTS + i : SLOTS + i + 1] for i in range(3))
    value = a + b + c
    return value[:, :half], value[:, half : 2 * half], c


def log_sum(values):
    high = jnp.max(values, axis=0, keepdims=True)
    return high + jnp.log(jnp.sum(jnp.exp(values - high), axis=0, keepdims=True))


def columns_of(rows):
    fill = jnp.zeros((LANES - rows.shape[0], rows.shape[1]), F32)
    return jnp.concatenate([rows, fill], axis=0).T


def own_first(positive, group, swapped):
    count = positive.shape[1] // (2 * group)
    even = [positive[:, 2 * i * group : (2 * i + 1) * group] for i in range(count)]
    odd = [positive[:, (2 * i + 1) * group : (2 * i + 2) * group] for i in range(count)]
    even, odd = jnp.concatenate(even, axis=1), jnp.concatenate(odd, axis=1)
    return jnp.concatenate(
        [jnp.where(swapped, odd, even), jnp.where(swapped, even, odd)], axis=1
    )


def chip_of(owner, n_index):
    return lax.div(lax.div(owner, n_index), 2) * n_index + lax.rem(owner, n_index)


def slot_plan(aims, group, shard):
    total_q = aims.shape[1]
    half = total_q // 2
    blocks = size(LINE)
    sub = group // blocks
    n_index = size(INDEX)
    across = n_index // blocks
    chip = chip_of(lax.div(aims, shard), n_index)
    query = iota((1, total_q), 1)
    part = lax.div(lax.rem(query, group), sub) + lax.div(query, half) * blocks
    key = (part * (size(ALL) // 2) + chip).astype(F32)
    down = columns_of(key)[:, 0:1]
    earlier = (down == key) & (iota((total_q, 1), 0) < query)
    rank = jnp.sum(earlier.astype(F32), axis=0, keepdims=True)
    rounds = lax.div(jnp.max(rank, axis=1, keepdims=True).astype(jnp.int32), SLOTS) + 1
    rank = rank.astype(jnp.int32)
    fits = rank < SLOTS
    slot = jnp.where((chip == index(("yl",) + INDEX)) & fits, part * TAIL + rank, -1)
    match = slot[:, :half] == iota((blocks * TAIL, 1), 0)
    found = jnp.sum(jnp.where(match, (aims[:, :half] + 1).astype(F32), 0.0), axis=1, keepdims=True)
    along = lax.rem(chip, n_index)
    near = (lax.div(chip, n_index) == index(("yl",))) & (lax.rem(along, across) == index(("z", "yh")))
    height = half // blocks + TAIL
    code = lax.div(along, across) * height + (height - TAIL) + rank
    code = jnp.where(near & fits, code, -1)[:, :half]
    return found.astype(jnp.int32) - 1, code.astype(F32), rounds


def copies_kernel(value, out, sems):
    copies = [
        pltpu.make_async_copy(value, out.at[i], sems.at[i]) for i in range(out.shape[0])
    ]
    for copy in copies:
        copy.start()
    for copy in copies:
        copy.wait()


def first_kernel(queries, passages, partner, positive, sent, notes, rounds):
    shard, width = passages.shape
    group = queries.shape[1]
    half = queries.shape[0] * group
    blocks = sent.shape[0]
    sub = group // blocks
    core = lax.axis_index("core")
    scale = 1.0 / math.sqrt(width)
    bases = [
        (index(("yl",)) * 2 + c) * (size(INDEX) * shard) + index(INDEX) * shard
        for c in (core, 1 - core)
    ]
    tables = [passages, partner]
    aims = own_first(positive[...], group, core == 1)
    wanted, code, rounds[...] = slot_plan(aims, group, shard)
    notes[...] = jnp.broadcast_to(code, notes.shape)
    block = queries[...].reshape(half, width)
    others, top, only = [], None, None
    for base, table in zip(bases, tables):
        score = scale * lax.dot_general(
            table[...], block, (((1,), (1,)), ((), ())), preferred_element_type=F32
        )
        hit = aims[:, :half] == base + iota((shard, 1), 0)
        others.append(jnp.where(hit, LOW, score))
        high = jnp.max(others[-1], axis=0, keepdims=True)
        one = jnp.max(jnp.where(hit, score, LOW), axis=0, keepdims=True)
        top = high if top is None else jnp.maximum(top, high)
        only = one if only is None else jnp.maximum(only, one)
    picked = jnp.where(only > LOW, only, 0.0)
    terms = [jnp.exp(o - top) for o in others]
    total = sum(jnp.sum(t, axis=0, keepdims=True) for t in terms)
    high = jnp.maximum(top, only)
    level = high + jnp.log(total * jnp.exp(top - high) + jnp.exp(only - high))
    share = jnp.exp(top - level)
    pulled, slots = 0.0, 0.0
    for base, table, term in zip(bases, tables, terms):
        pulled = pulled + lax.dot_general(
            (term * share).astype(BF16),
            table[...],
            (((0,), (0,)), ((), ())),
            preferred_element_type=F32,
        )
        match = (wanted == base + iota((1, shard), 1)).astype(BF16)
        slots = slots + jnp.dot(match, table[...], preferred_element_type=F32)
    tile = notes_out(level, total * share, parted_sum(picked), width)
    for b in range(blocks):
        firsts = range(b * sub, half, group)
        piece = [pulled[i : i + sub] for i in firsts] + [slots[b * TAIL : (b + 1) * TAIL] + tile]
        sent[b] = jnp.concatenate(piece, axis=0).astype(BF16)


def line_kernel(got, notes, extra, sent, turned):
    peers, height, width = got.shape
    rows = height - TAIL
    half = rows * peers
    groups = lax.axis_size("yl")
    sub = rows // groups
    parts = [got[s].astype(F32) for s in range(peers)]
    read = [notes_in(p[rows:], half) for p in parts]
    levels = jnp.concatenate([r[0] for r in read], axis=0)
    rests = jnp.concatenate([r[1] for r in read], axis=0)
    last = jnp.concatenate([r[2] for r in read], axis=0)
    sums = sums_in(last, iota(last.shape, 1), 2 * half)
    level = log_sum(levels)
    keep = jnp.exp(levels - level)
    rest = jnp.sum(rests * keep, axis=0, keepdims=True)
    turned[...] = columns_of(jnp.concatenate([keep, rest, level, notes[0:1]], axis=0))
    first = lax.axis_index("x") * sub
    cols = jnp.concatenate(
        [turned[pl.ds(pl.multiple_of(g * sub * peers + first, 8), sub), :] for g in range(groups)],
        axis=0,
    )
    pulled = parts[0][:rows] * cols[:, 0:1]
    for s in range(1, peers):
        pulled = pulled + parts[s][:rows] * cols[:, s : s + 1]
    whole = jnp.concatenate(parts, axis=0).astype(BF16)
    code = cols[:, peers + 2 : peers + 3].astype(jnp.int32)
    fits = (code == iota((rows, peers * height), 1)).astype(BF16)
    chosen = jnp.dot(fits, whole, preferred_element_type=F32) + extra[...]
    lane = iota((rows, LANES), 1)
    beside = sums_out(sums, lane, 16)
    for i, term in enumerate(split3(cols[:, peers + 1 : peers + 2]) + split3(cols[:, peers : peers + 1])):
        beside = jnp.where(lane == i, term, beside)
    chunks = half // LANES
    down = iota((8, LANES), 0)
    wide = jnp.zeros((8, LANES), F32)
    for t, term in enumerate(split3(level)):
        for j in range(chunks):
            wide = jnp.where(down == t * chunks + j, term[:, j * LANES : (j + 1) * LANES], wide)
    across = width // LANES
    owners = sent.shape[0] // groups
    for d in range(sent.shape[0]):
        r, c = d % owners // across, d % owners % across
        if r * 8 < sub:
            at = d // owners * sub + r * 8
            here, span = slice(at, at + 8), slice(c * LANES, (c + 1) * LANES)
            tile = [pulled[here, span], chosen[here, span], beside[here]]
        else:
            tile = [jnp.zeros((16, LANES), F32), beside[:8]]
        sent[d] = jnp.concatenate(tile + [wide], axis=0).astype(BF16)


def make_last_kernel(total_q, scale):
    chunks = total_q // 2 // LANES

    def last_kernel(got, sent, level):
        peers = got.shape[0]
        lane = iota((1, LANES), 1)
        parts = [got[s].astype(F32) for s in range(peers)]
        notes = jnp.concatenate([p[16:24] for p in parts], axis=0)
        pick = iota((LANES, LANES), 0)
        tops, rests = (
            jnp.dot(notes.astype(BF16), m.astype(BF16), preferred_element_type=F32)
            for m in (pick < 3, (pick >= 3) & (pick < 6))
        )
        tops = [tops[8 * s : 8 * s + 8] for s in range(peers)]
        rests = [rests[8 * s : 8 * s + 8] for s in range(peers)]
        wides = [
            p[24 : 24 + chunks] + p[24 + chunks : 24 + 2 * chunks] + p[24 + 2 * chunks : 24 + 3 * chunks]
            for p in parts
        ]
        high, top = wides[0], tops[0]
        for s in range(1, peers):
            high, top = jnp.maximum(high, wides[s]), jnp.maximum(top, tops[s])
        total = jnp.zeros((chunks, LANES), F32)
        full, rest, pulled, chosen, beside = (jnp.zeros((8, LANES), F32) for _ in range(5))
        for s in range(peers):
            total = total + jnp.exp(wides[s] - high)
            keep = jnp.exp(tops[s] - top)
            full = full + keep
            rest = rest + keep * rests[s]
            pulled = pulled + keep * parts[s][:8]
            chosen = chosen + parts[s][8:16]
            beside = beside + parts[s][16:24]
        lse = high + jnp.log(total)
        tile = ((pulled - rest * chosen) / full * (scale / total_q)).astype(BF16)
        for d in range(sent.shape[0]):
            sent[d] = tile
        picked = sums_in(beside[0:1], lane, 16)
        terms = [a - b for a, b in zip(parted_sum(lse), picked)]
        for i in range(3):
            level[chunks + i : chunks + i + 1, :] = jnp.broadcast_to(terms[i], (1, LANES))
        level[:chunks, :] = lse

    return last_kernel


def passage_kernel(passages, level, level2, queries, queries2, positive, out, loss):
    shard, width = out.shape
    group = queries.shape[1]
    half = queries.shape[0] * group
    total_q = 2 * half
    chunks = half // LANES
    core = lax.axis_index("core")
    down = index(ALL) * shard + iota((shard, 1), 0)
    scale = 1.0 / math.sqrt(width)
    aims = own_first(positive[...], group, core == 1)
    total = None
    for side, (block, logs) in enumerate([(queries, level), (queries2, level2)]):
        block = block[...].reshape(half, width)
        score = scale * lax.dot_general(
            passages[...], block, (((1,), (1,)), ((), ())), preferred_element_type=F32
        )
        lse = jnp.concatenate([logs[j : j + 1, :] for j in range(chunks)], axis=1)
        hit = aims[:, side * half : (side + 1) * half] == down
        weight = (jnp.exp(score - lse) - hit.astype(F32)) * (1.0 / total_q)
        term = jnp.dot(weight.astype(BF16), block, preferred_element_type=F32)
        total = term if total is None else total + term
    out[...] = (total * scale).astype(BF16)
    parts = level[chunks : chunks + 3, 0:1] + level2[chunks : chunks + 3, 0:1]
    loss[...] = (parts[0:1] + parts[1:2] + parts[2:3]) * (1.0 / total_q)


def make_assembly(down, across):
    def assembly(tiles, out):
        per = tiles.shape[0] // (out.shape[0] // (8 * down))
        for y in range(out.shape[0] // (8 * down)):
            for r in range(0, down, 2):
                for c in range(across):
                    pair = [tiles[y * per + (r + i) * across + c].astype(F32) for i in range(2)]
                    row = (y * down + r) * 8
                    out[row : row + 16, c * LANES : (c + 1) * LANES] = jnp.concatenate(
                        pair, axis=0
                    ).astype(BF16)

    return assembly


def on_device(queries, passages, positive):
    group, width = queries.shape
    scale = 1.0 / math.sqrt(width)
    total_q = positive.shape[0]
    half = total_q // 2
    shard = passages.shape[0]
    n_index = size(INDEX)
    n_line = size(LINE)
    n_rest = size(REST)
    block = half // n_line
    sub = group // n_line
    core = lax.axis_index("core")
    n_yl = lax.axis_size("yl")
    columns = lax.axis_index(ALL) * shard + jnp.arange(shard, dtype=jnp.int32)

    def swap(value):
        return lax.ppermute(value, "core", [(0, 1), (1, 0)])

    row = positive.reshape(1, total_q)
    product = total_q * shard * width
    (copies,) = call(
        copies_kernel,
        [shaped((n_yl, group, width), BF16)],
        [queries],
        group * width,
        [pltpu.SemaphoreType.DMA((n_yl,))],
        in_specs=[pl.BlockSpec(memory_space=pl.ANY)],
    )
    copies, table = lax.optimization_barrier((copies, passages))
    mine = lax.all_to_all(copies, "yl", 0, 0, tiled=True)
    partner = swap(table)
    sent, notes, rounds = call(
        first_kernel,
        [
            shaped((n_line, block + TAIL, width), BF16),
            shaped((8, half), F32),
            shaped((1, 1), jnp.int32),
        ],
        [mine, passages, partner, row],
        4 * product,
    )

    def later_turn(turn, held):
        late, turn = lax.optimization_barrier((positive, turn))
        aims = late.reshape(n_yl, 2, n_line, sub).transpose(1, 2, 0, 3).reshape(2, n_line, block)
        aims = jnp.where(core == 0, aims, aims[::-1])
        chip = chip_of(aims // shard, n_index)
        same = chip[..., :, None] == chip[..., None, :]
        before = jnp.arange(block)[:, None] > jnp.arange(block)[None, :]
        rank = jnp.sum((same & before).astype(jnp.int32), axis=-1)
        slots = turn * SLOTS + jnp.arange(SLOTS, dtype=jnp.int32)
        fits = (chip[0] == index(("yl",) + INDEX))[..., None] & (rank[0][..., None] == slots)
        wanted = jnp.max(jnp.where(fits, aims[0][..., None], -1), axis=1).reshape(-1, 1)
        rows = 0.0
        for side, table in ((core, passages), (1 - core, partner)):
            owner = (lax.axis_index("yl") * 2 + side) * n_index + lax.axis_index(INDEX)
            match = (wanted == owner * shard + jnp.arange(shard, dtype=jnp.int32)).astype(BF16)
            rows = rows + jnp.dot(match, table, preferred_element_type=F32)
        rows = rows.astype(BF16).reshape(n_line, SLOTS, width)
        rows = lax.all_to_all(rows, LINE, 0, 0, tiled=True)
        place = lax.axis_index("x")
        my_chip = lax.dynamic_index_in_dim(chip[0], place, 0, keepdims=False)
        my_rank = lax.dynamic_index_in_dim(rank[0], place, 0, keepdims=False)
        peer = jnp.arange(n_line, dtype=jnp.int32) * (n_index // n_line)
        peer_chip = lax.axis_index("yl") * n_index + peer + lax.axis_index(("z", "yh"))
        fits = (my_chip[:, None] == peer_chip[None, :])[..., None]
        fits = (fits & (my_rank[:, None, None] == slots)).astype(BF16)
        fits = fits.reshape(block, n_line * SLOTS)
        return held + jnp.dot(fits, rows.reshape(-1, width), preferred_element_type=F32)

    extra = lax.fori_loop(1, rounds[0, 0], later_turn, jnp.zeros((block, width), F32))
    got = lax.all_to_all(sent, LINE, 0, 0, tiled=True)
    theirs = swap(mine)
    (sent,) = call(
        line_kernel,
        [shaped((n_rest, 32, LANES), BF16)],
        [got, notes, extra],
        half * width * 8,
        [pltpu.VMEM((half, LANES), F32)],
    )
    got = lax.all_to_all(sent, REST, 0, 0, tiled=True)
    spread = n_index
    sent, level = call(
        make_last_kernel(total_q, scale),
        [shaped((spread, 8, LANES), BF16), shaped((8, LANES), F32)],
        [got],
        half * width * 8,
    )
    tiles = lax.all_to_all(sent, INDEX, 0, 0, tiled=True)
    passage_grad, loss = call(
        passage_kernel,
        [shaped((shard, width), BF16), shaped((1, 1), F32)],
        [passages, level, swap(level), mine, theirs, row],
        4 * product,
    )
    (query_grad,) = call(
        make_assembly(sub // 8, width // LANES),
        [shaped((group, width), BF16)],
        [tiles],
        group * width,
    )
    return (loss[0, 0], query_grad, passage_grad)


def build(mesh):
    return jax.shard_map(
        on_device,
        mesh=mesh,
        in_specs=(P(QUERY, None), P(ALL, None), P()),
        out_specs=(P(), P(QUERY, None), P(ALL, None)),
        check_vma=False,
    )


def solution(mesh):
    devices = np.asarray(mesh.devices).reshape(4, 2, 4, 8, 2)
    return build(Mesh(devices, ("yl", "core", "x", "z", "yh")))
```

```python
import math

import jax
import jax.numpy as jnp
import numpy as np
from jax import lax
from jax.experimental import pallas as pl
from jax.experimental.pallas import tpu as pltpu
from jax.sharding import Mesh
from jax.sharding import PartitionSpec as P

QUERY = ("yl", "core")
INDEX = ("x", "z", "yh")
ALL = QUERY + INDEX
PLANE = ("x", "z")
RING = ("yl", "yh")
SPREAD = ("yh", "x", "z")
LOW = -1e30
SLOTS = 5
LANES = 128
F32 = jnp.float32
BF16 = jnp.bfloat16


def size(axes):
    return math.prod(lax.axis_size(a) for a in axes)


def index(axes):
    place = 0
    for a in axes:
        place = place * lax.axis_size(a) + lax.axis_index(a)
    return place


def call(body, outs, ins, flops, scratch=(), **specs):
    moved = sum(math.prod(o.shape) * o.dtype.itemsize for o in list(outs) + list(ins))
    return pl.pallas_call(
        body,
        out_shape=tuple(outs),
        scratch_shapes=list(scratch),
        **specs,
        cost_estimate=pl.CostEstimate(flops=flops, bytes_accessed=moved, transcendentals=0),
        compiler_params=pltpu.CompilerParams(vmem_limit_bytes=40 << 20),
    )(*ins)


def shaped(shape, dtype):
    return jax.ShapeDtypeStruct(shape, dtype)


def iota(shape, dim):
    return lax.broadcasted_iota(jnp.int32, shape, dim)


def split3(value):
    a = value.astype(BF16).astype(F32)
    b = (value - a).astype(BF16).astype(F32)
    c = (value - a - b).astype(BF16).astype(F32)
    return a, b, c


def parted_sum(values):
    coarse = jnp.round(values * (1 / 16)) * 16.0
    middle = jnp.round((values - coarse) * 64.0) * (1 / 64)
    parts = (coarse, middle, values - coarse - middle)
    return [jnp.sum(p, axis=(0, 1), keepdims=True) for p in parts]


def sums_out(sums, lane, first):
    spread = jnp.zeros(lane.shape, F32)
    for i in range(3):
        spread = jnp.where((lane - first) % 3 == i, sums[i], spread)
    a, b, c = split3(spread)
    terms = jnp.where(lane < first + 3, a, jnp.where(lane < first + 6, b, c))
    return jnp.where((lane >= first) & (lane < first + 9), terms, 0.0)


def sums_in(terms, lane, first):
    inside = (lane >= first) & (lane < first + 9)
    return [
        jnp.sum(jnp.where(inside & ((lane - first) % 3 == i), terms, 0.0), axis=(0, 1), keepdims=True)
        for i in range(3)
    ]


def notes_out(level, rest, sums, width):
    count = 2 * level.shape[1]
    value = jnp.concatenate([level, rest, jnp.zeros((1, width - count), F32)], axis=1)
    lane = iota((1, width), 1)
    a, b, c = split3(value)
    c = jnp.where(lane < count, c, sums_out(sums, lane, count))
    sub = iota((8, width), 0)
    return jnp.where(sub == 5, a, jnp.where(sub == 6, b, jnp.where(sub == 7, c, 0.0)))


def notes_in(tile, half):
    a, b, c = tile[5:6], tile[6:7], tile[7:8]
    value = a + b + c
    return value[:, :half], value[:, half : 2 * half], c


def log_sum(values):
    high = jnp.max(values, axis=0, keepdims=True)
    return high + jnp.log(jnp.sum(jnp.exp(values - high), axis=0, keepdims=True))


def columns_of(rows):
    fill = jnp.zeros((LANES - rows.shape[0], rows.shape[1]), F32)
    return jnp.concatenate([rows, fill], axis=0).T


def own_first(positive, group, swapped):
    count = positive.shape[1] // (2 * group)
    even = [positive[:, 2 * i * group : (2 * i + 1) * group] for i in range(count)]
    odd = [positive[:, (2 * i + 1) * group : (2 * i + 2) * group] for i in range(count)]
    even, odd = jnp.concatenate(even, axis=1), jnp.concatenate(odd, axis=1)
    return jnp.concatenate(
        [jnp.where(swapped, odd, even), jnp.where(swapped, even, odd)], axis=1
    )


def chip_of(owner, n_index):
    return lax.div(lax.div(owner, n_index), 2) * n_index + lax.rem(owner, n_index)


def slot_plan(aims, block, shard):
    total_q = aims.shape[1]
    half = total_q // 2
    n_index = size(INDEX)
    n_yh = lax.axis_size("yh")
    owner = lax.div(aims, shard)
    chip = chip_of(owner, n_index)
    query = iota((1, total_q), 1)
    part = lax.div(query, block)
    key = (part * (size(ALL) // 2) + chip).astype(F32)
    down = columns_of(key)[:, 0:1]
    earlier = (down == key) & (iota((total_q, 1), 0) < query)
    rank = jnp.sum(earlier.astype(F32), axis=0, keepdims=True)
    rounds = lax.div(jnp.max(rank, axis=1, keepdims=True).astype(jnp.int32), SLOTS) + 1
    rank = rank.astype(jnp.int32)
    fits = rank < SLOTS
    slot = jnp.where((chip == index(("yl",) + INDEX)) & fits, part * 8 + rank, -1)
    count = half // block * 8
    match = slot[:, :half] == iota((count, 1), 0)
    found = jnp.sum(jnp.where(match, (aims[:, :half] + 1).astype(F32), 0.0), axis=1, keepdims=True)
    along = lax.rem(chip, n_index)
    peer = lax.div(chip, n_index) * n_yh + lax.rem(along, n_yh)
    near = (lax.div(along, n_yh) == index(PLANE)) & fits
    code = jnp.where(near, peer * (block + 8) + block + rank, -1)[:, :half]
    return found.astype(jnp.int32) - 1, code.astype(F32), rounds


def first_kernel(every, passages, partner, positive, sent, notes, rounds):
    shard, width = passages.shape
    group = every.shape[2]
    half = every.shape[0] * group
    blocks = sent.shape[0]
    rows = half // blocks
    core = lax.axis_index("core")
    scale = 1.0 / math.sqrt(width)
    bases = [
        (index(("yl",)) * 2 + c) * (size(INDEX) * shard) + index(INDEX) * shard
        for c in (core, 1 - core)
    ]
    tables = [passages, partner]
    block = every[:, core].reshape(half, width)
    scores = [
        scale
        * lax.dot_general(t[...], block, (((1,), (1,)), ((), ())), preferred_element_type=F32)
        for t in tables
    ]
    aims = own_first(positive[...] - 1, group, core == 1)
    wanted, code, rounds[...] = slot_plan(aims, rows, shard)
    notes[...] = jnp.broadcast_to(code, notes.shape)
    others, top, only = [], None, None
    for base, score in zip(bases, scores):
        hit = aims[:, :half] == base + iota((shard, 1), 0)
        others.append(jnp.where(hit, LOW, score))
        high = jnp.max(others[-1], axis=0, keepdims=True)
        one = jnp.max(jnp.where(hit, score, LOW), axis=0, keepdims=True)
        top = high if top is None else jnp.maximum(top, high)
        only = one if only is None else jnp.maximum(only, one)
    picked = jnp.where(only > LOW, only, 0.0)
    terms = [jnp.exp(o - top) for o in others]
    total = sum(jnp.sum(t, axis=0, keepdims=True) for t in terms)
    high = jnp.maximum(top, only)
    level = high + jnp.log(total * jnp.exp(top - high) + jnp.exp(only - high))
    share = jnp.exp(top - level)
    pulled, slots = 0.0, 0.0
    for base, table, term in zip(bases, tables, terms):
        pulled = pulled + lax.dot_general(
            (term * share).astype(BF16),
            table[...],
            (((0,), (0,)), ((), ())),
            preferred_element_type=F32,
        )
        match = (wanted == base + iota((1, shard), 1)).astype(BF16)
        slots = slots + jnp.dot(match, table[...], preferred_element_type=F32)
    tile = notes_out(level, total * share, parted_sum(picked), width)
    for b in range(blocks):
        piece = [pulled[b * rows : (b + 1) * rows], slots[b * 8 : (b + 1) * 8] + tile]
        sent[b] = jnp.concatenate(piece, axis=0).astype(BF16)


def ring_kernel(got, notes, extra, sent, turned):
    peers, height, width = got.shape
    rows = height - 8
    planes = sent.shape[0]
    half = rows * peers
    parts = [got[s].astype(F32) for s in range(peers)]
    read = [notes_in(p[rows:], half) for p in parts]
    levels = jnp.concatenate([r[0] for r in read], axis=0)
    rests = jnp.concatenate([r[1] for r in read], axis=0)
    last = jnp.concatenate([r[2] for r in read], axis=0)
    sums = sums_in(last, iota(last.shape, 1), 2 * half)
    level = log_sum(levels)
    keep = jnp.exp(levels - level)
    rest = jnp.sum(rests * keep, axis=0, keepdims=True)
    turned[...] = columns_of(jnp.concatenate([keep, rest, level, notes[0:1]], axis=0))
    cols = turned[pl.ds(pl.multiple_of(index(RING) * rows, 8), rows), :]
    pulled = parts[0][:rows] * cols[:, 0:1]
    for s in range(1, peers):
        pulled = pulled + parts[s][:rows] * cols[:, s : s + 1]
    whole = jnp.concatenate(parts, axis=0).astype(BF16)
    code = cols[:, peers + 2 : peers + 3].astype(jnp.int32)
    fits = (code == iota((rows, peers * height), 1)).astype(BF16)
    chosen = jnp.dot(fits, whole, preferred_element_type=F32) + extra[...]
    lane = iota((rows, LANES), 1)
    beside = sums_out(sums, lane, 16)
    for i, term in enumerate(split3(cols[:, peers + 1 : peers + 2]) + split3(cols[:, peers : peers + 1])):
        beside = jnp.where(lane == i, term, beside)
    chunks = half // LANES
    sub = iota((8, LANES), 0)
    wide = jnp.zeros((8, LANES), F32)
    for t, term in enumerate(split3(level)):
        for j in range(chunks):
            wide = jnp.where(sub == t * chunks + j, term[:, j * LANES : (j + 1) * LANES], wide)
    across = width // LANES
    for d in range(planes):
        r, c = d // across, d % across
        if r * 8 < rows:
            here, span = slice(r * 8, r * 8 + 8), slice(c * LANES, (c + 1) * LANES)
            tile = [pulled[here, span], chosen[here, span], beside[here]]
        else:
            tile = [jnp.zeros((16, LANES), F32), beside[:8]]
        sent[d] = jnp.concatenate(tile + [wide], axis=0).astype(BF16)


def make_plane_kernel(total_q, scale):
    chunks = total_q // 2 // LANES

    def plane_kernel(got, sent, level):
        peers = got.shape[0]
        lane = iota((8, LANES), 1)
        tops, rests, wides = [], [], []
        chosen = jnp.zeros((8, LANES), F32)
        beside = jnp.zeros((8, LANES), F32)
        for s in range(peers):
            part = got[s].astype(F32)
            note = part[16:24]
            tops.append(jnp.sum(jnp.where(lane < 3, note, 0.0), axis=1, keepdims=True))
            rests.append(
                jnp.sum(jnp.where((lane >= 3) & (lane < 6), note, 0.0), axis=1, keepdims=True)
            )
            wide = part[24:]
            wides.append(wide[:chunks] + wide[chunks : 2 * chunks] + wide[2 * chunks : 3 * chunks])
            chosen = chosen + part[8:16]
            beside = beside + note
        high, top = wides[0], tops[0]
        for s in range(1, peers):
            high, top = jnp.maximum(high, wides[s]), jnp.maximum(top, tops[s])
        total = jnp.zeros((chunks, LANES), F32)
        full = jnp.zeros((8, 1), F32)
        rest = jnp.zeros((8, 1), F32)
        pulled = jnp.zeros((8, LANES), F32)
        for s in range(peers):
            total = total + jnp.exp(wides[s] - high)
            keep = jnp.exp(tops[s] - top)
            full = full + keep
            rest = rest + keep * rests[s]
            pulled = pulled + keep * got[s].astype(F32)[:8]
        lse = high + jnp.log(total)
        tile = ((pulled - rest * chosen) / full * (scale / total_q)).astype(BF16)
        for d in range(sent.shape[0]):
            sent[d] = tile
        picked = sums_in(beside[0:1], lane[0:1], 16)
        terms = [a - b for a, b in zip(parted_sum(lse), picked)]
        for i in range(3):
            level[chunks + i : chunks + i + 1, :] = jnp.broadcast_to(terms[i], (1, LANES))
        level[:chunks, :] = lse

    return plane_kernel


def passage_kernel(passages, level, level2, every, positive, out, loss):
    shard, width = out.shape
    group = every.shape[2]
    half = every.shape[0] * group
    total_q = 2 * half
    chunks = half // LANES
    core = lax.axis_index("core")
    down = index(ALL) * shard + iota((shard, 1), 0)
    scale = 1.0 / math.sqrt(width)
    aims = own_first(positive[...] - 1, group, core == 1)
    total = None
    for side, logs in enumerate([level, level2]):
        block = every[:, lax.rem(core + side, 2)].reshape(half, width)
        score = scale * lax.dot_general(
            passages[...], block, (((1,), (1,)), ((), ())), preferred_element_type=F32
        )
        lse = jnp.concatenate([logs[j : j + 1, :] for j in range(chunks)], axis=1)
        hit = aims[:, side * half : (side + 1) * half] == down
        weight = (jnp.exp(score - lse) - hit.astype(F32)) * (1.0 / total_q)
        term = jnp.dot(weight.astype(BF16), block, preferred_element_type=F32)
        total = term if total is None else total + term
    out[...] = (total * scale).astype(BF16)
    parts = level[chunks : chunks + 3, 0:1] + level2[chunks : chunks + 3, 0:1]
    loss[...] = (parts[0:1] + parts[1:2] + parts[2:3]) * (1.0 / total_q)


def make_assembly(down, across):
    def assembly(tiles, out):
        per = tiles.shape[0] // (out.shape[0] // (8 * down))
        for y in range(out.shape[0] // (8 * down)):
            for r in range(0, down, 2):
                for c in range(across):
                    pair = [tiles[y * per + (r + i) * across + c].astype(F32) for i in range(2)]
                    row = (y * down + r) * 8
                    out[row : row + 16, c * LANES : (c + 1) * LANES] = jnp.concatenate(
                        pair, axis=0
                    ).astype(BF16)

    return assembly


def on_device(queries, passages, positive):
    group, width = queries.shape
    scale = 1.0 / math.sqrt(width)
    total_q = positive.shape[0]
    half = total_q // 2
    shard = passages.shape[0]
    n_index = size(INDEX)
    n_ring = size(RING)
    n_plane = size(PLANE)
    block = half // n_ring
    core = lax.axis_index("core")
    n_yl, n_yh = lax.axis_size("yl"), lax.axis_size("yh")
    columns = lax.axis_index(ALL) * shard + jnp.arange(shard, dtype=jnp.int32)

    def swap(value):
        return lax.ppermute(value, "core", [(0, 1), (1, 0)])

    row = positive.reshape(1, total_q) + 1
    product = total_q * shard * width
    partner = swap(passages)
    queries, row = lax.optimization_barrier((queries, row))
    every = lax.all_gather(queries, QUERY, axis=0, tiled=True).reshape(n_yl, 2, group, width)
    sent, notes, rounds = call(
        first_kernel,
        [
            shaped((n_ring, block + 8, width), BF16),
            shaped((8, half), F32),
            shaped((1, 1), jnp.int32),
        ],
        [every, passages, partner, row],
        4 * product,
    )

    def later_turn(turn, held):
        late, turn = lax.optimization_barrier((row, turn))
        aims = (late - 1).reshape(n_yl, 2, group).transpose(1, 0, 2).reshape(2, n_ring, block)
        aims = jnp.where(core == 0, aims, aims[::-1])
        chip = chip_of(aims // shard, n_index)
        same = chip[..., :, None] == chip[..., None, :]
        before = jnp.arange(block)[:, None] > jnp.arange(block)[None, :]
        rank = jnp.sum((same & before).astype(jnp.int32), axis=-1)
        slots = turn * SLOTS + jnp.arange(SLOTS, dtype=jnp.int32)
        fits = (chip[0] == index(("yl",) + INDEX))[..., None] & (rank[0][..., None] == slots)
        wanted = jnp.max(jnp.where(fits, aims[0][..., None], -1), axis=1).reshape(-1, 1)
        rows = 0.0
        for side, table in ((core, passages), (1 - core, partner)):
            owner = (lax.axis_index("yl") * 2 + side) * n_index + lax.axis_index(INDEX)
            match = (wanted == owner * shard + jnp.arange(shard, dtype=jnp.int32)).astype(BF16)
            rows = rows + jnp.dot(match, table, preferred_element_type=F32)
        rows = rows.astype(BF16).reshape(n_ring, SLOTS, width)
        rows = lax.all_to_all(rows, RING, 0, 0, tiled=True)
        place = lax.axis_index(RING)
        my_chip = lax.dynamic_index_in_dim(chip[0], place, 0, keepdims=False)
        my_rank = lax.dynamic_index_in_dim(rank[0], place, 0, keepdims=False)
        peer = jnp.arange(n_ring, dtype=jnp.int32)
        peer_chip = (peer // n_yh) * n_index + lax.axis_index(PLANE) * n_yh + peer % n_yh
        fits = (my_chip[:, None] == peer_chip[None, :])[..., None]
        fits = (fits & (my_rank[:, None, None] == slots)).astype(BF16)
        fits = fits.reshape(block, n_ring * SLOTS)
        return held + jnp.dot(fits, rows.reshape(-1, width), preferred_element_type=F32)

    extra = lax.fori_loop(1, rounds[0, 0], later_turn, jnp.zeros((block, width), F32))
    got = lax.all_to_all(sent, RING, 0, 0, tiled=True)
    (sent,) = call(
        ring_kernel,
        [shaped((n_plane, 32, LANES), BF16)],
        [got, notes, extra],
        half * width * 8,
        [pltpu.VMEM((half, LANES), F32)],
    )
    got = lax.all_to_all(sent, PLANE, 0, 0, tiled=True)
    spread = n_plane * n_yh
    sent, level = call(
        make_plane_kernel(total_q, scale),
        [shaped((spread, 8, LANES), BF16), shaped((8, LANES), F32)],
        [got],
        half * width * 8,
    )
    tiles = lax.all_to_all(sent, SPREAD, 0, 0, tiled=True)
    passage_grad, loss = call(
        passage_kernel,
        [shaped((shard, width), BF16), shaped((1, 1), F32)],
        [passages, level, swap(level), every, row],
        4 * product,
    )
    (query_grad,) = call(
        make_assembly(block // 8, width // LANES),
        [shaped((group, width), BF16)],
        [tiles],
        group * width,
    )
    return (loss[0, 0], query_grad, passage_grad)


def build(mesh):
    return jax.shard_map(
        on_device,
        mesh=mesh,
        in_specs=(P(QUERY, None), P(ALL, None), P()),
        out_specs=(P(), P(QUERY, None), P(ALL, None)),
        check_vma=False,
    )


def solution(mesh):
    devices = np.asarray(mesh.devices).reshape(4, 2, 4, 8, 2)
    return build(Mesh(devices, ("yl", "core", "x", "z", "yh")))
```

```python
import math

import jax
import jax.numpy as jnp
import numpy as np
from jax import lax
from jax.experimental import pallas as pl
from jax.experimental.pallas import tpu as pltpu
from jax.sharding import Mesh
from jax.sharding import PartitionSpec as P

QUERY = ("yl", "core")
INDEX = ("x", "z", "yh")
ALL = QUERY + INDEX
PLANE = ("x", "z")
RING = ("yl", "yh")
SPREAD = ("yh", "x", "z")
LOW = -1e30
SLOTS = 5
LANES = 128
F32 = jnp.float32
BF16 = jnp.bfloat16


def size(axes):
    return math.prod(lax.axis_size(a) for a in axes)


def index(axes):
    place = 0
    for a in axes:
        place = place * lax.axis_size(a) + lax.axis_index(a)
    return place


def call(body, outs, ins, flops, scratch=(), **specs):
    moved = sum(math.prod(o.shape) * o.dtype.itemsize for o in list(outs) + list(ins))
    return pl.pallas_call(
        body,
        out_shape=tuple(outs),
        scratch_shapes=list(scratch),
        **specs,
        cost_estimate=pl.CostEstimate(flops=flops, bytes_accessed=moved, transcendentals=0),
        compiler_params=pltpu.CompilerParams(vmem_limit_bytes=40 << 20),
    )(*ins)


def shaped(shape, dtype):
    return jax.ShapeDtypeStruct(shape, dtype)


def iota(shape, dim):
    return lax.broadcasted_iota(jnp.int32, shape, dim)


def split3(value):
    a = value.astype(BF16).astype(F32)
    b = (value - a).astype(BF16).astype(F32)
    c = (value - a - b).astype(BF16).astype(F32)
    return a, b, c


def parted_sum(values):
    coarse = jnp.round(values * (1 / 16)) * 16.0
    middle = jnp.round((values - coarse) * 64.0) * (1 / 64)
    parts = (coarse, middle, values - coarse - middle)
    return [jnp.sum(p, axis=(0, 1), keepdims=True) for p in parts]


def sums_out(sums, lane, first):
    spread = jnp.zeros(lane.shape, F32)
    for i in range(3):
        spread = jnp.where((lane - first) % 3 == i, sums[i], spread)
    a, b, c = split3(spread)
    terms = jnp.where(lane < first + 3, a, jnp.where(lane < first + 6, b, c))
    return jnp.where((lane >= first) & (lane < first + 9), terms, 0.0)


def sums_in(terms, lane, first):
    inside = (lane >= first) & (lane < first + 9)
    return [
        jnp.sum(jnp.where(inside & ((lane - first) % 3 == i), terms, 0.0), axis=(0, 1), keepdims=True)
        for i in range(3)
    ]


def notes_out(level, rest, sums, width):
    count = 2 * level.shape[1]
    value = jnp.concatenate([level, rest, jnp.zeros((1, width - count), F32)], axis=1)
    lane = iota((1, width), 1)
    a, b, c = split3(value)
    c = jnp.where(lane < count, c, sums_out(sums, lane, count))
    sub = iota((8, width), 0)
    return jnp.where(sub == 5, a, jnp.where(sub == 6, b, jnp.where(sub == 7, c, 0.0)))


def notes_in(tile, half):
    a, b, c = tile[5:6], tile[6:7], tile[7:8]
    value = a + b + c
    return value[:, :half], value[:, half : 2 * half], c


def log_sum(values):
    high = jnp.max(values, axis=0, keepdims=True)
    return high + jnp.log(jnp.sum(jnp.exp(values - high), axis=0, keepdims=True))


def columns_of(rows):
    fill = jnp.zeros((LANES - rows.shape[0], rows.shape[1]), F32)
    return jnp.concatenate([rows, fill], axis=0).T


def own_first(positive, group, swapped):
    count = positive.shape[1] // (2 * group)
    even = [positive[:, 2 * i * group : (2 * i + 1) * group] for i in range(count)]
    odd = [positive[:, (2 * i + 1) * group : (2 * i + 2) * group] for i in range(count)]
    even, odd = jnp.concatenate(even, axis=1), jnp.concatenate(odd, axis=1)
    return jnp.concatenate(
        [jnp.where(swapped, odd, even), jnp.where(swapped, even, odd)], axis=1
    )


def chip_of(owner, n_index):
    return lax.div(lax.div(owner, n_index), 2) * n_index + lax.rem(owner, n_index)


def slot_plan(aims, block, shard):
    total_q = aims.shape[1]
    half = total_q // 2
    n_index = size(INDEX)
    n_yh = lax.axis_size("yh")
    owner = lax.div(aims, shard)
    chip = chip_of(owner, n_index)
    query = iota((1, total_q), 1)
    part = lax.div(query, block)
    key = (part * (size(ALL) // 2) + chip).astype(F32)
    down = columns_of(key)[:, 0:1]
    earlier = (down == key) & (iota((total_q, 1), 0) < query)
    rank = jnp.sum(earlier.astype(F32), axis=0, keepdims=True)
    rounds = lax.div(jnp.max(rank, axis=1, keepdims=True).astype(jnp.int32), SLOTS) + 1
    rank = rank.astype(jnp.int32)
    fits = rank < SLOTS
    slot = jnp.where((chip == index(("yl",) + INDEX)) & fits, part * 8 + rank, -1)
    count = half // block * 8
    match = slot[:, :half] == iota((count, 1), 0)
    found = jnp.sum(jnp.where(match, (aims[:, :half] + 1).astype(F32), 0.0), axis=1, keepdims=True)
    along = lax.rem(chip, n_index)
    peer = lax.div(chip, n_index) * n_yh + lax.rem(along, n_yh)
    near = (lax.div(along, n_yh) == index(PLANE)) & fits
    code = jnp.where(near, peer * (block + 8) + block + rank, -1)[:, :half]
    return found.astype(jnp.int32) - 1, code.astype(F32), rounds


def first_kernel(every, passages, partner, positive, sent, notes, rounds):
    shard, width = passages.shape
    group = every.shape[2]
    half = every.shape[0] * group
    blocks = sent.shape[0]
    rows = half // blocks
    core = lax.axis_index("core")
    scale = 1.0 / math.sqrt(width)
    bases = [
        (index(("yl",)) * 2 + c) * (size(INDEX) * shard) + index(INDEX) * shard
        for c in (core, 1 - core)
    ]
    tables = [passages, partner]
    block = every[:, core].reshape(half, width)
    scores = [
        scale
        * lax.dot_general(t[...], block, (((1,), (1,)), ((), ())), preferred_element_type=F32)
        for t in tables
    ]
    aims = own_first(positive[...] - 1, group, core == 1)
    wanted, code, rounds[...] = slot_plan(aims, rows, shard)
    notes[...] = jnp.broadcast_to(code, notes.shape)
    others, top, only = [], None, None
    for base, score in zip(bases, scores):
        hit = aims[:, :half] == base + iota((shard, 1), 0)
        others.append(jnp.where(hit, LOW, score))
        high = jnp.max(others[-1], axis=0, keepdims=True)
        one = jnp.max(jnp.where(hit, score, LOW), axis=0, keepdims=True)
        top = high if top is None else jnp.maximum(top, high)
        only = one if only is None else jnp.maximum(only, one)
    picked = jnp.where(only > LOW, only, 0.0)
    terms = [jnp.exp(o - top) for o in others]
    total = sum(jnp.sum(t, axis=0, keepdims=True) for t in terms)
    high = jnp.maximum(top, only)
    level = high + jnp.log(total * jnp.exp(top - high) + jnp.exp(only - high))
    share = jnp.exp(top - level)
    pulled, slots = 0.0, 0.0
    for base, table, term in zip(bases, tables, terms):
        pulled = pulled + lax.dot_general(
            (term * share).astype(BF16),
            table[...],
            (((0,), (0,)), ((), ())),
            preferred_element_type=F32,
        )
        match = (wanted == base + iota((1, shard), 1)).astype(BF16)
        slots = slots + jnp.dot(match, table[...], preferred_element_type=F32)
    tile = notes_out(level, total * share, parted_sum(picked), width)
    for b in range(blocks):
        piece = [pulled[b * rows : (b + 1) * rows], slots[b * 8 : (b + 1) * 8] + tile]
        sent[b] = jnp.concatenate(piece, axis=0).astype(BF16)


def ring_kernel(got, notes, extra, sent, turned):
    peers, height, width = got.shape
    rows = height - 8
    planes = sent.shape[0]
    half = rows * peers
    parts = [got[s].astype(F32) for s in range(peers)]
    read = [notes_in(p[rows:], half) for p in parts]
    levels = jnp.concatenate([r[0] for r in read], axis=0)
    rests = jnp.concatenate([r[1] for r in read], axis=0)
    last = jnp.concatenate([r[2] for r in read], axis=0)
    sums = sums_in(last, iota(last.shape, 1), 2 * half)
    level = log_sum(levels)
    keep = jnp.exp(levels - level)
    rest = jnp.sum(rests * keep, axis=0, keepdims=True)
    turned[...] = columns_of(jnp.concatenate([keep, rest, level, notes[0:1]], axis=0))
    cols = turned[pl.ds(pl.multiple_of(index(RING) * rows, 8), rows), :]
    pulled = parts[0][:rows] * cols[:, 0:1]
    for s in range(1, peers):
        pulled = pulled + parts[s][:rows] * cols[:, s : s + 1]
    whole = jnp.concatenate(parts, axis=0).astype(BF16)
    code = cols[:, peers + 2 : peers + 3].astype(jnp.int32)
    fits = (code == iota((rows, peers * height), 1)).astype(BF16)
    chosen = jnp.dot(fits, whole, preferred_element_type=F32) + extra[...]
    mine = columns_of(cols)[:LANES]
    a, b, c = split3(mine)
    terms = a + pltpu.roll(b, 32, 1) + pltpu.roll(c, 64, 1)
    lane = iota((1, LANES), 1)
    beside = terms[peers : peers + 1] + sums_out(sums, lane, 96)
    chunks = half // LANES
    sub = iota((8, LANES), 0)
    wide = jnp.zeros((8, LANES), F32)
    for t, term in enumerate(split3(level)):
        for j in range(chunks):
            wide = jnp.where(sub == t * chunks + j, term[:, j * LANES : (j + 1) * LANES], wide)
    wide = jnp.where(sub == 6, terms[peers + 1 : peers + 2], jnp.where(sub == 7, beside, wide))
    across = width // LANES
    for d in range(planes):
        r, c = d // across, d % across
        if r * 8 < rows:
            here, span = slice(r * 8, r * 8 + 8), slice(c * LANES, (c + 1) * LANES)
            tile = [pulled[here, span], chosen[here, span]]
        else:
            tile = [jnp.zeros((16, LANES), F32)]
        sent[d] = jnp.concatenate(tile + [wide], axis=0).astype(BF16)


def make_plane_kernel(total_q, scale, rows, across):
    chunks = total_q // 2 // LANES

    def plane_kernel(got, sent, level, turned):
        peers = got.shape[0]
        lane = iota((1, LANES), 1)
        parts = [got[s].astype(F32) for s in range(peers)]
        for i in range(2):
            terms = jnp.concatenate([p[22 + i : 23 + i] for p in parts], axis=0)
            value = terms + pltpu.roll(terms, LANES - 32, 1) + pltpu.roll(terms, LANES - 64, 1)
            turned[i] = columns_of(value)
        picked = sums_in(terms, iota(terms.shape, 1), 96)
        first = jnp.minimum(lax.div(index(PLANE), across) * 8, rows - 8)
        here = pl.ds(pl.multiple_of(first, 8), 8)
        tops = jnp.where(lane < peers, turned[0, here, :], LOW)
        keep = jnp.exp(tops - jnp.max(tops, axis=1, keepdims=True))
        keep = keep / jnp.sum(keep, axis=1, keepdims=True)
        rest = jnp.sum(keep * turned[1, here, :], axis=1, keepdims=True)
        wides = [
            p[16 : 16 + chunks] + p[16 + chunks : 16 + 2 * chunks] + p[16 + 2 * chunks : 16 + 3 * chunks]
            for p in parts
        ]
        high = wides[0]
        for s in range(1, peers):
            high = jnp.maximum(high, wides[s])
        total = jnp.zeros((chunks, LANES), F32)
        pulled, chosen = jnp.zeros((8, LANES), F32), jnp.zeros((8, LANES), F32)
        for s in range(peers):
            total = total + jnp.exp(wides[s] - high)
            pulled = pulled + keep[:, s : s + 1] * parts[s][:8]
            chosen = chosen + parts[s][8:16]
        lse = high + jnp.log(total)
        tile = ((pulled - rest * chosen) * (scale / total_q)).astype(BF16)
        for d in range(sent.shape[0]):
            sent[d] = tile
        terms = [a - b for a, b in zip(parted_sum(lse), picked)]
        for i in range(3):
            level[chunks + i : chunks + i + 1, :] = jnp.broadcast_to(terms[i], (1, LANES))
        level[:chunks, :] = lse

    return plane_kernel


def passage_kernel(passages, level, level2, every, positive, out, loss):
    shard, width = out.shape
    group = every.shape[2]
    half = every.shape[0] * group
    total_q = 2 * half
    chunks = half // LANES
    core = lax.axis_index("core")
    down = index(ALL) * shard + iota((shard, 1), 0)
    scale = 1.0 / math.sqrt(width)
    aims = own_first(positive[...] - 1, group, core == 1)
    total = None
    for side, logs in enumerate([level, level2]):
        block = every[:, lax.rem(core + side, 2)].reshape(half, width)
        score = scale * lax.dot_general(
            passages[...], block, (((1,), (1,)), ((), ())), preferred_element_type=F32
        )
        lse = jnp.concatenate([logs[j : j + 1, :] for j in range(chunks)], axis=1)
        hit = aims[:, side * half : (side + 1) * half] == down
        weight = (jnp.exp(score - lse) - hit.astype(F32)) * (1.0 / total_q)
        term = jnp.dot(weight.astype(BF16), block, preferred_element_type=F32)
        total = term if total is None else total + term
    out[...] = (total * scale).astype(BF16)
    parts = level[chunks : chunks + 3, 0:1] + level2[chunks : chunks + 3, 0:1]
    loss[...] = (parts[0:1] + parts[1:2] + parts[2:3]) * (1.0 / total_q)


def make_assembly(down, across):
    def assembly(tiles, out):
        per = tiles.shape[0] // (out.shape[0] // (8 * down))
        for y in range(out.shape[0] // (8 * down)):
            for r in range(0, down, 2):
                for c in range(across):
                    pair = [tiles[y * per + (r + i) * across + c].astype(F32) for i in range(2)]
                    row = (y * down + r) * 8
                    out[row : row + 16, c * LANES : (c + 1) * LANES] = jnp.concatenate(
                        pair, axis=0
                    ).astype(BF16)

    return assembly


def on_device(queries, passages, positive):
    group, width = queries.shape
    scale = 1.0 / math.sqrt(width)
    total_q = positive.shape[0]
    half = total_q // 2
    shard = passages.shape[0]
    n_index = size(INDEX)
    n_ring = size(RING)
    n_plane = size(PLANE)
    block = half // n_ring
    core = lax.axis_index("core")
    n_yl, n_yh = lax.axis_size("yl"), lax.axis_size("yh")
    columns = lax.axis_index(ALL) * shard + jnp.arange(shard, dtype=jnp.int32)

    def swap(value):
        return lax.ppermute(value, "core", [(0, 1), (1, 0)])

    row = positive.reshape(1, total_q) + 1
    product = total_q * shard * width
    partner = swap(passages)
    queries, row = lax.optimization_barrier((queries, row))
    every = lax.all_gather(queries, QUERY, axis=0, tiled=True).reshape(n_yl, 2, group, width)
    sent, notes, rounds = call(
        first_kernel,
        [
            shaped((n_ring, block + 8, width), BF16),
            shaped((8, half), F32),
            shaped((1, 1), jnp.int32),
        ],
        [every, passages, partner, row],
        4 * product,
    )

    def later_turn(turn, held):
        late, turn = lax.optimization_barrier((row, turn))
        aims = (late - 1).reshape(n_yl, 2, group).transpose(1, 0, 2).reshape(2, n_ring, block)
        aims = jnp.where(core == 0, aims, aims[::-1])
        chip = chip_of(aims // shard, n_index)
        same = chip[..., :, None] == chip[..., None, :]
        before = jnp.arange(block)[:, None] > jnp.arange(block)[None, :]
        rank = jnp.sum((same & before).astype(jnp.int32), axis=-1)
        slots = turn * SLOTS + jnp.arange(SLOTS, dtype=jnp.int32)
        fits = (chip[0] == index(("yl",) + INDEX))[..., None] & (rank[0][..., None] == slots)
        wanted = jnp.max(jnp.where(fits, aims[0][..., None], -1), axis=1).reshape(-1, 1)
        rows = 0.0
        for side, table in ((core, passages), (1 - core, partner)):
            owner = (lax.axis_index("yl") * 2 + side) * n_index + lax.axis_index(INDEX)
            match = (wanted == owner * shard + jnp.arange(shard, dtype=jnp.int32)).astype(BF16)
            rows = rows + jnp.dot(match, table, preferred_element_type=F32)
        rows = rows.astype(BF16).reshape(n_ring, SLOTS, width)
        rows = lax.all_to_all(rows, RING, 0, 0, tiled=True)
        place = lax.axis_index(RING)
        my_chip = lax.dynamic_index_in_dim(chip[0], place, 0, keepdims=False)
        my_rank = lax.dynamic_index_in_dim(rank[0], place, 0, keepdims=False)
        peer = jnp.arange(n_ring, dtype=jnp.int32)
        peer_chip = (peer // n_yh) * n_index + lax.axis_index(PLANE) * n_yh + peer % n_yh
        fits = (my_chip[:, None] == peer_chip[None, :])[..., None]
        fits = (fits & (my_rank[:, None, None] == slots)).astype(BF16)
        fits = fits.reshape(block, n_ring * SLOTS)
        return held + jnp.dot(fits, rows.reshape(-1, width), preferred_element_type=F32)

    extra = lax.fori_loop(1, rounds[0, 0], later_turn, jnp.zeros((block, width), F32))
    got = lax.all_to_all(sent, RING, 0, 0, tiled=True)
    (sent,) = call(
        ring_kernel,
        [shaped((n_plane, 24, LANES), BF16)],
        [got, notes, extra],
        half * width * 8,
        [pltpu.VMEM((half, LANES), F32)],
    )
    got = lax.all_to_all(sent, PLANE, 0, 0, tiled=True)
    spread = n_plane * n_yh
    sent, level = call(
        make_plane_kernel(total_q, scale, block, width // LANES),
        [shaped((spread, 8, LANES), BF16), shaped((8, LANES), F32)],
        [got],
        half * width * 8,
        [pltpu.VMEM((2, LANES, LANES), F32)],
    )
    tiles = lax.all_to_all(sent, SPREAD, 0, 0, tiled=True)
    passage_grad, loss = call(
        passage_kernel,
        [shaped((shard, width), BF16), shaped((1, 1), F32)],
        [passages, level, swap(level), every, row],
        4 * product,
    )
    (query_grad,) = call(
        make_assembly(block // 8, width // LANES),
        [shaped((group, width), BF16)],
        [tiles],
        group * width,
    )
    return (loss[0, 0], query_grad, passage_grad)


def build(mesh):
    return jax.shard_map(
        on_device,
        mesh=mesh,
        in_specs=(P(QUERY, None), P(ALL, None), P()),
        out_specs=(P(), P(QUERY, None), P(ALL, None)),
        check_vma=False,
    )


def solution(mesh):
    devices = np.asarray(mesh.devices).reshape(4, 2, 4, 8, 2)
    return build(Mesh(devices, ("yl", "core", "x", "z", "yh")))
```

```python
import math

import jax
import jax.numpy as jnp
import numpy as np
from jax import lax
from jax.experimental import pallas as pl
from jax.experimental.pallas import tpu as pltpu
from jax.sharding import Mesh
from jax.sharding import PartitionSpec as P

QUERY = ("yl", "core")
INDEX = ("x", "z", "yh")
ALL = QUERY + INDEX
LINE = ("x",)
REST = ("yl", "z", "yh")
LOW = -1e30
TAIL = 16
SLOTS = TAIL - 3
LANES = 128
F32 = jnp.float32
BF16 = jnp.bfloat16


def size(axes):
    return math.prod(lax.axis_size(a) for a in axes)


def index(axes):
    place = 0
    for a in axes:
        place = place * lax.axis_size(a) + lax.axis_index(a)
    return place


def call(body, outs, ins, flops, scratch=(), **specs):
    moved = sum(math.prod(o.shape) * o.dtype.itemsize for o in list(outs) + list(ins))
    return pl.pallas_call(
        body,
        out_shape=tuple(outs),
        scratch_shapes=list(scratch),
        **specs,
        cost_estimate=pl.CostEstimate(flops=flops, bytes_accessed=moved, transcendentals=0),
        compiler_params=pltpu.CompilerParams(vmem_limit_bytes=40 << 20),
    )(*ins)


def shaped(shape, dtype):
    return jax.ShapeDtypeStruct(shape, dtype)


def iota(shape, dim):
    return lax.broadcasted_iota(jnp.int32, shape, dim)


def split3(value):
    a = value.astype(BF16).astype(F32)
    b = (value - a).astype(BF16).astype(F32)
    c = (value - a - b).astype(BF16).astype(F32)
    return a, b, c


def parted_sum(values):
    coarse = jnp.round(values * (1 / 16)) * 16.0
    middle = jnp.round((values - coarse) * 64.0) * (1 / 64)
    parts = (coarse, middle, values - coarse - middle)
    return [jnp.sum(p, axis=(0, 1), keepdims=True) for p in parts]


def sums_out(sums, lane, first):
    spread = jnp.zeros(lane.shape, F32)
    for i in range(3):
        spread = jnp.where((lane - first) % 3 == i, sums[i], spread)
    a, b, c = split3(spread)
    terms = jnp.where(lane < first + 3, a, jnp.where(lane < first + 6, b, c))
    return jnp.where((lane >= first) & (lane < first + 9), terms, 0.0)


def sums_in(terms, lane, first):
    inside = (lane >= first) & (lane < first + 9)
    return [
        jnp.sum(jnp.where(inside & ((lane - first) % 3 == i), terms, 0.0), axis=(0, 1), keepdims=True)
        for i in range(3)
    ]


def notes_out(level, rest, sums, width):
    count = 2 * level.shape[1]
    value = jnp.concatenate([level, rest, jnp.zeros((1, width - count), F32)], axis=1)
    lane = iota((1, width), 1)
    a, b, c = split3(value)
    c = jnp.where(lane < count, c, sums_out(sums, lane, count))
    sub = iota((TAIL, width), 0) - SLOTS
    return jnp.where(sub == 0, a, jnp.where(sub == 1, b, jnp.where(sub == 2, c, 0.0)))


def notes_in(tail, half):
    a, b, c = (tail[SLOTS + i : SLOTS + i + 1] for i in range(3))
    value = a + b + c
    return value[:, :half], value[:, half : 2 * half], c


def log_sum(values):
    high = jnp.max(values, axis=0, keepdims=True)
    return high + jnp.log(jnp.sum(jnp.exp(values - high), axis=0, keepdims=True))


def columns_of(rows):
    fill = jnp.zeros((LANES - rows.shape[0], rows.shape[1]), F32)
    return jnp.concatenate([rows, fill], axis=0).T


def own_first(positive, group, swapped):
    count = positive.shape[1] // (2 * group)
    even = [positive[:, 2 * i * group : (2 * i + 1) * group] for i in range(count)]
    odd = [positive[:, (2 * i + 1) * group : (2 * i + 2) * group] for i in range(count)]
    even, odd = jnp.concatenate(even, axis=1), jnp.concatenate(odd, axis=1)
    return jnp.concatenate(
        [jnp.where(swapped, odd, even), jnp.where(swapped, even, odd)], axis=1
    )


def chip_of(owner, n_index):
    return lax.div(lax.div(owner, n_index), 2) * n_index + lax.rem(owner, n_index)


def slot_plan(aims, group, shard):
    total_q = aims.shape[1]
    half = total_q // 2
    blocks = size(LINE)
    sub = group // blocks
    n_index = size(INDEX)
    across = n_index // blocks
    chip = chip_of(lax.div(aims, shard), n_index)
    query = iota((1, total_q), 1)
    part = lax.div(lax.rem(query, group), sub) + lax.div(query, half) * blocks
    key = (part * (size(ALL) // 2) + chip).astype(F32)
    down = columns_of(key)[:, 0:1]
    earlier = (down == key) & (iota((total_q, 1), 0) < query)
    rank = jnp.sum(earlier.astype(F32), axis=0, keepdims=True)
    rounds = lax.div(jnp.max(rank, axis=1, keepdims=True).astype(jnp.int32), SLOTS) + 1
    rank = rank.astype(jnp.int32)
    fits = rank < SLOTS
    slot = jnp.where((chip == index(("yl",) + INDEX)) & fits, part * TAIL + rank, -1)
    match = slot[:, :half] == iota((blocks * TAIL, 1), 0)
    found = jnp.sum(jnp.where(match, (aims[:, :half] + 1).astype(F32), 0.0), axis=1, keepdims=True)
    along = lax.rem(chip, n_index)
    near = (lax.div(chip, n_index) == index(("yl",))) & (lax.rem(along, across) == index(("z", "yh")))
    height = half // blocks + TAIL
    code = lax.div(along, across) * height + (height - TAIL) + rank
    code = jnp.where(near & fits, code, -1)[:, :half]
    return found.astype(jnp.int32) - 1, code.astype(F32), rounds


def first_kernel(every, passages, partner, positive, sent, notes, rounds):
    shard, width = passages.shape
    group = every.shape[2]
    half = every.shape[0] * group
    blocks = sent.shape[0]
    sub = group // blocks
    core = lax.axis_index("core")
    scale = 1.0 / math.sqrt(width)
    bases = [
        (index(("yl",)) * 2 + c) * (size(INDEX) * shard) + index(INDEX) * shard
        for c in (core, 1 - core)
    ]
    tables = [passages, partner]
    aims = own_first(positive[...] - 1, group, core == 1)
    wanted, code, rounds[...] = slot_plan(aims, group, shard)
    notes[...] = jnp.broadcast_to(code, notes.shape)
    block = every[:, core].reshape(half, width)
    others, top, only = [], None, None
    for base, table in zip(bases, tables):
        score = scale * lax.dot_general(
            table[...], block, (((1,), (1,)), ((), ())), preferred_element_type=F32
        )
        hit = aims[:, :half] == base + iota((shard, 1), 0)
        others.append(jnp.where(hit, LOW, score))
        high = jnp.max(others[-1], axis=0, keepdims=True)
        one = jnp.max(jnp.where(hit, score, LOW), axis=0, keepdims=True)
        top = high if top is None else jnp.maximum(top, high)
        only = one if only is None else jnp.maximum(only, one)
    picked = jnp.where(only > LOW, only, 0.0)
    terms = [jnp.exp(o - top) for o in others]
    total = sum(jnp.sum(t, axis=0, keepdims=True) for t in terms)
    high = jnp.maximum(top, only)
    level = high + jnp.log(total * jnp.exp(top - high) + jnp.exp(only - high))
    share = jnp.exp(top - level)
    pulled, slots = 0.0, 0.0
    for base, table, term in zip(bases, tables, terms):
        pulled = pulled + lax.dot_general(
            (term * share).astype(BF16),
            table[...],
            (((0,), (0,)), ((), ())),
            preferred_element_type=F32,
        )
        match = (wanted == base + iota((1, shard), 1)).astype(BF16)
        slots = slots + jnp.dot(match, table[...], preferred_element_type=F32)
    tile = notes_out(level, total * share, parted_sum(picked), width)
    for b in range(blocks):
        firsts = range(b * sub, half, group)
        piece = [pulled[i : i + sub] for i in firsts] + [slots[b * TAIL : (b + 1) * TAIL] + tile]
        sent[b] = jnp.concatenate(piece, axis=0).astype(BF16)


def line_kernel(got, notes, extra, sent, turned):
    peers, height, width = got.shape
    rows = height - TAIL
    half = rows * peers
    groups = lax.axis_size("yl")
    sub = rows // groups
    parts = [got[s].astype(F32) for s in range(peers)]
    read = [notes_in(p[rows:], half) for p in parts]
    levels = jnp.concatenate([r[0] for r in read], axis=0)
    rests = jnp.concatenate([r[1] for r in read], axis=0)
    last = jnp.concatenate([r[2] for r in read], axis=0)
    sums = sums_in(last, iota(last.shape, 1), 2 * half)
    level = log_sum(levels)
    keep = jnp.exp(levels - level)
    rest = jnp.sum(rests * keep, axis=0, keepdims=True)
    turned[...] = columns_of(jnp.concatenate([keep, rest, level, notes[0:1]], axis=0))
    first = lax.axis_index("x") * sub
    cols = jnp.concatenate(
        [turned[pl.ds(pl.multiple_of(g * sub * peers + first, 8), sub), :] for g in range(groups)],
        axis=0,
    )
    pulled = parts[0][:rows] * cols[:, 0:1]
    for s in range(1, peers):
        pulled = pulled + parts[s][:rows] * cols[:, s : s + 1]
    whole = jnp.concatenate(parts, axis=0).astype(BF16)
    code = cols[:, peers + 2 : peers + 3].astype(jnp.int32)
    fits = (code == iota((rows, peers * height), 1)).astype(BF16)
    chosen = jnp.dot(fits, whole, preferred_element_type=F32) + extra[...]
    mine = columns_of(cols)[:LANES]
    lane = iota((1, LANES), 1)
    tags = sums_out(sums, lane, 96)
    beside = []
    for g in range(groups):
        here = mine if g == 0 else pltpu.roll(mine, LANES - g * sub, 1)
        terms = split3(jnp.where(lane < sub, here, 0.0))
        spread = [[terms[0], pltpu.roll(terms[0], 48, 1)]]
        spread += [[pltpu.roll(terms[i], 16 * i + 48 * j, 1) for j in range(2)] for i in (1, 2)]
        own, rest = (spread[0][j] + spread[1][j] + spread[2][j] for j in range(2))
        beside.append(own[peers + 1 : peers + 2] + rest[peers : peers + 1] + tags)
    chunks = half // LANES
    down = iota((8, LANES), 0)
    wide = jnp.zeros((8, LANES), F32)
    for t, term in enumerate(split3(level)):
        for j in range(chunks):
            wide = jnp.where(down == t * chunks + j, term[:, j * LANES : (j + 1) * LANES], wide)
    wides = [jnp.where(down == 6, beside[g], wide) for g in range(groups)]
    across = width // LANES
    owners = sent.shape[0] // groups
    for d in range(sent.shape[0]):
        g = d // owners
        r, c = d % owners // across, d % owners % across
        if r * 8 < sub:
            at = g * sub + r * 8
            here, span = slice(at, at + 8), slice(c * LANES, (c + 1) * LANES)
            tile = [pulled[here, span], chosen[here, span]]
        else:
            tile = [jnp.zeros((16, LANES), F32)]
        sent[d] = jnp.concatenate(tile + [wides[g]], axis=0).astype(BF16)


def make_last_kernel(total_q, scale, rows, across):
    chunks = total_q // 2 // LANES

    def last_kernel(got, sent, level, turned):
        peers = got.shape[0]
        lane = iota((1, LANES), 1)
        parts = [got[s].astype(F32) for s in range(peers)]
        terms = jnp.concatenate([p[22:23] for p in parts], axis=0)
        picked = sums_in(terms, iota(terms.shape, 1), 96)
        moved = [terms] + [pltpu.roll(terms, LANES - 16 * i, 1) for i in range(1, 6)]
        own, rest = moved[0] + moved[1] + moved[2], moved[3] + moved[4] + moved[5]
        turned[0] = columns_of(own)
        turned[1] = columns_of(rest)
        first = jnp.minimum(lax.div(index(("z", "yh")), across) * 8, rows - 8)
        here = pl.ds(pl.multiple_of(first, 8), 8)
        tops = jnp.where(lane < peers, turned[0, here, :], LOW)
        keep = jnp.exp(tops - jnp.max(tops, axis=1, keepdims=True))
        keep = keep / jnp.sum(keep, axis=1, keepdims=True)
        rest = jnp.sum(keep * turned[1, here, :], axis=1, keepdims=True)
        wides = [
            p[16 : 16 + chunks] + p[16 + chunks : 16 + 2 * chunks] + p[16 + 2 * chunks : 16 + 3 * chunks]
            for p in parts
        ]
        high = wides[0]
        for s in range(1, peers):
            high = jnp.maximum(high, wides[s])
        total = jnp.zeros((chunks, LANES), F32)
        pulled, chosen = jnp.zeros((8, LANES), F32), jnp.zeros((8, LANES), F32)
        for s in range(peers):
            total = total + jnp.exp(wides[s] - high)
            pulled = pulled + keep[:, s : s + 1] * parts[s][:8]
            chosen = chosen + parts[s][8:16]
        lse = high + jnp.log(total)
        tile = ((pulled - rest * chosen) * (scale / total_q)).astype(BF16)
        for d in range(sent.shape[0]):
            sent[d] = tile
        terms = [a - b for a, b in zip(parted_sum(lse), picked)]
        for i in range(3):
            level[chunks + i : chunks + i + 1, :] = jnp.broadcast_to(terms[i], (1, LANES))
        level[:chunks, :] = lse

    return last_kernel


def passage_kernel(passages, level, level2, every, positive, out, loss):
    shard, width = out.shape
    group = every.shape[2]
    half = every.shape[0] * group
    total_q = 2 * half
    chunks = half // LANES
    core = lax.axis_index("core")
    down = index(ALL) * shard + iota((shard, 1), 0)
    scale = 1.0 / math.sqrt(width)
    aims = own_first(positive[...] - 1, group, core == 1)
    total = None
    for side, logs in enumerate([level, level2]):
        block = every[:, lax.rem(core + side, 2)].reshape(half, width)
        score = scale * lax.dot_general(
            passages[...], block, (((1,), (1,)), ((), ())), preferred_element_type=F32
        )
        lse = jnp.concatenate([logs[j : j + 1, :] for j in range(chunks)], axis=1)
        hit = aims[:, side * half : (side + 1) * half] == down
        weight = (jnp.exp(score - lse) - hit.astype(F32)) * (1.0 / total_q)
        term = jnp.dot(weight.astype(BF16), block, preferred_element_type=F32)
        total = term if total is None else total + term
    out[...] = (total * scale).astype(BF16)
    parts = level[chunks : chunks + 3, 0:1] + level2[chunks : chunks + 3, 0:1]
    loss[...] = (parts[0:1] + parts[1:2] + parts[2:3]) * (1.0 / total_q)


def make_assembly(down, across):
    def assembly(tiles, out):
        per = tiles.shape[0] // (out.shape[0] // (8 * down))
        for y in range(out.shape[0] // (8 * down)):
            for r in range(0, down, 2):
                for c in range(across):
                    pair = [tiles[y * per + (r + i) * across + c].astype(F32) for i in range(2)]
                    row = (y * down + r) * 8
                    out[row : row + 16, c * LANES : (c + 1) * LANES] = jnp.concatenate(
                        pair, axis=0
                    ).astype(BF16)

    return assembly


def on_device(queries, passages, positive):
    group, width = queries.shape
    scale = 1.0 / math.sqrt(width)
    total_q = positive.shape[0]
    half = total_q // 2
    shard = passages.shape[0]
    n_index = size(INDEX)
    n_line = size(LINE)
    n_rest = size(REST)
    block = half // n_line
    sub = group // n_line
    core = lax.axis_index("core")
    n_yl = lax.axis_size("yl")
    columns = lax.axis_index(ALL) * shard + jnp.arange(shard, dtype=jnp.int32)

    def swap(value):
        return lax.ppermute(value, "core", [(0, 1), (1, 0)])

    row = positive.reshape(1, total_q) + 1
    product = total_q * shard * width
    partner = swap(passages)
    queries, row = lax.optimization_barrier((queries, row))
    every = lax.all_gather(queries, QUERY, axis=0, tiled=True).reshape(n_yl, 2, group, width)
    sent, notes, rounds = call(
        first_kernel,
        [
            shaped((n_line, block + TAIL, width), BF16),
            shaped((8, half), F32),
            shaped((1, 1), jnp.int32),
        ],
        [every, passages, partner, row],
        4 * product,
    )

    def later_turn(turn, held):
        late, turn = lax.optimization_barrier((row, turn))
        aims = (late - 1).reshape(n_yl, 2, n_line, sub).transpose(1, 2, 0, 3).reshape(2, n_line, block)
        aims = jnp.where(core == 0, aims, aims[::-1])
        chip = chip_of(aims // shard, n_index)
        same = chip[..., :, None] == chip[..., None, :]
        before = jnp.arange(block)[:, None] > jnp.arange(block)[None, :]
        rank = jnp.sum((same & before).astype(jnp.int32), axis=-1)
        slots = turn * SLOTS + jnp.arange(SLOTS, dtype=jnp.int32)
        fits = (chip[0] == index(("yl",) + INDEX))[..., None] & (rank[0][..., None] == slots)
        wanted = jnp.max(jnp.where(fits, aims[0][..., None], -1), axis=1).reshape(-1, 1)
        rows = 0.0
        for side, table in ((core, passages), (1 - core, partner)):
            owner = (lax.axis_index("yl") * 2 + side) * n_index + lax.axis_index(INDEX)
            match = (wanted == owner * shard + jnp.arange(shard, dtype=jnp.int32)).astype(BF16)
            rows = rows + jnp.dot(match, table, preferred_element_type=F32)
        rows = rows.astype(BF16).reshape(n_line, SLOTS, width)
        rows = lax.all_to_all(rows, LINE, 0, 0, tiled=True)
        place = lax.axis_index("x")
        my_chip = lax.dynamic_index_in_dim(chip[0], place, 0, keepdims=False)
        my_rank = lax.dynamic_index_in_dim(rank[0], place, 0, keepdims=False)
        peer = jnp.arange(n_line, dtype=jnp.int32) * (n_index // n_line)
        peer_chip = lax.axis_index("yl") * n_index + peer + lax.axis_index(("z", "yh"))
        fits = (my_chip[:, None] == peer_chip[None, :])[..., None]
        fits = (fits & (my_rank[:, None, None] == slots)).astype(BF16)
        fits = fits.reshape(block, n_line * SLOTS)
        return held + jnp.dot(fits, rows.reshape(-1, width), preferred_element_type=F32)

    extra = lax.fori_loop(1, rounds[0, 0], later_turn, jnp.zeros((block, width), F32))
    got = lax.all_to_all(sent, LINE, 0, 0, tiled=True)
    (sent,) = call(
        line_kernel,
        [shaped((n_rest, 24, LANES), BF16)],
        [got, notes, extra],
        half * width * 8,
        [pltpu.VMEM((half, LANES), F32)],
    )
    got = lax.all_to_all(sent, REST, 0, 0, tiled=True)
    spread = n_index
    sent, level = call(
        make_last_kernel(total_q, scale, sub, width // LANES),
        [shaped((spread, 8, LANES), BF16), shaped((8, LANES), F32)],
        [got],
        half * width * 8,
        [pltpu.VMEM((2, LANES, LANES), F32)],
    )
    tiles = lax.all_to_all(sent, INDEX, 0, 0, tiled=True)
    passage_grad, loss = call(
        passage_kernel,
        [shaped((shard, width), BF16), shaped((1, 1), F32)],
        [passages, level, swap(level), every, row],
        4 * product,
    )
    (query_grad,) = call(
        make_assembly(sub // 8, width // LANES),
        [shaped((group, width), BF16)],
        [tiles],
        group * width,
    )
    return (loss[0, 0], query_grad, passage_grad)


def build(mesh):
    return jax.shard_map(
        on_device,
        mesh=mesh,
        in_specs=(P(QUERY, None), P(ALL, None), P()),
        out_specs=(P(), P(QUERY, None), P(ALL, None)),
        check_vma=False,
    )


def solution(mesh):
    devices = np.asarray(mesh.devices).reshape(4, 2, 4, 8, 2)
    return build(Mesh(devices, ("yl", "core", "x", "z", "yh")))
```

```python
import math

import jax
import jax.numpy as jnp
import numpy as np
from jax import lax
from jax.experimental import pallas as pl
from jax.experimental.pallas import tpu as pltpu
from jax.sharding import Mesh
from jax.sharding import PartitionSpec as P

QUERY = ("yl", "core")
INDEX = ("x", "z", "yh")
ALL = QUERY + INDEX
LINE = ("x",)
REST = ("yl", "z", "yh")
LOW = -1e30
TAIL = 8
SLOTS = TAIL - 3
LANES = 128
F32 = jnp.float32
BF16 = jnp.bfloat16


def size(axes):
    return math.prod(lax.axis_size(a) for a in axes)


def index(axes):
    place = 0
    for a in axes:
        place = place * lax.axis_size(a) + lax.axis_index(a)
    return place


def call(body, outs, ins, flops, scratch=(), **specs):
    moved = sum(math.prod(o.shape) * o.dtype.itemsize for o in list(outs) + list(ins))
    return pl.pallas_call(
        body,
        out_shape=tuple(outs),
        scratch_shapes=list(scratch),
        **specs,
        cost_estimate=pl.CostEstimate(flops=flops, bytes_accessed=moved, transcendentals=0),
        compiler_params=pltpu.CompilerParams(vmem_limit_bytes=40 << 20),
    )(*ins)


def shaped(shape, dtype):
    return jax.ShapeDtypeStruct(shape, dtype)


def iota(shape, dim):
    return lax.broadcasted_iota(jnp.int32, shape, dim)


def split3(value):
    a = value.astype(BF16).astype(F32)
    b = (value - a).astype(BF16).astype(F32)
    c = (value - a - b).astype(BF16).astype(F32)
    return a, b, c


def parted_sum(values):
    coarse = jnp.round(values * (1 / 16)) * 16.0
    middle = jnp.round((values - coarse) * 64.0) * (1 / 64)
    parts = (coarse, middle, values - coarse - middle)
    return [jnp.sum(p, axis=(0, 1), keepdims=True) for p in parts]


def sums_out(sums, lane, first):
    spread = jnp.zeros(lane.shape, F32)
    for i in range(3):
        spread = jnp.where((lane - first) % 3 == i, sums[i], spread)
    a, b, c = split3(spread)
    terms = jnp.where(lane < first + 3, a, jnp.where(lane < first + 6, b, c))
    return jnp.where((lane >= first) & (lane < first + 9), terms, 0.0)


def sums_in(terms, lane, first):
    inside = (lane >= first) & (lane < first + 9)
    return [
        jnp.sum(jnp.where(inside & ((lane - first) % 3 == i), terms, 0.0), axis=(0, 1), keepdims=True)
        for i in range(3)
    ]


def notes_out(level, rest, sums, width):
    count = 2 * level.shape[1]
    value = jnp.concatenate([level, rest, jnp.zeros((1, width - count), F32)], axis=1)
    lane = iota((1, width), 1)
    a, b, c = split3(value)
    c = jnp.where(lane < count, c, sums_out(sums, lane, count))
    sub = iota((TAIL, width), 0) - SLOTS
    return jnp.where(sub == 0, a, jnp.where(sub == 1, b, jnp.where(sub == 2, c, 0.0)))


def notes_in(tail, half):
    a, b, c = (tail[SLOTS + i : SLOTS + i + 1] for i in range(3))
    value = a + b + c
    return value[:, :half], value[:, half : 2 * half], c


def log_sum(values):
    high = jnp.max(values, axis=0, keepdims=True)
    return high + jnp.log(jnp.sum(jnp.exp(values - high), axis=0, keepdims=True))


def columns_of(rows):
    fill = jnp.zeros((LANES - rows.shape[0], rows.shape[1]), F32)
    return jnp.concatenate([rows, fill], axis=0).T


def own_first(positive, group, swapped):
    count = positive.shape[1] // (2 * group)
    even = [positive[:, 2 * i * group : (2 * i + 1) * group] for i in range(count)]
    odd = [positive[:, (2 * i + 1) * group : (2 * i + 2) * group] for i in range(count)]
    even, odd = jnp.concatenate(even, axis=1), jnp.concatenate(odd, axis=1)
    return jnp.concatenate(
        [jnp.where(swapped, odd, even), jnp.where(swapped, even, odd)], axis=1
    )


def chip_of(owner, n_index):
    return lax.div(lax.div(owner, n_index), 2) * n_index + lax.rem(owner, n_index)


def slot_plan(aims, group, shard):
    total_q = aims.shape[1]
    half = total_q // 2
    blocks = size(LINE)
    sub = group // blocks
    n_index = size(INDEX)
    across = n_index // blocks
    chip = chip_of(lax.div(aims, shard), n_index)
    query = iota((1, total_q), 1)
    part = lax.div(lax.rem(query, group), sub) + lax.div(query, half) * blocks
    key = (part * (size(ALL) // 2) + chip).astype(F32)
    down = columns_of(key)[:, 0:1]
    earlier = (down == key) & (iota((total_q, 1), 0) < query)
    rank = jnp.sum(earlier.astype(F32), axis=0, keepdims=True)
    rounds = lax.div(jnp.max(rank, axis=1, keepdims=True).astype(jnp.int32), SLOTS) + 1
    rank = rank.astype(jnp.int32)
    fits = rank < SLOTS
    slot = jnp.where((chip == index(("yl",) + INDEX)) & fits, part * TAIL + rank, -1)
    match = slot[:, :half] == iota((blocks * TAIL, 1), 0)
    found = jnp.sum(jnp.where(match, (aims[:, :half] + 1).astype(F32), 0.0), axis=1, keepdims=True)
    along = lax.rem(chip, n_index)
    near = (lax.div(chip, n_index) == index(("yl",))) & (lax.rem(along, across) == index(("z", "yh")))
    height = half // blocks + TAIL
    code = lax.div(along, across) * height + (height - TAIL) + rank
    code = jnp.where(near & fits, code, -1)[:, :half]
    return found.astype(jnp.int32) - 1, code.astype(F32), rounds


def make_plan_kernel(group, shard):
    def plan_kernel(positive, aims, wanted, notes, rounds):
        value = own_first(positive[...], group, lax.axis_index("core") == 1)
        aims[...] = value
        wanted[...], code, rounds[...] = slot_plan(value, group, shard)
        notes[...] = jnp.broadcast_to(code, notes.shape)

    return plan_kernel


def first_kernel(every, passages, partner, aims, wanted, sent):
    shard, width = passages.shape
    group = every.shape[2]
    half = every.shape[0] * group
    blocks = sent.shape[0]
    sub = group // blocks
    core = lax.axis_index("core")
    scale = 1.0 / math.sqrt(width)
    bases = [
        (index(("yl",)) * 2 + c) * (size(INDEX) * shard) + index(INDEX) * shard
        for c in (core, 1 - core)
    ]
    tables = [passages, partner]
    block = every[:, core].reshape(half, width)
    others, top, only = [], None, None
    for base, table in zip(bases, tables):
        score = scale * lax.dot_general(
            table[...], block, (((1,), (1,)), ((), ())), preferred_element_type=F32
        )
        hit = aims[0:1, :half] == base + iota((shard, 1), 0)
        others.append(jnp.where(hit, LOW, score))
        high = jnp.max(others[-1], axis=0, keepdims=True)
        one = jnp.max(jnp.where(hit, score, LOW), axis=0, keepdims=True)
        top = high if top is None else jnp.maximum(top, high)
        only = one if only is None else jnp.maximum(only, one)
    picked = jnp.where(only > LOW, only, 0.0)
    terms = [jnp.exp(o - top) for o in others]
    total = sum(jnp.sum(t, axis=0, keepdims=True) for t in terms)
    high = jnp.maximum(top, only)
    level = high + jnp.log(total * jnp.exp(top - high) + jnp.exp(only - high))
    share = jnp.exp(top - level)
    pulled, slots = 0.0, 0.0
    for base, table, term in zip(bases, tables, terms):
        pulled = pulled + lax.dot_general(
            (term * share).astype(BF16),
            table[...],
            (((0,), (0,)), ((), ())),
            preferred_element_type=F32,
        )
        match = (wanted[...] == base + iota((1, shard), 1)).astype(BF16)
        slots = slots + jnp.dot(match, table[...], preferred_element_type=F32)
    tile = notes_out(level, total * share, parted_sum(picked), width)
    for b in range(blocks):
        firsts = range(b * sub, half, group)
        piece = [pulled[i : i + sub] for i in firsts] + [slots[b * TAIL : (b + 1) * TAIL] + tile]
        sent[b] = jnp.concatenate(piece, axis=0).astype(BF16)


def line_kernel(got, notes, extra, sent, turned):
    peers, height, width = got.shape
    rows = height - TAIL
    half = rows * peers
    groups = lax.axis_size("yl")
    sub = rows // groups
    parts = [got[s].astype(F32) for s in range(peers)]
    read = [notes_in(p[rows:], half) for p in parts]
    levels = jnp.concatenate([r[0] for r in read], axis=0)
    rests = jnp.concatenate([r[1] for r in read], axis=0)
    last = jnp.concatenate([r[2] for r in read], axis=0)
    sums = sums_in(last, iota(last.shape, 1), 2 * half)
    level = log_sum(levels)
    keep = jnp.exp(levels - level)
    rest = jnp.sum(rests * keep, axis=0, keepdims=True)
    turned[...] = columns_of(jnp.concatenate([keep, rest, level, notes[0:1]], axis=0))
    first = lax.axis_index("x") * sub
    cols = jnp.concatenate(
        [turned[pl.ds(pl.multiple_of(g * sub * peers + first, 8), sub), :] for g in range(groups)],
        axis=0,
    )
    pulled = parts[0][:rows] * cols[:, 0:1]
    for s in range(1, peers):
        pulled = pulled + parts[s][:rows] * cols[:, s : s + 1]
    whole = jnp.concatenate(parts, axis=0).astype(BF16)
    code = cols[:, peers + 2 : peers + 3].astype(jnp.int32)
    fits = (code == iota((rows, peers * height), 1)).astype(BF16)
    chosen = jnp.dot(fits, whole, preferred_element_type=F32) + extra[...]
    mine = columns_of(cols)[:LANES]
    lane = iota((1, LANES), 1)
    tags = sums_out(sums, lane, 96)
    beside = []
    for g in range(groups):
        here = mine if g == 0 else pltpu.roll(mine, LANES - g * sub, 1)
        terms = split3(jnp.where(lane < sub, here, 0.0))
        spread = [[terms[0], pltpu.roll(terms[0], 48, 1)]]
        spread += [[pltpu.roll(terms[i], 16 * i + 48 * j, 1) for j in range(2)] for i in (1, 2)]
        own, rest = (spread[0][j] + spread[1][j] + spread[2][j] for j in range(2))
        beside.append(own[peers + 1 : peers + 2] + rest[peers : peers + 1] + tags)
    chunks = half // LANES
    down = iota((8, LANES), 0)
    wide = jnp.zeros((8, LANES), F32)
    for t, term in enumerate(split3(level)):
        for j in range(chunks):
            wide = jnp.where(down == t * chunks + j, term[:, j * LANES : (j + 1) * LANES], wide)
    wides = [jnp.where(down == 6, beside[g], wide) for g in range(groups)]
    across = width // LANES
    owners = sent.shape[0] // groups
    for d in range(sent.shape[0]):
        g = d // owners
        r, c = d % owners // across, d % owners % across
        if r * 8 < sub:
            at = g * sub + r * 8
            here, span = slice(at, at + 8), slice(c * LANES, (c + 1) * LANES)
            tile = [pulled[here, span], chosen[here, span]]
        else:
            tile = [jnp.zeros((16, LANES), F32)]
        sent[d] = jnp.concatenate(tile + [wides[g]], axis=0).astype(BF16)


def make_last_kernel(total_q, scale, rows, across):
    chunks = total_q // 2 // LANES

    def last_kernel(got, sent, level, turned):
        peers = got.shape[0]
        lane = iota((1, LANES), 1)
        parts = [got[s].astype(F32) for s in range(peers)]
        terms = jnp.concatenate([p[22:23] for p in parts], axis=0)
        picked = sums_in(terms, iota(terms.shape, 1), 96)
        moved = [terms] + [pltpu.roll(terms, LANES - 16 * i, 1) for i in range(1, 6)]
        own, rest = moved[0] + moved[1] + moved[2], moved[3] + moved[4] + moved[5]
        turned[0] = columns_of(own)
        turned[1] = columns_of(rest)
        first = jnp.minimum(lax.div(index(("z", "yh")), across) * 8, rows - 8)
        here = pl.ds(pl.multiple_of(first, 8), 8)
        tops = jnp.where(lane < peers, turned[0, here, :], LOW)
        keep = jnp.exp(tops - jnp.max(tops, axis=1, keepdims=True))
        keep = keep / jnp.sum(keep, axis=1, keepdims=True)
        rest = jnp.sum(keep * turned[1, here, :], axis=1, keepdims=True)
        wides = [
            p[16 : 16 + chunks] + p[16 + chunks : 16 + 2 * chunks] + p[16 + 2 * chunks : 16 + 3 * chunks]
            for p in parts
        ]
        high = wides[0]
        for s in range(1, peers):
            high = jnp.maximum(high, wides[s])
        total = jnp.zeros((chunks, LANES), F32)
        pulled, chosen = jnp.zeros((8, LANES), F32), jnp.zeros((8, LANES), F32)
        for s in range(peers):
            total = total + jnp.exp(wides[s] - high)
            pulled = pulled + keep[:, s : s + 1] * parts[s][:8]
            chosen = chosen + parts[s][8:16]
        lse = high + jnp.log(total)
        tile = ((pulled - rest * chosen) * (scale / total_q)).astype(BF16)
        for d in range(sent.shape[0]):
            sent[d] = tile
        terms = [a - b for a, b in zip(parted_sum(lse), picked)]
        for i in range(3):
            level[chunks + i : chunks + i + 1, :] = jnp.broadcast_to(terms[i], (1, LANES))
        level[:chunks, :] = lse

    return last_kernel


def passage_kernel(passages, level, level2, every, aims, out, loss):
    shard, width = out.shape
    group = every.shape[2]
    half = every.shape[0] * group
    total_q = 2 * half
    chunks = half // LANES
    core = lax.axis_index("core")
    down = index(ALL) * shard + iota((shard, 1), 0)
    scale = 1.0 / math.sqrt(width)
    total = None
    for side, logs in enumerate([level, level2]):
        block = every[:, lax.rem(core + side, 2)].reshape(half, width)
        score = scale * lax.dot_general(
            passages[...], block, (((1,), (1,)), ((), ())), preferred_element_type=F32
        )
        lse = jnp.concatenate([logs[j : j + 1, :] for j in range(chunks)], axis=1)
        hit = aims[:, side * half : (side + 1) * half] == down
        weight = (jnp.exp(score - lse) - hit.astype(F32)) * (1.0 / total_q)
        term = jnp.dot(weight.astype(BF16), block, preferred_element_type=F32)
        total = term if total is None else total + term
    out[...] = (total * scale).astype(BF16)
    parts = level[chunks : chunks + 3, 0:1] + level2[chunks : chunks + 3, 0:1]
    loss[...] = (parts[0:1] + parts[1:2] + parts[2:3]) * (1.0 / total_q)


def make_assembly(down, across):
    def assembly(tiles, out):
        per = tiles.shape[0] // (out.shape[0] // (8 * down))
        for y in range(out.shape[0] // (8 * down)):
            for r in range(0, down, 2):
                for c in range(across):
                    pair = [tiles[y * per + (r + i) * across + c].astype(F32) for i in range(2)]
                    row = (y * down + r) * 8
                    out[row : row + 16, c * LANES : (c + 1) * LANES] = jnp.concatenate(
                        pair, axis=0
                    ).astype(BF16)

    return assembly


def on_device(queries, passages, positive):
    group, width = queries.shape
    scale = 1.0 / math.sqrt(width)
    total_q = positive.shape[0]
    half = total_q // 2
    shard = passages.shape[0]
    n_index = size(INDEX)
    n_line = size(LINE)
    n_rest = size(REST)
    block = half // n_line
    sub = group // n_line
    core = lax.axis_index("core")
    n_yl = lax.axis_size("yl")
    columns = lax.axis_index(ALL) * shard + jnp.arange(shard, dtype=jnp.int32)

    def swap(value):
        return lax.ppermute(value, "core", [(0, 1), (1, 0)])

    product = total_q * shard * width
    partner = swap(passages)
    aims, wanted, notes, rounds = call(
        make_plan_kernel(group, shard),
        [
            shaped((1, total_q), jnp.int32),
            shaped((n_line * TAIL, 1), jnp.int32),
            shaped((8, half), F32),
            shaped((1, 1), jnp.int32),
        ],
        [positive.reshape(1, total_q)],
        total_q * total_q,
    )
    queries, aims = lax.optimization_barrier((queries, aims))
    every = lax.all_gather(queries, QUERY, axis=0, tiled=True).reshape(n_yl, 2, group, width)
    (sent,) = call(
        first_kernel,
        [shaped((n_line, block + TAIL, width), BF16)],
        [every, passages, partner, aims, wanted],
        4 * product,
    )

    def later_turn(turn, held):
        late, turn = lax.optimization_barrier((aims, turn))
        late = late.reshape(2, n_yl, n_line, sub).transpose(0, 2, 1, 3).reshape(2, n_line, block)
        chip = chip_of(late // shard, n_index)
        same = chip[..., :, None] == chip[..., None, :]
        before = jnp.arange(block)[:, None] > jnp.arange(block)[None, :]
        rank = jnp.sum((same & before).astype(jnp.int32), axis=-1)
        slots = turn * SLOTS + jnp.arange(SLOTS, dtype=jnp.int32)
        fits = (chip[0] == index(("yl",) + INDEX))[..., None] & (rank[0][..., None] == slots)
        wanted = jnp.max(jnp.where(fits, late[0][..., None], -1), axis=1).reshape(-1, 1)
        rows = 0.0
        for side, table in ((core, passages), (1 - core, partner)):
            owner = (lax.axis_index("yl") * 2 + side) * n_index + lax.axis_index(INDEX)
            match = (wanted == owner * shard + jnp.arange(shard, dtype=jnp.int32)).astype(BF16)
            rows = rows + jnp.dot(match, table, preferred_element_type=F32)
        rows = rows.astype(BF16).reshape(n_line, SLOTS, width)
        rows = lax.all_to_all(rows, LINE, 0, 0, tiled=True)
        place = lax.axis_index("x")
        my_chip = lax.dynamic_index_in_dim(chip[0], place, 0, keepdims=False)
        my_rank = lax.dynamic_index_in_dim(rank[0], place, 0, keepdims=False)
        peer = jnp.arange(n_line, dtype=jnp.int32) * (n_index // n_line)
        peer_chip = lax.axis_index("yl") * n_index + peer + lax.axis_index(("z", "yh"))
        fits = (my_chip[:, None] == peer_chip[None, :])[..., None]
        fits = (fits & (my_rank[:, None, None] == slots)).astype(BF16)
        fits = fits.reshape(block, n_line * SLOTS)
        return held + jnp.dot(fits, rows.reshape(-1, width), preferred_element_type=F32)

    extra = lax.fori_loop(1, rounds[0, 0], later_turn, jnp.zeros((block, width), F32))
    got = lax.all_to_all(sent, LINE, 0, 0, tiled=True)
    (sent,) = call(
        line_kernel,
        [shaped((n_rest, 24, LANES), BF16)],
        [got, notes, extra],
        half * width * 8,
        [pltpu.VMEM((half, LANES), F32)],
    )
    got = lax.all_to_all(sent, REST, 0, 0, tiled=True)
    spread = n_index
    sent, level = call(
        make_last_kernel(total_q, scale, sub, width // LANES),
        [shaped((spread, 8, LANES), BF16), shaped((8, LANES), F32)],
        [got],
        half * width * 8,
        [pltpu.VMEM((2, LANES, LANES), F32)],
    )
    tiles = lax.all_to_all(sent, INDEX, 0, 0, tiled=True)
    passage_grad, loss = call(
        passage_kernel,
        [shaped((shard, width), BF16), shaped((1, 1), F32)],
        [passages, level, swap(level), every, aims],
        4 * product,
    )
    (query_grad,) = call(
        make_assembly(sub // 8, width // LANES),
        [shaped((group, width), BF16)],
        [tiles],
        group * width,
    )
    return (loss[0, 0], query_grad, passage_grad)


def build(mesh):
    return jax.shard_map(
        on_device,
        mesh=mesh,
        in_specs=(P(QUERY, None), P(ALL, None), P()),
        out_specs=(P(), P(QUERY, None), P(ALL, None)),
        check_vma=False,
    )


def solution(mesh):
    devices = np.asarray(mesh.devices).reshape(4, 2, 4, 8, 2)
    return build(Mesh(devices, ("yl", "core", "x", "z", "yh")))
```

```python
import math

import jax
import jax.numpy as jnp
import numpy as np
from jax import lax
from jax.experimental import pallas as pl
from jax.experimental.pallas import tpu as pltpu
from jax.sharding import Mesh
from jax.sharding import PartitionSpec as P

QUERY = ("yl", "core")
INDEX = ("x", "z", "yh")
ALL = QUERY + INDEX
LINE = ("x",)
REST = ("yl", "z", "yh")
LOW = -1e30
TAIL = 8
SLOTS = TAIL - 3
LANES = 128
F32 = jnp.float32
BF16 = jnp.bfloat16


def size(axes):
    return math.prod(lax.axis_size(a) for a in axes)


def index(axes):
    place = 0
    for a in axes:
        place = place * lax.axis_size(a) + lax.axis_index(a)
    return place


def call(body, outs, ins, flops, scratch=(), **specs):
    moved = sum(math.prod(o.shape) * o.dtype.itemsize for o in list(outs) + list(ins))
    return pl.pallas_call(
        body,
        out_shape=tuple(outs),
        scratch_shapes=list(scratch),
        **specs,
        cost_estimate=pl.CostEstimate(flops=flops, bytes_accessed=moved, transcendentals=0),
        compiler_params=pltpu.CompilerParams(vmem_limit_bytes=40 << 20),
    )(*ins)


def shaped(shape, dtype):
    return jax.ShapeDtypeStruct(shape, dtype)


def iota(shape, dim):
    return lax.broadcasted_iota(jnp.int32, shape, dim)


def split3(value):
    a = value.astype(BF16).astype(F32)
    b = (value - a).astype(BF16).astype(F32)
    c = (value - a - b).astype(BF16).astype(F32)
    return a, b, c


def parted_sum(values):
    coarse = jnp.round(values * (1 / 16)) * 16.0
    middle = jnp.round((values - coarse) * 64.0) * (1 / 64)
    parts = (coarse, middle, values - coarse - middle)
    return [jnp.sum(p, axis=(0, 1), keepdims=True) for p in parts]


def sums_out(sums, lane, first):
    spread = jnp.zeros(lane.shape, F32)
    for i in range(3):
        spread = jnp.where((lane - first) % 3 == i, sums[i], spread)
    a, b, c = split3(spread)
    terms = jnp.where(lane < first + 3, a, jnp.where(lane < first + 6, b, c))
    return jnp.where((lane >= first) & (lane < first + 9), terms, 0.0)


def sums_in(terms, lane, first):
    inside = (lane >= first) & (lane < first + 9)
    return [
        jnp.sum(jnp.where(inside & ((lane - first) % 3 == i), terms, 0.0), axis=(0, 1), keepdims=True)
        for i in range(3)
    ]


def notes_out(level, rest, sums, width):
    count = 2 * level.shape[1]
    value = jnp.concatenate([level, rest, jnp.zeros((1, width - count), F32)], axis=1)
    lane = iota((1, width), 1)
    a, b, c = split3(value)
    c = jnp.where(lane < count, c, sums_out(sums, lane, count))
    sub = iota((TAIL, width), 0) - SLOTS
    return jnp.where(sub == 0, a, jnp.where(sub == 1, b, jnp.where(sub == 2, c, 0.0)))


def notes_in(tail, half):
    a, b, c = (tail[SLOTS + i : SLOTS + i + 1] for i in range(3))
    value = a + b + c
    return value[:, :half], value[:, half : 2 * half], c


def log_sum(values):
    high = jnp.max(values, axis=0, keepdims=True)
    return high + jnp.log(jnp.sum(jnp.exp(values - high), axis=0, keepdims=True))


def columns_of(rows):
    fill = jnp.zeros((LANES - rows.shape[0], rows.shape[1]), F32)
    return jnp.concatenate([rows, fill], axis=0).T


def own_first(positive, group, swapped):
    count = positive.shape[1] // (2 * group)
    even = [positive[:, 2 * i * group : (2 * i + 1) * group] for i in range(count)]
    odd = [positive[:, (2 * i + 1) * group : (2 * i + 2) * group] for i in range(count)]
    even, odd = jnp.concatenate(even, axis=1), jnp.concatenate(odd, axis=1)
    return jnp.concatenate(
        [jnp.where(swapped, odd, even), jnp.where(swapped, even, odd)], axis=1
    )


def chip_of(owner, n_index):
    return lax.div(lax.div(owner, n_index), 2) * n_index + lax.rem(owner, n_index)


def slot_plan(aims, group, shard):
    total_q = aims.shape[1]
    half = total_q // 2
    blocks = size(LINE)
    sub = group // blocks
    n_index = size(INDEX)
    across = n_index // blocks
    chip = chip_of(lax.div(aims, shard), n_index)
    query = iota((1, total_q), 1)
    part = lax.div(lax.rem(query, group), sub) + lax.div(query, half) * blocks
    key = (part * (size(ALL) // 2) + chip).astype(F32)
    down = columns_of(key)[:, 0:1]
    earlier = (down == key) & (iota((total_q, 1), 0) < query)
    rank = jnp.sum(earlier.astype(F32), axis=0, keepdims=True)
    rounds = lax.div(jnp.max(rank, axis=1, keepdims=True).astype(jnp.int32), SLOTS) + 1
    rank = rank.astype(jnp.int32)
    fits = rank < SLOTS
    slot = jnp.where((chip == index(("yl",) + INDEX)) & fits, part * TAIL + rank, -1)
    match = slot[:, :half] == iota((blocks * TAIL, 1), 0)
    found = jnp.sum(jnp.where(match, (aims[:, :half] + 1).astype(F32), 0.0), axis=1, keepdims=True)
    along = lax.rem(chip, n_index)
    near = (lax.div(chip, n_index) == index(("yl",))) & (lax.rem(along, across) == index(("z", "yh")))
    height = half // blocks + TAIL
    code = lax.div(along, across) * height + (height - TAIL) + rank
    code = jnp.where(near & fits, code, -1)[:, :half]
    return found.astype(jnp.int32) - 1, code.astype(F32), rounds


def first_kernel(every, passages, partner, positive, sent, notes, rounds):
    shard, width = passages.shape
    group = every.shape[2]
    half = every.shape[0] * group
    blocks = sent.shape[0]
    sub = group // blocks
    core = lax.axis_index("core")
    scale = 1.0 / math.sqrt(width)
    bases = [
        (index(("yl",)) * 2 + c) * (size(INDEX) * shard) + index(INDEX) * shard
        for c in (core, 1 - core)
    ]
    tables = [passages, partner]
    aims = own_first(positive[...] - 1, group, core == 1)
    wanted, code, rounds[...] = slot_plan(aims, group, shard)
    notes[...] = jnp.broadcast_to(code, notes.shape)
    block = every[:, core].reshape(half, width)
    others, top, only = [], None, None
    for base, table in zip(bases, tables):
        score = scale * lax.dot_general(
            table[...], block, (((1,), (1,)), ((), ())), preferred_element_type=F32
        )
        hit = aims[:, :half] == base + iota((shard, 1), 0)
        others.append(jnp.where(hit, LOW, score))
        high = jnp.max(others[-1], axis=0, keepdims=True)
        one = jnp.max(jnp.where(hit, score, LOW), axis=0, keepdims=True)
        top = high if top is None else jnp.maximum(top, high)
        only = one if only is None else jnp.maximum(only, one)
    picked = jnp.where(only > LOW, only, 0.0)
    terms = [jnp.exp(o - top) for o in others]
    total = sum(jnp.sum(t, axis=0, keepdims=True) for t in terms)
    high = jnp.maximum(top, only)
    level = high + jnp.log(total * jnp.exp(top - high) + jnp.exp(only - high))
    share = jnp.exp(top - level)
    pulled, slots = 0.0, 0.0
    for base, table, term in zip(bases, tables, terms):
        pulled = pulled + lax.dot_general(
            (term * share).astype(BF16),
            table[...],
            (((0,), (0,)), ((), ())),
            preferred_element_type=F32,
        )
        match = (wanted == base + iota((1, shard), 1)).astype(BF16)
        slots = slots + jnp.dot(match, table[...], preferred_element_type=F32)
    tile = notes_out(level, total * share, parted_sum(picked), width)
    for b in range(blocks):
        firsts = range(b * sub, half, group)
        piece = [pulled[i : i + sub] for i in firsts] + [slots[b * TAIL : (b + 1) * TAIL] + tile]
        sent[b] = jnp.concatenate(piece, axis=0).astype(BF16)


def line_kernel(got, notes, extra, sent, turned):
    peers, height, width = got.shape
    rows = height - TAIL
    half = rows * peers
    groups = lax.axis_size("yl")
    sub = rows // groups
    parts = [got[s].astype(F32) for s in range(peers)]
    read = [notes_in(p[rows:], half) for p in parts]
    levels = jnp.concatenate([r[0] for r in read], axis=0)
    rests = jnp.concatenate([r[1] for r in read], axis=0)
    last = jnp.concatenate([r[2] for r in read], axis=0)
    sums = sums_in(last, iota(last.shape, 1), 2 * half)
    level = log_sum(levels)
    keep = jnp.exp(levels - level)
    rest = jnp.sum(rests * keep, axis=0, keepdims=True)
    turned[...] = columns_of(jnp.concatenate([keep, rest, level, notes[0:1]], axis=0))
    first = lax.axis_index("x") * sub
    cols = jnp.concatenate(
        [turned[pl.ds(pl.multiple_of(g * sub * peers + first, 8), sub), :] for g in range(groups)],
        axis=0,
    )
    pulled = parts[0][:rows] * cols[:, 0:1]
    for s in range(1, peers):
        pulled = pulled + parts[s][:rows] * cols[:, s : s + 1]
    whole = jnp.concatenate(parts, axis=0).astype(BF16)
    code = cols[:, peers + 2 : peers + 3].astype(jnp.int32)
    fits = (code == iota((rows, peers * height), 1)).astype(BF16)
    chosen = jnp.dot(fits, whole, preferred_element_type=F32) + extra[...]
    mine = columns_of(cols)[:LANES]
    lane = iota((1, LANES), 1)
    tags = sums_out(sums, lane, 96)
    beside = []
    for g in range(groups):
        here = mine if g == 0 else pltpu.roll(mine, LANES - g * sub, 1)
        terms = split3(jnp.where(lane < sub, here, 0.0))
        spread = [[terms[0], pltpu.roll(terms[0], 48, 1)]]
        spread += [[pltpu.roll(terms[i], 16 * i + 48 * j, 1) for j in range(2)] for i in (1, 2)]
        own, rest = (spread[0][j] + spread[1][j] + spread[2][j] for j in range(2))
        beside.append(own[peers + 1 : peers + 2] + rest[peers : peers + 1] + tags)
    chunks = half // LANES
    down = iota((8, LANES), 0)
    wide = jnp.zeros((8, LANES), F32)
    for t, term in enumerate(split3(level)):
        for j in range(chunks):
            wide = jnp.where(down == t * chunks + j, term[:, j * LANES : (j + 1) * LANES], wide)
    wides = [jnp.where(down == 6, beside[g], wide) for g in range(groups)]
    across = width // LANES
    owners = sent.shape[0] // groups
    for d in range(sent.shape[0]):
        g = d // owners
        r, c = d % owners // across, d % owners % across
        if r * 8 < sub:
            at = g * sub + r * 8
            here, span = slice(at, at + 8), slice(c * LANES, (c + 1) * LANES)
            tile = [pulled[here, span], chosen[here, span]]
        else:
            tile = [jnp.zeros((16, LANES), F32)]
        sent[d] = jnp.concatenate(tile + [wides[g]], axis=0).astype(BF16)


def make_last_kernel(total_q, scale, rows, across):
    chunks = total_q // 2 // LANES

    def last_kernel(got, sent, level, turned):
        peers = got.shape[0]
        lane = iota((1, LANES), 1)
        parts = [got[s].astype(F32) for s in range(peers)]
        terms = jnp.concatenate([p[22:23] for p in parts], axis=0)
        picked = sums_in(terms, iota(terms.shape, 1), 96)
        moved = [terms] + [pltpu.roll(terms, LANES - 16 * i, 1) for i in range(1, 6)]
        own, rest = moved[0] + moved[1] + moved[2], moved[3] + moved[4] + moved[5]
        turned[0] = columns_of(own)
        turned[1] = columns_of(rest)
        first = jnp.minimum(lax.div(index(("z", "yh")), across) * 8, rows - 8)
        here = pl.ds(pl.multiple_of(first, 8), 8)
        tops = jnp.where(lane < peers, turned[0, here, :], LOW)
        keep = jnp.exp(tops - jnp.max(tops, axis=1, keepdims=True))
        keep = keep / jnp.sum(keep, axis=1, keepdims=True)
        rest = jnp.sum(keep * turned[1, here, :], axis=1, keepdims=True)
        wides = [
            p[16 : 16 + chunks] + p[16 + chunks : 16 + 2 * chunks] + p[16 + 2 * chunks : 16 + 3 * chunks]
            for p in parts
        ]
        high = wides[0]
        for s in range(1, peers):
            high = jnp.maximum(high, wides[s])
        total = jnp.zeros((chunks, LANES), F32)
        pulled, chosen = jnp.zeros((8, LANES), F32), jnp.zeros((8, LANES), F32)
        for s in range(peers):
            total = total + jnp.exp(wides[s] - high)
            pulled = pulled + keep[:, s : s + 1] * parts[s][:8]
            chosen = chosen + parts[s][8:16]
        lse = high + jnp.log(total)
        tile = ((pulled - rest * chosen) * (scale / total_q)).astype(BF16)
        for d in range(sent.shape[0]):
            sent[d] = tile
        terms = [a - b for a, b in zip(parted_sum(lse), picked)]
        for i in range(3):
            level[chunks + i : chunks + i + 1, :] = jnp.broadcast_to(terms[i], (1, LANES))
        level[:chunks, :] = lse

    return last_kernel


def passage_kernel(passages, level, level2, every, positive, out, loss):
    shard, width = out.shape
    group = every.shape[2]
    half = every.shape[0] * group
    total_q = 2 * half
    chunks = half // LANES
    core = lax.axis_index("core")
    down = index(ALL) * shard + iota((shard, 1), 0)
    scale = 1.0 / math.sqrt(width)
    aims = own_first(positive[...] - 1, group, core == 1)
    total = None
    for side, logs in enumerate([level, level2]):
        block = every[:, lax.rem(core + side, 2)].reshape(half, width)
        score = scale * lax.dot_general(
            passages[...], block, (((1,), (1,)), ((), ())), preferred_element_type=F32
        )
        lse = jnp.concatenate([logs[j : j + 1, :] for j in range(chunks)], axis=1)
        hit = aims[:, side * half : (side + 1) * half] == down
        weight = (jnp.exp(score - lse) - hit.astype(F32)) * (1.0 / total_q)
        term = jnp.dot(weight.astype(BF16), block, preferred_element_type=F32)
        total = term if total is None else total + term
    out[...] = (total * scale).astype(BF16)
    parts = level[chunks : chunks + 3, 0:1] + level2[chunks : chunks + 3, 0:1]
    loss[...] = (parts[0:1] + parts[1:2] + parts[2:3]) * (1.0 / total_q)


def make_assembly(down, across):
    def assembly(tiles, out):
        per = tiles.shape[0] // (out.shape[0] // (8 * down))
        for y in range(out.shape[0] // (8 * down)):
            for r in range(0, down, 2):
                for c in range(across):
                    pair = [tiles[y * per + (r + i) * across + c].astype(F32) for i in range(2)]
                    row = (y * down + r) * 8
                    out[row : row + 16, c * LANES : (c + 1) * LANES] = jnp.concatenate(
                        pair, axis=0
                    ).astype(BF16)

    return assembly


def on_device(queries, passages, positive):
    group, width = queries.shape
    scale = 1.0 / math.sqrt(width)
    total_q = positive.shape[0]
    half = total_q // 2
    shard = passages.shape[0]
    n_index = size(INDEX)
    n_line = size(LINE)
    n_rest = size(REST)
    block = half // n_line
    sub = group // n_line
    core = lax.axis_index("core")
    n_yl = lax.axis_size("yl")
    columns = lax.axis_index(ALL) * shard + jnp.arange(shard, dtype=jnp.int32)

    def swap(value):
        return lax.ppermute(value, "core", [(0, 1), (1, 0)])

    row = positive.reshape(1, total_q) + 1
    product = total_q * shard * width
    partner = swap(passages)
    queries, row = lax.optimization_barrier((queries, row))
    every = lax.all_gather(queries, QUERY, axis=0, tiled=True).reshape(n_yl, 2, group, width)
    sent, notes, rounds = call(
        first_kernel,
        [
            shaped((n_line, block + TAIL, width), BF16),
            shaped((8, half), F32),
            shaped((1, 1), jnp.int32),
        ],
        [every, passages, partner, row],
        4 * product,
    )

    def later_turn(turn, held):
        late, turn = lax.optimization_barrier((row, turn))
        aims = (late - 1).reshape(n_yl, 2, n_line, sub).transpose(1, 2, 0, 3).reshape(2, n_line, block)
        aims = jnp.where(core == 0, aims, aims[::-1])
        chip = chip_of(aims // shard, n_index)
        same = chip[..., :, None] == chip[..., None, :]
        before = jnp.arange(block)[:, None] > jnp.arange(block)[None, :]
        rank = jnp.sum((same & before).astype(jnp.int32), axis=-1)
        slots = turn * SLOTS + jnp.arange(SLOTS, dtype=jnp.int32)
        fits = (chip[0] == index(("yl",) + INDEX))[..., None] & (rank[0][..., None] == slots)
        wanted = jnp.max(jnp.where(fits, aims[0][..., None], -1), axis=1).reshape(-1, 1)
        rows = 0.0
        for side, table in ((core, passages), (1 - core, partner)):
            owner = (lax.axis_index("yl") * 2 + side) * n_index + lax.axis_index(INDEX)
            match = (wanted == owner * shard + jnp.arange(shard, dtype=jnp.int32)).astype(BF16)
            rows = rows + jnp.dot(match, table, preferred_element_type=F32)
        rows = rows.astype(BF16).reshape(n_line, SLOTS, width)
        rows = lax.all_to_all(rows, LINE, 0, 0, tiled=True)
        place = lax.axis_index("x")
        my_chip = lax.dynamic_index_in_dim(chip[0], place, 0, keepdims=False)
        my_rank = lax.dynamic_index_in_dim(rank[0], place, 0, keepdims=False)
        peer = jnp.arange(n_line, dtype=jnp.int32) * (n_index // n_line)
        peer_chip = lax.axis_index("yl") * n_index + peer + lax.axis_index(("z", "yh"))
        fits = (my_chip[:, None] == peer_chip[None, :])[..., None]
        fits = (fits & (my_rank[:, None, None] == slots)).astype(BF16)
        fits = fits.reshape(block, n_line * SLOTS)
        return held + jnp.dot(fits, rows.reshape(-1, width), preferred_element_type=F32)

    extra = lax.fori_loop(1, rounds[0, 0], later_turn, jnp.zeros((block, width), F32))
    got = lax.all_to_all(sent, LINE, 0, 0, tiled=True)
    (sent,) = call(
        line_kernel,
        [shaped((n_rest, 24, LANES), BF16)],
        [got, notes, extra],
        half * width * 8,
        [pltpu.VMEM((half, LANES), F32)],
    )
    got = lax.all_to_all(sent, REST, 0, 0, tiled=True)
    spread = n_index
    sent, level = call(
        make_last_kernel(total_q, scale, sub, width // LANES),
        [shaped((spread, 8, LANES), BF16), shaped((8, LANES), F32)],
        [got],
        half * width * 8,
        [pltpu.VMEM((2, LANES, LANES), F32)],
    )
    tiles = lax.all_to_all(sent, INDEX, 0, 0, tiled=True)
    passage_grad, loss = call(
        passage_kernel,
        [shaped((shard, width), BF16), shaped((1, 1), F32)],
        [passages, level, swap(level), every, row],
        4 * product,
    )
    (query_grad,) = call(
        make_assembly(sub // 8, width // LANES),
        [shaped((group, width), BF16)],
        [tiles],
        group * width,
    )
    return (loss[0, 0], query_grad, passage_grad)


def build(mesh):
    return jax.shard_map(
        on_device,
        mesh=mesh,
        in_specs=(P(QUERY, None), P(ALL, None), P()),
        out_specs=(P(), P(QUERY, None), P(ALL, None)),
        check_vma=False,
    )


def solution(mesh):
    devices = np.asarray(mesh.devices).reshape(4, 2, 4, 8, 2)
    return build(Mesh(devices, ("yl", "core", "x", "z", "yh")))
```
